32 devices in a mesh: date: 8 (over y, x, core), row: 4 (over z).
Axes of the slice: x: 2, y: 2, z: 4, core: 2. Of those that a mesh axis runs over, the one named last changes fastest.
Arguments:
- slc: float32 [2, 32, 32, 1024], P(None, 'date', 'row'), may hold values from -6 to 6
- offsets: int32 [2, 32], replicated, may hold values from -2 to 2, as said below
- masks: int32 [5, 32, 1024], P(None, 'row', 'date'), may hold values from 0 to 262143, as said below
Outputs:
- linked: float32 [2, 32, 32, 1024], P(None, None, 'row', 'date')
- eigen: float32 [32, 1024], P('row', 'date')
The draws below stay inside these ranges and needn't reach their ends.
Inputs may be any that keep to these rules, and one draw needn't show every extreme that they name: `offsets`: row offset in the first row, column offset in the second; some date has 2 in both and another date -2 in both. `masks`: bit (k mod 18) of word k // 18 tells whether slot k of the pixel's neighbourhood is used; the centre slot 40 is always set; bits of slots 81 and above are zero.
All inputs are finite; a program needn't handle non-finite values.
Results may differ from the reference program's by a relative error of at most 0.00011.
Values sent between devices are 32-bit elements; how exact they have to be, the bound alone decides.
No kernel may reach another device: no remote copies, remote signals or barrier semaphores. Data moves between devices by JAX's collectives and lax.ppermute only.
A program may use at most 64 MiB of HBM per device.

```python
import jax
import jax.numpy as jnp
from jax import lax

NDATE = 32
HALF = 4
SHIFT = 2
ITERS = 2
ROWS = 32
COLS = 1024
SLOTS = 81
WORDS = 5


def draw_offsets(key, part):
    base = jax.random.randint(jax.random.fold_in(key, 1), (2, NDATE), -SHIFT, SHIFT + 1).astype(jnp.int32)
    order = jax.random.permutation(jax.random.fold_in(key, 2), NDATE).astype(jnp.int32)
    date_ids = jnp.arange(NDATE, dtype=jnp.int32)
    base = jnp.where((date_ids == order[0])[None, :], SHIFT, base)
    base = jnp.where((date_ids == order[1])[None, :], -SHIFT, base)
    return base.astype(jnp.int32)


def draw_masks(key, part):
    density = jax.random.randint(jax.random.fold_in(key, 1), (ROWS, COLS), 15, 101).astype(jnp.int32)
    centre = SLOTS // 2
    weights = jnp.left_shift(jnp.ones((18,), jnp.int32), jnp.arange(18, dtype=jnp.int32))
    packed = []
    for word_index in range(WORDS):
        uniform_draws = jax.random.randint(jax.random.fold_in(key, 10 + word_index), (18, ROWS, COLS), 0, 100).astype(jnp.int32)
        slot_ids = word_index * 18 + jnp.arange(18, dtype=jnp.int32)
        mask_bits = (uniform_draws < density[None]).astype(jnp.int32)
        mask_bits = jnp.where((slot_ids == centre)[:, None, None], 1, mask_bits)
        mask_bits = jnp.where((slot_ids < SLOTS)[:, None, None], mask_bits, 0)
        packed.append(jnp.sum(mask_bits * weights[:, None, None], axis=0).astype(jnp.int32))
    return jnp.stack(packed).astype(jnp.int32)


def level_of(key, shape, shards, smallest, top_value):
    def one(axis_at, shards_of):
        steps = jax.random.uniform(jax.random.fold_in(jax.random.fold_in(key, 6), axis_at), (shards_of,), jnp.float32, smallest / len(shards), top_value / len(shards))
        return jnp.repeat(jnp.exp(steps), shape[axis_at] // shards_of).reshape((-1,) + (1,) * (len(shape) - axis_at - 1))

    loudness = one(*shards[0])
    for cut in shards[1:]:
        loudness = loudness * one(*cut)
    return loudness


def scatter_about(stream_key, dims, width, reach, cuts=(), held_as=jnp.bfloat16):
    values = jax.random.normal(stream_key, dims, jnp.float32) * width
    if len(cuts) > 0:
        values = level_of(stream_key, dims, cuts, -0.22, 0.18) * values
    return jnp.clip(values, min=-reach, max=reach).astype(held_as)


def setup_inputs(seed: int = 0) -> dict:
    splits = jax.random.split(jax.random.key(seed), 4)
    return {
        "slc": scatter_about(splits[0], (2, NDATE, ROWS, COLS), 1.0, 6.0, ((1, 8), (2, 4)), jnp.float32),
        "offsets": draw_offsets(jax.random.fold_in(splits[3], 71), 0),
        "masks": draw_masks(jax.random.fold_in(splits[3], 71), 0),
    }


TAPS = (-0.0625, 0.5625, 0.5625, -0.0625)
EPSILON = 1e-06

def shift_mix(image_plane, shifts, margin, out_rows, out_cols):
    row_taps = lax.dynamic_slice_in_dim(image_plane, margin - 1 + shifts[0], out_rows + 3, 1)
    row_mixed = TAPS[0] * row_taps[:, 0:out_rows]
    for tap_index in range(1, 4):
        row_mixed = row_mixed + TAPS[tap_index] * row_taps[:, tap_index:tap_index + out_rows]
    col_taps = lax.dynamic_slice_in_dim(row_mixed, margin - 1 + shifts[1], out_cols + 3, 2)
    col_mixed = TAPS[0] * col_taps[:, :, 0:out_cols]
    for tap_index in range(1, 4):
        col_mixed = col_mixed + TAPS[tap_index] * col_taps[:, :, tap_index:tap_index + out_cols]
    return col_mixed

def unpack_bits(mask_words):
    shift_ids = jnp.arange(18, dtype=jnp.int32)
    spread = jnp.right_shift(mask_words[:, None, :], shift_ids[None, :, None]) & 1
    return spread.reshape(-1, mask_words.shape[-1])[:SLOTS].astype(jnp.float32)

def power_norm(vec_real, vec_imag):
    return jnp.sqrt(lax.optimization_barrier(jnp.sum(vec_real * vec_real + vec_imag * vec_imag, axis=0)) + EPSILON)

def link_phases(patches, mask_bits):
    dates = patches.shape[0] // 2
    population = lax.optimization_barrier(jnp.sum(mask_bits, axis=0))
    weighted = patches * mask_bits[None]
    gram_matrix = jnp.einsum('ikp,jkp->ijp', weighted, patches, precision=lax.Precision.HIGHEST) / population
    cov_real = gram_matrix[:dates, :dates] + gram_matrix[dates:, dates:]
    cov_imag = gram_matrix[dates:, :dates] - gram_matrix[:dates, dates:]
    vec_real = jnp.ones((dates, patches.shape[-1]), jnp.float32)
    vec_imag = jnp.zeros((dates, patches.shape[-1]), jnp.float32)
    norm_prev = power_norm(vec_real, vec_imag)
    for step_index in range(ITERS):
        norm_prev = power_norm(vec_real, vec_imag)
        next_real = jnp.einsum('tup,up->tp', cov_real, vec_real, precision=lax.Precision.HIGHEST) - jnp.einsum('tup,up->tp', cov_imag, vec_imag, precision=lax.Precision.HIGHEST)
        next_imag = jnp.einsum('tup,up->tp', cov_real, vec_imag, precision=lax.Precision.HIGHEST) + jnp.einsum('tup,up->tp', cov_imag, vec_real, precision=lax.Precision.HIGHEST)
        vec_real, vec_imag = (next_real, next_imag)
    norm_last = power_norm(vec_real, vec_imag)
    linked = jnp.stack([vec_real, vec_imag]) * (jnp.sqrt(jnp.float32(dates)) / norm_last)
    return (linked, norm_last / norm_prev)

def reference(slc, offsets, masks):
    margin = SHIFT + 2
    padded_raw = jnp.pad(slc, ((0, 0), (0, 0), (margin, margin), (margin, margin)))
    resampled = jax.vmap(lambda image_plane, shifts: shift_mix(image_plane, shifts, margin, ROWS, COLS), in_axes=(1, 1), out_axes=1)(padded_raw, offsets)
    window = jnp.pad(resampled, ((0, 0), (0, 0), (HALF, HALF), (HALF, HALF)))
    side = 2 * HALF + 1

    def one_row(row_index):
        row_block = lax.dynamic_slice_in_dim(window, row_index, side, 2)
        patches = jnp.stack([row_block[..., col_step:col_step + COLS] for col_step in range(side)], axis=3)
        patches = patches.reshape(2 * NDATE, SLOTS, COLS)
        mask_bits = unpack_bits(lax.dynamic_index_in_dim(masks, row_index, 1, keepdims=False))
        return link_phases(patches, mask_bits)
    linked_rows, eigen_rows = lax.map(one_row, jnp.arange(ROWS, dtype=jnp.int32))
    return (jnp.transpose(linked_rows, (1, 2, 0, 3)), eigen_rows)
```

```python
import functools

import jax
import jax.numpy as jnp
from jax import lax
from jax.experimental import pallas as pl
from jax.experimental.pallas import tpu as pltpu
from jax.sharding import PartitionSpec as P

NDATE = 32
SLOT_COLS = 9
EPSILON = 1e-06
LANES = 128
TILE = 8
GROUPS = 8
TAP_COUNT = 8
WINDOW_ROWS = 16
WINDOW_COLS = 136
BLOCKS = 16

FLOAT = jnp.float32
HALF_FLOAT = jnp.bfloat16


def lane_ids(shape):
    return lax.broadcasted_iota(jnp.int32, shape, len(shape) - 1)


def sublane_ids(shape):
    return lax.broadcasted_iota(jnp.int32, shape, len(shape) - 2)


def pack_kernel(slc_ref, send_ref):
    planes = slc_ref.shape[0]
    blocks = send_ref.shape[0]
    for block in range(blocks):
        for plane in range(planes):
            send_ref[block, pl.ds(plane, TILE, stride=planes), :] = slc_ref[
                plane, :, block * LANES : (block + 1) * LANES
            ]
    lanes = lane_ids((planes, LANES))
    rims = [jnp.zeros((planes, LANES), FLOAT) for _ in range(blocks)]
    for row in range(TILE):
        start = 16 * row
        turned = [
            pltpu.roll(
                send_ref[block, row * planes : (row + 1) * planes, :],
                (start + 8) % LANES,
                axis=1,
            )
            for block in range(blocks)
        ]
        left = (lanes >= start) & (lanes < start + 8)
        right = (lanes >= start + 8) & (lanes < start + 16)
        for block in range(blocks):
            if block > 0:
                rims[block] = jnp.where(left, turned[block - 1], rims[block])
            if block < blocks - 1:
                rims[block] = jnp.where(right, turned[block + 1], rims[block])
    for block in range(blocks):
        send_ref[block, TILE * planes : (TILE + 1) * planes, :] = rims[block]


def tap_weight(distance):
    spread = jnp.abs(2 * distance - 1)
    return jnp.where(spread == 1, 0.5625, jnp.where(spread == 3, -0.0625, 0.0)).astype(FLOAT)


def prepare_kernel(
    offsets_ref, masks_ref, picks_ref, population_ref, row_sub_ref, row_lane_ref, col_lane_ref, words_ref
):
    words = masks_ref.shape[0]
    total = jnp.zeros((TILE, LANES), jnp.int32)
    for word in range(words):
        bits = masks_ref[word]
        bits = bits - (lax.shift_right_logical(bits, 1) & 0x55555555)
        bits = (bits & 0x33333333) + (lax.shift_right_logical(bits, 2) & 0x33333333)
        bits = (bits + lax.shift_right_logical(bits, 4)) & 0x0F0F0F0F
        bits = bits + lax.shift_right_logical(bits, 8)
        bits = bits + lax.shift_right_logical(bits, 16)
        total = total + (bits & 0xFF)
    population_ref[...] = total.astype(FLOAT)

    lanes = lane_ids((TILE, LANES))
    subs = sublane_ids((TILE, LANES))
    lane_dates = ((lanes % 64) // 8) * 4 + lanes % 4
    row_shift = jnp.zeros((TILE, LANES), jnp.int32)
    col_shift = jnp.zeros((TILE, LANES), jnp.int32)
    for date in range(NDATE):
        here = lane_dates == date
        row_shift = jnp.where(here, offsets_ref[0, date], row_shift)
        col_shift = jnp.where(here, offsets_ref[1, date], col_shift)
    for tap in range(TAP_COUNT):
        row_lane_ref[tap] = tap_weight(tap - 3 - row_shift)
        col_lane_ref[tap] = tap_weight(tap - 3 - col_shift)
    for group in range(GROUPS):
        shift = jnp.zeros((TILE, LANES), jnp.int32)
        for date in range(4):
            shift = jnp.where(subs % 4 == date, offsets_ref[0, 4 * group + date], shift)
        for tap in range(TAP_COUNT):
            row_sub_ref[tap, group * TILE : (group + 1) * TILE, :] = tap_weight(tap - 3 - shift)

    flat = [masks_ref[word] for word in range(words)]
    flat = flat + [jnp.zeros((TILE, LANES), jnp.int32)] * (LANES // TILE - words)
    words_ref[...] = jnp.transpose(jnp.concatenate(flat, axis=0))

    def one_block(block, carry):
        packed = words_ref[pl.ds(pl.multiple_of(block * TILE, TILE), TILE), :]
        for row_pair in range(TILE // 2):
            spread = [[], []]
            for row in (2 * row_pair, 2 * row_pair + 1):
                row_words = [
                    jnp.broadcast_to(
                        packed[:, word * TILE + row : word * TILE + row + 1], (TILE, LANES)
                    )
                    for word in range(words)
                ]
                for half in range(2):
                    near = 8 * half + lanes // 16 - row
                    across = lanes % 16 - subs
                    inside = (near >= 0) & (near <= 8) & (across >= 0) & (across <= 8)
                    amount = jnp.where(inside, (near & 1) * SLOT_COLS + across, 31)
                    first = max(0, 8 * half - row) // 2
                    last = min(8, 8 * half + 7 - row) // 2
                    chosen = row_words[first]
                    for word in range(first + 1, last + 1):
                        chosen = jnp.where(near >= 2 * word, row_words[word], chosen)
                    bits = lax.shift_right_logical(chosen, amount) & 1
                    spread[half].append(bits.astype(FLOAT))
            for half in range(2):
                picks_ref[
                    block, 16 * row_pair : 16 * row_pair + 16, half * LANES : (half + 1) * LANES
                ] = jnp.concatenate(spread[half], axis=0).astype(HALF_FLOAT)
        return carry

    lax.fori_loop(0, BLOCKS, one_block, 0)


def split_halves(values):
    high = values.astype(HALF_FLOAT)
    low = values - high.astype(FLOAT)
    return high, low


def dot(a, b, contract):
    return lax.dot_general(
        a, b, (((contract[0],), (contract[1],)), ((), ())), preferred_element_type=FLOAT
    )


def link_kernel(
    above_ref,
    own_ref,
    below_ref,
    picks_ref,
    population_ref,
    row_sub_ref,
    row_lane_ref,
    col_lane_ref,
    linked_ref,
    eigen_ref,
    mixed_ref,
    rims_ref,
    turned_ref,
    z_ref,
    y_ref,
    result_ref,
):
    row_at, row_count = lax.axis_index("row"), lax.axis_size("row")
    col_at, col_count = lax.axis_index("date"), lax.axis_size("date")
    sources = (above_ref, own_ref, below_ref)

    def mix_group(group, carry):
        weights = [
            row_sub_ref[tap, pl.ds(pl.multiple_of(group * TILE, TILE), TILE), :]
            for tap in range(TAP_COUNT)
        ]
        raw = [
            sources[row // 8][group, (row % 8) * TILE : (row % 8 + 1) * TILE, :] for row in range(24)
        ]
        for row in range(WINDOW_ROWS):
            mixed = weights[0] * raw[row + 1]
            for tap in range(1, TAP_COUNT):
                mixed = mixed + weights[tap] * raw[row + 1 + tap]
            start = pl.multiple_of((row // 8) * 64 + group * TILE, TILE)
            mixed_ref[row % 8, pl.ds(start, TILE), :] = mixed
        return carry

    lax.fori_loop(0, GROUPS, mix_group, 0)

    packed = [source[:, 8 * TILE : 9 * TILE, :].reshape(64, LANES) for source in sources]
    rims_ref[0:LANES, :] = jnp.transpose(jnp.concatenate([packed[0], packed[1]], axis=0))
    rims_ref[LANES : 2 * LANES, :] = jnp.transpose(jnp.concatenate([packed[1], packed[2]], axis=0))
    row_weights = [row_lane_ref[tap, 0:1, :] for tap in range(TAP_COUNT)]
    for row in range(8):
        turned_ref[row, 8 : 8 + LANES, :] = jnp.transpose(mixed_ref[row])
        rim = row_weights[0] * rims_ref[(row + 1) * 16 : (row + 2) * 16, :]
        for tap in range(1, TAP_COUNT):
            rim = rim + row_weights[tap] * rims_ref[(row + 1 + tap) * 16 : (row + 2 + tap) * 16, :]
        turned_ref[row, 0:8, :] = rim[0:8]
        turned_ref[row, 8 + LANES : 16 + LANES, :] = rim[8:16]

    lanes = lane_ids((1, LANES))
    lower = lanes < 64
    real = (lanes % 8) < 4
    places = sublane_ids((WINDOW_COLS, LANES))
    col_inside = ((places >= 4) | (col_at > 0)) & ((places < 132) | (col_at < col_count - 1))
    term = lax.broadcasted_iota(jnp.int32, (2 * LANES, 2 * LANES), 0) % LANES
    gives = lax.broadcasted_iota(jnp.int32, (2 * LANES, 2 * LANES), 1)
    same_part = ((term % 8) < 4) == (gives < LANES)
    sums = jnp.where(((term < 64) == ((gives % LANES) < 64)) & same_part, 1.0, 0.0).astype(HALF_FLOAT)

    def swapped(values):
        return jnp.where(
            real, pltpu.roll(values, LANES - 4, axis=1), -pltpu.roll(values, 4, axis=1)
        )

    def store_windows(target, row, values):
        high, low = split_halves(values)
        high = high.astype(FLOAT)
        rows = (
            jnp.where(lower, high, pltpu.roll(low, 64, axis=1)).astype(HALF_FLOAT),
            jnp.where(lower, pltpu.roll(high, 64, axis=1), low).astype(HALF_FLOAT),
        )
        for part in range(2):
            start = pl.multiple_of((row + 8 * part) * 16, 16)
            for block in range(BLOCKS):
                target[block, pl.ds(start, 16), :] = rows[part][block * 8 : block * 8 + 16]

    def one_row(row, carry):
        mixed = col_lane_ref[0, 0:1, :] * turned_ref[row, 1 : 1 + WINDOW_COLS, :]
        for tap in range(1, TAP_COUNT):
            mixed = mixed + col_lane_ref[tap, 0:1, :] * turned_ref[
                row, 1 + tap : 1 + tap + WINDOW_COLS, :
            ]
        row_inside = (lower & ((row >= 4) | (row_at > 0))) | (
            (lanes >= 64) & ((row < 4) | (row_at < row_count - 1))
        )
        z = jnp.where(col_inside & row_inside, mixed, 0.0)
        high, low = split_halves(z)
        total = dot(jnp.concatenate([high, low.astype(HALF_FLOAT)], axis=1), sums, (1, 0))
        y = z * total[:, :LANES] + swapped(z) * total[:, LANES:]
        store_windows(z_ref, row, z)
        store_windows(y_ref, row, y)
        return carry

    lax.fori_loop(0, 8, one_row, 0)

    def one_block(block, carry):
        z = z_ref[block]
        picks = picks_ref[block]
        first = dot(picks, y_ref[block], (1, 0))
        first = first + pltpu.roll(first, 64, axis=1)
        high, low = split_halves(jnp.concatenate([first, swapped(first)], axis=0))
        inner = dot(
            jnp.concatenate([high, low.astype(HALF_FLOAT)], axis=1),
            jnp.concatenate([z, z], axis=1),
            (1, 1),
        )
        picks = picks.astype(FLOAT)
        inner = inner * jnp.concatenate([picks, picks], axis=0)
        high, low = split_halves(inner)
        outer = dot(jnp.concatenate([high, low.astype(HALF_FLOAT)], axis=0), z, (1, 0))
        outer = outer[:128] + outer[128:]
        outer = outer + pltpu.roll(outer, 64, axis=1)
        second = outer[:64] - swapped(outer[64:])
        both = jnp.where(lower, second, first)
        start = pl.multiple_of(block * 8, 8)
        for row in range(8):
            result_ref[row, pl.ds(start, 8), :] = both[row * 8 : row * 8 + 8]
        return carry

    lax.fori_loop(0, BLOCKS, one_block, 0)

    inverse = 1.0 / population_ref[...]
    for row in range(8):
        turned = jnp.transpose(result_ref[row])
        second, first = turned[:64], turned[64:]
        scale = inverse[row : row + 1]
        square = scale * scale
        norm_first = jnp.sqrt(jnp.sum(first * first, axis=0, keepdims=True) * square + EPSILON)
        norm_last = jnp.sqrt(
            jnp.sum(second * second, axis=0, keepdims=True) * (square * square) + EPSILON
        )
        eigen_ref[row : row + 1, :] = norm_last / norm_first
        linked = second * (square * (jnp.sqrt(jnp.float32(NDATE)) / norm_last))
        for group in range(GROUPS):
            for part in range(2):
                begin = ((part * NDATE + 4 * group) * 8) + row
                at = group * 8 + part * 4
                linked_ref[pl.ds(begin, 4, stride=8), :] = linked[at : at + 4]


def canonical(received, dates_dev):
    sources = received.shape[0]
    if dates_dev == 4:
        return received
    cells = received.reshape(sources, 9, 2, dates_dev, LANES)
    cells = jnp.transpose(cells, (1, 2, 0, 3, 4)).reshape(9, 2, GROUPS, 4, LANES)
    return jnp.transpose(cells, (2, 0, 1, 3, 4)).reshape(GROUPS, 9 * TILE, LANES)


def vmem(count):
    return [pl.BlockSpec(memory_space=pltpu.VMEM)] * count


def on_device(slc, offsets, masks):
    dates_dev = slc.shape[1]
    rows_dev = slc.shape[2]
    cols_all = slc.shape[3]
    rows_count = lax.axis_size("row")
    cols_count = lax.axis_size("date")
    planes_dev = 2 * dates_dev
    assert rows_dev == TILE and cols_all == cols_count * LANES

    outgoing = pl.pallas_call(
        pack_kernel,
        out_shape=jax.ShapeDtypeStruct((cols_count, 9 * planes_dev, LANES), FLOAT),
        in_specs=vmem(1),
        out_specs=vmem(1)[0],
        cost_estimate=pl.CostEstimate(flops=0, bytes_accessed=600_000, transcendentals=0),
        name="pack",
    )(slc.reshape(planes_dev, rows_dev, cols_all))
    received = lax.all_to_all(outgoing, "date", split_axis=0, concat_axis=0, tiled=True)
    own = canonical(received, dates_dev)
    above = lax.ppermute(own, "row", [(i, i + 1) for i in range(rows_count - 1)])
    below = lax.ppermute(own, "row", [(i + 1, i) for i in range(rows_count - 1)])

    picks, population, row_sub, row_lane, col_lane = pl.pallas_call(
        prepare_kernel,
        out_shape=(
            jax.ShapeDtypeStruct((BLOCKS, 64, 256), HALF_FLOAT),
            jax.ShapeDtypeStruct((TILE, LANES), FLOAT),
            jax.ShapeDtypeStruct((TAP_COUNT, 64, LANES), FLOAT),
            jax.ShapeDtypeStruct((TAP_COUNT, TILE, LANES), FLOAT),
            jax.ShapeDtypeStruct((TAP_COUNT, TILE, LANES), FLOAT),
        ),
        in_specs=[pl.BlockSpec(memory_space=pltpu.SMEM)] + vmem(1),
        out_specs=tuple(vmem(5)),
        scratch_shapes=[pltpu.VMEM((LANES, LANES), jnp.int32)],
        cost_estimate=pl.CostEstimate(flops=4_000_000, bytes_accessed=1_000_000, transcendentals=0),
        name="prepare",
    )(offsets, masks)

    linked, eigen = pl.pallas_call(
        link_kernel,
        out_shape=(
            jax.ShapeDtypeStruct((2 * NDATE * TILE, LANES), FLOAT),
            jax.ShapeDtypeStruct((TILE, LANES), FLOAT),
        ),
        in_specs=vmem(8),
        out_specs=tuple(vmem(2)),
        scratch_shapes=[
            pltpu.VMEM((8, LANES, LANES), FLOAT),
            pltpu.VMEM((2 * LANES, LANES), FLOAT),
            pltpu.VMEM((8, LANES + 16, LANES), FLOAT),
            pltpu.VMEM((BLOCKS, 256, LANES), HALF_FLOAT),
            pltpu.VMEM((BLOCKS, 256, LANES), HALF_FLOAT),
            pltpu.VMEM((8, LANES, LANES), FLOAT),
        ],
        compiler_params=pltpu.CompilerParams(vmem_limit_bytes=24 * 1024 * 1024),
        cost_estimate=pl.CostEstimate(
            flops=1_000_000_000, bytes_accessed=2_000_000, transcendentals=0
        ),
        name="link",
    )(above, own, below, picks, population, row_sub, row_lane, col_lane)
    return linked.reshape(2, NDATE, TILE, LANES), eigen


def solution(mesh):
    in_specs = (P(None, "date", "row", None), P(), P(None, "row", "date"))
    out_specs = (P(None, None, "row", "date"), P("row", "date"))
    return jax.shard_map(
        on_device, mesh=mesh, in_specs=in_specs, out_specs=out_specs, check_vma=False
    )
```

```python
import functools

import jax
import jax.numpy as jnp
from jax import lax
from jax.experimental import pallas as pl
from jax.experimental.pallas import tpu as pltpu
from jax.sharding import PartitionSpec as P

NDATE = 32
SLOT_COLS = 9
EPSILON = 1e-06
LANES = 128
TILE = 8
GROUPS = 8
TAP_COUNT = 8
WINDOW_ROWS = 16
WINDOW_COLS = 136
BLOCKS = 16

FLOAT = jnp.float32
HALF_FLOAT = jnp.bfloat16


def lane_ids(shape):
    return lax.broadcasted_iota(jnp.int32, shape, len(shape) - 1)


def sublane_ids(shape):
    return lax.broadcasted_iota(jnp.int32, shape, len(shape) - 2)


def pack_kernel(slc_ref, send_ref):
    planes = slc_ref.shape[0]
    blocks = send_ref.shape[0]
    for block in range(blocks):
        for plane in range(planes):
            send_ref[block, pl.ds(plane, TILE, stride=planes), :] = slc_ref[
                plane, :, block * LANES : (block + 1) * LANES
            ]
    lanes = lane_ids((planes, LANES))
    rims = [jnp.zeros((planes, LANES), FLOAT) for _ in range(blocks)]
    for row in range(TILE):
        start = 16 * row
        turned = [
            pltpu.roll(
                send_ref[block, row * planes : (row + 1) * planes, :],
                (start + 8) % LANES,
                axis=1,
            )
            for block in range(blocks)
        ]
        left = (lanes >= start) & (lanes < start + 8)
        right = (lanes >= start + 8) & (lanes < start + 16)
        for block in range(blocks):
            if block > 0:
                rims[block] = jnp.where(left, turned[block - 1], rims[block])
            if block < blocks - 1:
                rims[block] = jnp.where(right, turned[block + 1], rims[block])
    for block in range(blocks):
        send_ref[block, TILE * planes : (TILE + 1) * planes, :] = rims[block]


def tap_weight(distance):
    spread = jnp.abs(2 * distance - 1)
    return jnp.where(spread == 1, 0.5625, jnp.where(spread == 3, -0.0625, 0.0)).astype(FLOAT)


def prepare_kernel(
    offsets_ref, masks_ref, picks_ref, population_ref, row_sub_ref, row_lane_ref, col_lane_ref, words_ref
):
    words = masks_ref.shape[0]
    total = jnp.zeros((TILE, LANES), jnp.int32)
    for word in range(words):
        bits = masks_ref[word]
        bits = bits - (lax.shift_right_logical(bits, 1) & 0x55555555)
        bits = (bits & 0x33333333) + (lax.shift_right_logical(bits, 2) & 0x33333333)
        bits = (bits + lax.shift_right_logical(bits, 4)) & 0x0F0F0F0F
        bits = bits + lax.shift_right_logical(bits, 8)
        bits = bits + lax.shift_right_logical(bits, 16)
        total = total + (bits & 0xFF)
    population_ref[...] = total.astype(FLOAT)

    lanes = lane_ids((TILE, LANES))
    subs = sublane_ids((TILE, LANES))
    lane_dates = ((lanes % 64) // 8) * 4 + lanes % 4
    row_shift = jnp.zeros((TILE, LANES), jnp.int32)
    col_shift = jnp.zeros((TILE, LANES), jnp.int32)
    for date in range(NDATE):
        here = lane_dates == date
        row_shift = jnp.where(here, offsets_ref[0, date], row_shift)
        col_shift = jnp.where(here, offsets_ref[1, date], col_shift)
    for tap in range(TAP_COUNT):
        row_lane_ref[tap] = tap_weight(tap - 3 - row_shift)
        col_lane_ref[tap] = tap_weight(tap - 3 - col_shift)
    for group in range(GROUPS):
        shift = jnp.zeros((TILE, LANES), jnp.int32)
        for date in range(4):
            shift = jnp.where(subs % 4 == date, offsets_ref[0, 4 * group + date], shift)
        for tap in range(TAP_COUNT):
            row_sub_ref[tap, group * TILE : (group + 1) * TILE, :] = tap_weight(tap - 3 - shift)

    flat = [masks_ref[word] for word in range(words)]
    flat = flat + [jnp.zeros((TILE, LANES), jnp.int32)] * (LANES // TILE - words)
    words_ref[...] = jnp.transpose(jnp.concatenate(flat, axis=0))

    def one_block(block, carry):
        packed = words_ref[pl.ds(pl.multiple_of(block * TILE, TILE), TILE), :]
        for row_pair in range(TILE // 2):
            spread = [[], []]
            for row in (2 * row_pair, 2 * row_pair + 1):
                row_words = [
                    jnp.broadcast_to(
                        packed[:, word * TILE + row : word * TILE + row + 1], (TILE, LANES)
                    )
                    for word in range(words)
                ]
                for half in range(2):
                    near = 8 * half + lanes // 16 - row
                    across = lanes % 16 - subs
                    inside = (near >= 0) & (near <= 8) & (across >= 0) & (across <= 8)
                    amount = jnp.where(inside, (near & 1) * SLOT_COLS + across, 31)
                    first = max(0, 8 * half - row) // 2
                    last = min(8, 8 * half + 7 - row) // 2
                    chosen = row_words[first]
                    for word in range(first + 1, last + 1):
                        chosen = jnp.where(near >= 2 * word, row_words[word], chosen)
                    bits = lax.shift_right_logical(chosen, amount) & 1
                    spread[half].append(bits.astype(FLOAT))
            for half in range(2):
                picks_ref[
                    block, 16 * row_pair : 16 * row_pair + 16, half * LANES : (half + 1) * LANES
                ] = jnp.concatenate(spread[half], axis=0).astype(HALF_FLOAT)
        return carry

    lax.fori_loop(0, BLOCKS, one_block, 0)


def split_halves(values):
    high = values.astype(HALF_FLOAT)
    low = values - high.astype(FLOAT)
    return high, low


def dot(a, b, contract):
    return lax.dot_general(
        a, b, (((contract[0],), (contract[1],)), ((), ())), preferred_element_type=FLOAT
    )


def link_kernel(
    own_ref,
    near_ref,
    far_ref,
    picks_ref,
    population_ref,
    row_sub_ref,
    row_lane_ref,
    col_lane_ref,
    linked_ref,
    eigen_ref,
    mixed_ref,
    rims_ref,
    turned_ref,
    z_ref,
    y_ref,
    result_ref,
):
    row_at, row_count = lax.axis_index("row"), lax.axis_size("row")
    col_at, col_count = lax.axis_index("date"), lax.axis_size("date")
    even = row_at % 2 == 0

    def raw_tile(row, group):
        at = (row % 8) * TILE
        if 8 <= row < 16:
            return own_ref[group, at : at + TILE, :]
        near, far = near_ref[group, at : at + TILE, :], far_ref[group, at : at + TILE, :]
        return jnp.where(even, far, near) if row < 8 else jnp.where(even, near, far)

    def mix_group(group, carry):
        weights = [
            row_sub_ref[tap, pl.ds(pl.multiple_of(group * TILE, TILE), TILE), :]
            for tap in range(TAP_COUNT)
        ]
        raw = [raw_tile(row, group) for row in range(24)]
        for row in range(WINDOW_ROWS):
            mixed = weights[0] * raw[row + 1]
            for tap in range(1, TAP_COUNT):
                mixed = mixed + weights[tap] * raw[row + 1 + tap]
            start = pl.multiple_of((row // 8) * 64 + group * TILE, TILE)
            mixed_ref[row % 8, pl.ds(start, TILE), :] = mixed
        return carry

    lax.fori_loop(0, GROUPS, mix_group, 0)

    near, own, far = [
        source[:, 8 * TILE : 9 * TILE, :].reshape(64, LANES)
        for source in (near_ref, own_ref, far_ref)
    ]
    packed = [jnp.where(even, far, near), own, jnp.where(even, near, far)]
    rims_ref[0:LANES, :] = jnp.transpose(jnp.concatenate([packed[0], packed[1]], axis=0))
    rims_ref[LANES : 2 * LANES, :] = jnp.transpose(jnp.concatenate([packed[1], packed[2]], axis=0))
    row_weights = [row_lane_ref[tap, 0:1, :] for tap in range(TAP_COUNT)]
    for row in range(8):
        turned_ref[row, 8 : 8 + LANES, :] = jnp.transpose(mixed_ref[row])
        rim = row_weights[0] * rims_ref[(row + 1) * 16 : (row + 2) * 16, :]
        for tap in range(1, TAP_COUNT):
            rim = rim + row_weights[tap] * rims_ref[(row + 1 + tap) * 16 : (row + 2 + tap) * 16, :]
        turned_ref[row, 0:8, :] = rim[0:8]
        turned_ref[row, 8 + LANES : 16 + LANES, :] = rim[8:16]

    lanes = lane_ids((1, LANES))
    lower = lanes < 64
    real = (lanes % 8) < 4
    places = sublane_ids((WINDOW_COLS, LANES))
    col_inside = ((places >= 4) | (col_at > 0)) & ((places < 132) | (col_at < col_count - 1))
    term = lax.broadcasted_iota(jnp.int32, (2 * LANES, 2 * LANES), 0) % LANES
    gives = lax.broadcasted_iota(jnp.int32, (2 * LANES, 2 * LANES), 1)
    same_part = ((term % 8) < 4) == (gives < LANES)
    sums = jnp.where(((term < 64) == ((gives % LANES) < 64)) & same_part, 1.0, 0.0).astype(HALF_FLOAT)

    def swapped(values):
        return jnp.where(
            real, pltpu.roll(values, LANES - 4, axis=1), -pltpu.roll(values, 4, axis=1)
        )

    def store_windows(target, row, values):
        high, low = split_halves(values)
        high = high.astype(FLOAT)
        rows = (
            jnp.where(lower, high, pltpu.roll(low, 64, axis=1)),
            jnp.where(lower, pltpu.roll(high, 64, axis=1), low),
        )
        for part in range(2):
            start = pl.multiple_of((row + 8 * part) * 16, 16)
            for block in range(BLOCKS):
                target[block, pl.ds(start, 16), :] = rows[part][block * 8 : block * 8 + 16].astype(
                    HALF_FLOAT
                )

    def one_row(row, carry):
        mixed = col_lane_ref[0, 0:1, :] * turned_ref[row, 1 : 1 + WINDOW_COLS, :]
        for tap in range(1, TAP_COUNT):
            mixed = mixed + col_lane_ref[tap, 0:1, :] * turned_ref[
                row, 1 + tap : 1 + tap + WINDOW_COLS, :
            ]
        row_inside = (lower & ((row >= 4) | (row_at > 0))) | (
            (lanes >= 64) & ((row < 4) | (row_at < row_count - 1))
        )
        z = jnp.where(col_inside & row_inside, mixed, 0.0)
        high, low = split_halves(z)
        total = dot(jnp.concatenate([high, low.astype(HALF_FLOAT)], axis=1), sums, (1, 0))
        y = z * total[:, :LANES] + swapped(z) * total[:, LANES:]
        store_windows(z_ref, row, z)
        store_windows(y_ref, row, y)
        return carry

    lax.fori_loop(0, 8, one_row, 0, unroll=2)

    def one_block(block, carry):
        z = z_ref[block]
        picks = picks_ref[block]
        first = dot(picks, y_ref[block], (1, 0))
        first = first + pltpu.roll(first, 64, axis=1)
        high, low = split_halves(jnp.concatenate([first, swapped(first)], axis=0))
        inner = dot(
            jnp.concatenate([high, low.astype(HALF_FLOAT)], axis=1),
            jnp.concatenate([z, z], axis=1),
            (1, 1),
        )
        high, low = split_halves(inner)
        chosen = jnp.concatenate([high, low.astype(HALF_FLOAT)], axis=0) * jnp.concatenate(
            [picks] * 4, axis=0
        )
        outer = dot(chosen, z, (1, 0))
        outer = outer[:128] + outer[128:]
        outer = outer + pltpu.roll(outer, 64, axis=1)
        second = outer[:64] - swapped(outer[64:])
        both = jnp.where(lower, second, first)
        start = pl.multiple_of(block * 8, 8)
        for row in range(8):
            result_ref[row, pl.ds(start, 8), :] = both[row * 8 : row * 8 + 8]
        return carry

    lax.fori_loop(0, BLOCKS, one_block, 0, unroll=4)

    inverse = 1.0 / population_ref[...]
    for row in range(8):
        turned = jnp.transpose(result_ref[row])
        second, first = turned[:64], turned[64:]
        scale = inverse[row : row + 1]
        square = scale * scale
        norm_first = jnp.sqrt(jnp.sum(first * first, axis=0, keepdims=True) * square + EPSILON)
        norm_last = jnp.sqrt(
            jnp.sum(second * second, axis=0, keepdims=True) * (square * square) + EPSILON
        )
        eigen_ref[row : row + 1, :] = norm_last / norm_first
        linked = second * (square * (jnp.sqrt(jnp.float32(NDATE)) / norm_last))
        for group in range(GROUPS):
            for part in range(2):
                begin = ((part * NDATE + 4 * group) * 8) + row
                at = group * 8 + part * 4
                linked_ref[pl.ds(begin, 4, stride=8), :] = linked[at : at + 4]


def canonical(received, dates_dev):
    sources = received.shape[0]
    if dates_dev == 4:
        return received
    cells = received.reshape(sources, 9, 2, dates_dev, LANES)
    cells = jnp.transpose(cells, (1, 2, 0, 3, 4)).reshape(9, 2, GROUPS, 4, LANES)
    return jnp.transpose(cells, (2, 0, 1, 3, 4)).reshape(GROUPS, 9 * TILE, LANES)


def vmem(count):
    return [pl.BlockSpec(memory_space=pltpu.VMEM)] * count


def on_device(slc, offsets, masks):
    dates_dev = slc.shape[1]
    rows_dev = slc.shape[2]
    cols_all = slc.shape[3]
    rows_count = lax.axis_size("row")
    cols_count = lax.axis_size("date")
    planes_dev = 2 * dates_dev
    assert rows_dev == TILE and cols_all == cols_count * LANES

    small = pltpu.CompilerParams(vmem_limit_bytes=4 * 1024 * 1024)
    outgoing = pl.pallas_call(
        pack_kernel,
        out_shape=jax.ShapeDtypeStruct((cols_count, 9 * planes_dev, LANES), FLOAT),
        in_specs=vmem(1),
        out_specs=vmem(1)[0],
        compiler_params=small,
        cost_estimate=pl.CostEstimate(flops=0, bytes_accessed=600_000, transcendentals=0),
        name="pack",
    )(slc.reshape(planes_dev, rows_dev, cols_all))
    received = lax.all_to_all(outgoing, "date", split_axis=0, concat_axis=0, tiled=True)
    own = canonical(received, dates_dev)
    near, far = [
        lax.ppermute(
            own,
            "row",
            [
                pair
                for low in range(first, rows_count - 1, 2)
                for pair in ((low, low + 1), (low + 1, low))
            ],
        )
        for first in range(2)
    ]

    picks, population, row_sub, row_lane, col_lane = pl.pallas_call(
        prepare_kernel,
        out_shape=(
            jax.ShapeDtypeStruct((BLOCKS, 64, 256), HALF_FLOAT),
            jax.ShapeDtypeStruct((TILE, LANES), FLOAT),
            jax.ShapeDtypeStruct((TAP_COUNT, 64, LANES), FLOAT),
            jax.ShapeDtypeStruct((TAP_COUNT, TILE, LANES), FLOAT),
            jax.ShapeDtypeStruct((TAP_COUNT, TILE, LANES), FLOAT),
        ),
        in_specs=[pl.BlockSpec(memory_space=pltpu.SMEM)] + vmem(1),
        out_specs=tuple(vmem(5)),
        scratch_shapes=[pltpu.VMEM((LANES, LANES), jnp.int32)],
        compiler_params=small,
        cost_estimate=pl.CostEstimate(flops=4_000_000, bytes_accessed=1_000_000, transcendentals=0),
        name="prepare",
    )(offsets, masks)

    linked, eigen = pl.pallas_call(
        link_kernel,
        out_shape=(
            jax.ShapeDtypeStruct((2 * NDATE * TILE, LANES), FLOAT),
            jax.ShapeDtypeStruct((TILE, LANES), FLOAT),
        ),
        in_specs=vmem(8),
        out_specs=tuple(vmem(2)),
        scratch_shapes=[
            pltpu.VMEM((8, LANES, LANES), FLOAT),
            pltpu.VMEM((2 * LANES, LANES), FLOAT),
            pltpu.VMEM((8, LANES + 16, LANES), FLOAT),
            pltpu.VMEM((BLOCKS, 256, LANES), HALF_FLOAT),
            pltpu.VMEM((BLOCKS, 256, LANES), HALF_FLOAT),
            pltpu.VMEM((8, LANES, LANES), FLOAT),
        ],
        compiler_params=pltpu.CompilerParams(vmem_limit_bytes=16 * 1024 * 1024),
        cost_estimate=pl.CostEstimate(
            flops=1_000_000_000, bytes_accessed=2_000_000, transcendentals=0
        ),
        name="link",
    )(own, near, far, picks, population, row_sub, row_lane, col_lane)
    return linked.reshape(2, NDATE, TILE, LANES), eigen


def solution(mesh):
    in_specs = (P(None, "date", "row", None), P(), P(None, "row", "date"))
    out_specs = (P(None, None, "row", "date"), P("row", "date"))
    return jax.shard_map(
        on_device, mesh=mesh, in_specs=in_specs, out_specs=out_specs, check_vma=False
    )
```

```python
import functools

import jax
import jax.numpy as jnp
from jax import lax
from jax.experimental import pallas as pl
from jax.experimental.pallas import tpu as pltpu
from jax.sharding import PartitionSpec as P

NDATE = 32
SLOT_COLS = 9
EPSILON = 1e-06
LANES = 128
TILE = 8
GROUPS = 8
TAP_COUNT = 8
WINDOW_ROWS = 16
WINDOW_COLS = 136
BLOCKS = 16

FLOAT = jnp.float32
HALF_FLOAT = jnp.bfloat16


def lane_ids(shape):
    return lax.broadcasted_iota(jnp.int32, shape, len(shape) - 1)


def sublane_ids(shape):
    return lax.broadcasted_iota(jnp.int32, shape, len(shape) - 2)


def pack_kernel(slc_ref, send_ref):
    planes = slc_ref.shape[0]
    blocks = send_ref.shape[0]
    for block in range(blocks):
        for plane in range(planes):
            send_ref[block, pl.ds(plane, TILE, stride=planes), :] = slc_ref[
                plane, :, block * LANES : (block + 1) * LANES
            ]
    lanes = lane_ids((planes, LANES))
    rims = [jnp.zeros((planes, LANES), FLOAT) for _ in range(blocks)]
    for row in range(TILE):
        start = 16 * row
        turned = [
            pltpu.roll(
                send_ref[block, row * planes : (row + 1) * planes, :],
                (start + 8) % LANES,
                axis=1,
            )
            for block in range(blocks)
        ]
        left = (lanes >= start) & (lanes < start + 8)
        right = (lanes >= start + 8) & (lanes < start + 16)
        for block in range(blocks):
            if block > 0:
                rims[block] = jnp.where(left, turned[block - 1], rims[block])
            if block < blocks - 1:
                rims[block] = jnp.where(right, turned[block + 1], rims[block])
    for block in range(blocks):
        send_ref[block, TILE * planes : (TILE + 1) * planes, :] = rims[block]


def tap_weight(distance):
    spread = jnp.abs(2 * distance - 1)
    return jnp.where(spread == 1, 0.5625, jnp.where(spread == 3, -0.0625, 0.0)).astype(FLOAT)


def prepare_kernel(
    offsets_ref, masks_ref, picks_ref, population_ref, row_sub_ref, row_lane_ref, col_lane_ref, words_ref
):
    words = masks_ref.shape[0]
    total = jnp.zeros((TILE, LANES), jnp.int32)
    for word in range(words):
        bits = masks_ref[word]
        bits = bits - (lax.shift_right_logical(bits, 1) & 0x55555555)
        bits = (bits & 0x33333333) + (lax.shift_right_logical(bits, 2) & 0x33333333)
        bits = (bits + lax.shift_right_logical(bits, 4)) & 0x0F0F0F0F
        bits = bits + lax.shift_right_logical(bits, 8)
        bits = bits + lax.shift_right_logical(bits, 16)
        total = total + (bits & 0xFF)
    population_ref[...] = total.astype(FLOAT)

    lanes = lane_ids((TILE, LANES))
    subs = sublane_ids((TILE, LANES))
    lane_dates = ((lanes % 64) // 8) * 4 + lanes % 4
    row_shift = jnp.zeros((TILE, LANES), jnp.int32)
    col_shift = jnp.zeros((TILE, LANES), jnp.int32)
    for date in range(NDATE):
        here = lane_dates == date
        row_shift = jnp.where(here, offsets_ref[0, date], row_shift)
        col_shift = jnp.where(here, offsets_ref[1, date], col_shift)
    for tap in range(TAP_COUNT):
        row_lane_ref[tap] = tap_weight(tap - 3 - row_shift)
        col_lane_ref[tap] = tap_weight(tap - 3 - col_shift)
    for group in range(GROUPS):
        shift = jnp.zeros((TILE, LANES), jnp.int32)
        for date in range(4):
            shift = jnp.where(subs % 4 == date, offsets_ref[0, 4 * group + date], shift)
        for tap in range(TAP_COUNT):
            row_sub_ref[tap, group * TILE : (group + 1) * TILE, :] = tap_weight(tap - 3 - shift)

    flat = [masks_ref[word] for word in range(words)]
    flat = flat + [jnp.zeros((TILE, LANES), jnp.int32)] * (LANES // TILE - words)
    words_ref[...] = jnp.transpose(jnp.concatenate(flat, axis=0))

    def one_block(block, carry):
        packed = words_ref[pl.ds(pl.multiple_of(block * TILE, TILE), TILE), :]
        for row_pair in range(TILE // 2):
            spread = [[], []]
            for row in (2 * row_pair, 2 * row_pair + 1):
                row_words = [
                    jnp.broadcast_to(
                        packed[:, word * TILE + row : word * TILE + row + 1], (TILE, LANES)
                    )
                    for word in range(words)
                ]
                for half in range(2):
                    near = 8 * half + lanes // 16 - row
                    across = lanes % 16 - subs
                    inside = (near >= 0) & (near <= 8) & (across >= 0) & (across <= 8)
                    amount = jnp.where(inside, (near & 1) * SLOT_COLS + across, 31)
                    first = max(0, 8 * half - row) // 2
                    last = min(8, 8 * half + 7 - row) // 2
                    chosen = row_words[first]
                    for word in range(first + 1, last + 1):
                        chosen = jnp.where(near >= 2 * word, row_words[word], chosen)
                    bits = lax.shift_right_logical(chosen, amount) & 1
                    spread[half].append(bits.astype(FLOAT))
            for half in range(2):
                picks_ref[
                    block, 16 * row_pair : 16 * row_pair + 16, half * LANES : (half + 1) * LANES
                ] = jnp.concatenate(spread[half], axis=0).astype(HALF_FLOAT)
        return carry

    lax.fori_loop(0, BLOCKS, one_block, 0)


def split_halves(values):
    high = values.astype(HALF_FLOAT)
    low = values - high.astype(FLOAT)
    return high, low


def dot(a, b, contract):
    return lax.dot_general(
        a, b, (((contract[0],), (contract[1],)), ((), ())), preferred_element_type=FLOAT
    )


def link_kernel(
    own_ref,
    far_ref,
    near_ref,
    picks_ref,
    population_ref,
    row_sub_ref,
    row_lane_ref,
    col_lane_ref,
    linked_ref,
    eigen_ref,
    mixed_ref,
    rims_ref,
    turned_ref,
    z_ref,
    y_ref,
    result_ref,
):
    row_at, row_count = lax.axis_index("row"), lax.axis_size("row")
    col_at, col_count = lax.axis_index("date"), lax.axis_size("date")
    even = row_at % 2 == 0

    def raw_tile(row, group):
        at = (row % 8) * TILE
        if 8 <= row < 16:
            return own_ref[group, at : at + TILE, :]
        near, far = near_ref[group, at : at + TILE, :], far_ref[group, at : at + TILE, :]
        return jnp.where(even, far, near) if row < 8 else jnp.where(even, near, far)

    def mix_group(group, carry):
        weights = [
            row_sub_ref[tap, pl.ds(pl.multiple_of(group * TILE, TILE), TILE), :]
            for tap in range(TAP_COUNT)
        ]
        raw = [raw_tile(row, group) for row in range(24)]
        for row in range(WINDOW_ROWS):
            mixed = weights[0] * raw[row + 1]
            for tap in range(1, TAP_COUNT):
                mixed = mixed + weights[tap] * raw[row + 1 + tap]
            start = pl.multiple_of((row // 8) * 64 + group * TILE, TILE)
            mixed_ref[row % 8, pl.ds(start, TILE), :] = mixed
        return carry

    lax.fori_loop(0, GROUPS, mix_group, 0)

    near, own, far = [
        source[:, 8 * TILE : 9 * TILE, :].reshape(64, LANES)
        for source in (near_ref, own_ref, far_ref)
    ]
    packed = [jnp.where(even, far, near), own, jnp.where(even, near, far)]
    rims_ref[0:LANES, :] = jnp.transpose(jnp.concatenate([packed[0], packed[1]], axis=0))
    rims_ref[LANES : 2 * LANES, :] = jnp.transpose(jnp.concatenate([packed[1], packed[2]], axis=0))
    row_weights = [row_lane_ref[tap, 0:1, :] for tap in range(TAP_COUNT)]
    for row in range(8):
        turned_ref[row, 8 : 8 + LANES, :] = jnp.transpose(mixed_ref[row])
        rim = row_weights[0] * rims_ref[(row + 1) * 16 : (row + 2) * 16, :]
        for tap in range(1, TAP_COUNT):
            rim = rim + row_weights[tap] * rims_ref[(row + 1 + tap) * 16 : (row + 2 + tap) * 16, :]
        turned_ref[row, 0:8, :] = rim[0:8]
        turned_ref[row, 8 + LANES : 16 + LANES, :] = rim[8:16]

    lanes = lane_ids((1, LANES))
    lower = lanes < 64
    real = (lanes % 8) < 4
    places = sublane_ids((WINDOW_COLS, LANES))
    col_inside = ((places >= 4) | (col_at > 0)) & ((places < 132) | (col_at < col_count - 1))
    term = lax.broadcasted_iota(jnp.int32, (2 * LANES, 2 * LANES), 0) % LANES
    gives = lax.broadcasted_iota(jnp.int32, (2 * LANES, 2 * LANES), 1)
    same_part = ((term % 8) < 4) == (gives < LANES)
    sums = jnp.where(((term < 64) == ((gives % LANES) < 64)) & same_part, 1.0, 0.0).astype(HALF_FLOAT)

    def swapped(values):
        return jnp.where(
            real, pltpu.roll(values, LANES - 4, axis=1), -pltpu.roll(values, 4, axis=1)
        )

    def store_windows(target, row, values):
        high, low = split_halves(values)
        high = high.astype(FLOAT)
        rows = (
            jnp.where(lower, high, pltpu.roll(low, 64, axis=1)),
            jnp.where(lower, pltpu.roll(high, 64, axis=1), low),
        )
        for part in range(2):
            start = pl.multiple_of((row + 8 * part) * 16, 16)
            for block in range(BLOCKS):
                target[block, pl.ds(start, 16), :] = rows[part][block * 8 : block * 8 + 16].astype(
                    HALF_FLOAT
                )

    def one_row(row, carry):
        mixed = col_lane_ref[0, 0:1, :] * turned_ref[row, 1 : 1 + WINDOW_COLS, :]
        for tap in range(1, TAP_COUNT):
            mixed = mixed + col_lane_ref[tap, 0:1, :] * turned_ref[
                row, 1 + tap : 1 + tap + WINDOW_COLS, :
            ]
        row_inside = (lower & ((row >= 4) | (row_at > 0))) | (
            (lanes >= 64) & ((row < 4) | (row_at < row_count - 1))
        )
        z = jnp.where(col_inside & row_inside, mixed, 0.0)
        high, low = split_halves(z)
        total = dot(jnp.concatenate([high, low.astype(HALF_FLOAT)], axis=1), sums, (1, 0))
        y = z * total[:, :LANES] + swapped(z) * total[:, LANES:]
        store_windows(z_ref, row, z)
        store_windows(y_ref, row, y)
        return carry

    lax.fori_loop(0, 8, one_row, 0, unroll=8)

    def one_block(block, carry):
        z = z_ref[block]
        picks = picks_ref[block]
        first = dot(picks, y_ref[block], (1, 0))
        first = first + pltpu.roll(first, 64, axis=1)
        high, low = split_halves(jnp.concatenate([first, swapped(first)], axis=0))
        inner = dot(
            jnp.concatenate([high, low.astype(HALF_FLOAT)], axis=1),
            jnp.concatenate([z, z], axis=1),
            (1, 1),
        )
        high, low = split_halves(inner)
        chosen = jnp.concatenate([high, low.astype(HALF_FLOAT)], axis=0) * jnp.concatenate(
            [picks] * 4, axis=0
        )
        outer = dot(chosen, z, (1, 0))
        outer = outer[:128] + outer[128:]
        outer = outer + pltpu.roll(outer, 64, axis=1)
        second = outer[:64] - swapped(outer[64:])
        both = jnp.where(lower, second, first)
        start = pl.multiple_of(block * 8, 8)
        for row in range(8):
            result_ref[row, pl.ds(start, 8), :] = both[row * 8 : row * 8 + 8]
        return carry

    lax.fori_loop(0, BLOCKS, one_block, 0, unroll=16)

    inverse = 1.0 / population_ref[...]
    for row in range(8):
        turned = jnp.transpose(result_ref[row])
        second, first = turned[:64], turned[64:]
        scale = inverse[row : row + 1]
        square = scale * scale
        norm_first = jnp.sqrt(jnp.sum(first * first, axis=0, keepdims=True) * square + EPSILON)
        norm_last = jnp.sqrt(
            jnp.sum(second * second, axis=0, keepdims=True) * (square * square) + EPSILON
        )
        eigen_ref[row : row + 1, :] = norm_last / norm_first
        linked = second * (square * (jnp.sqrt(jnp.float32(NDATE)) / norm_last))
        for group in range(GROUPS):
            for part in range(2):
                begin = ((part * NDATE + 4 * group) * 8) + row
                at = group * 8 + part * 4
                linked_ref[pl.ds(begin, 4, stride=8), :] = linked[at : at + 4]


def canonical(received, dates_dev):
    sources = received.shape[0]
    if dates_dev == 4:
        return received
    cells = received.reshape(sources, 9, 2, dates_dev, LANES)
    cells = jnp.transpose(cells, (1, 2, 0, 3, 4)).reshape(9, 2, GROUPS, 4, LANES)
    return jnp.transpose(cells, (2, 0, 1, 3, 4)).reshape(GROUPS, 9 * TILE, LANES)


def vmem(count):
    return [pl.BlockSpec(memory_space=pltpu.VMEM)] * count


def on_device(slc, offsets, masks):
    dates_dev = slc.shape[1]
    rows_dev = slc.shape[2]
    cols_all = slc.shape[3]
    rows_count = lax.axis_size("row")
    cols_count = lax.axis_size("date")
    planes_dev = 2 * dates_dev
    assert rows_dev == TILE and cols_all == cols_count * LANES

    small = pltpu.CompilerParams(vmem_limit_bytes=4 * 1024 * 1024)
    outgoing = pl.pallas_call(
        pack_kernel,
        out_shape=jax.ShapeDtypeStruct((cols_count, 9 * planes_dev, LANES), FLOAT),
        in_specs=vmem(1),
        out_specs=vmem(1)[0],
        compiler_params=small,
        cost_estimate=pl.CostEstimate(flops=0, bytes_accessed=600_000, transcendentals=0),
        name="pack",
    )(slc.reshape(planes_dev, rows_dev, cols_all))
    received = lax.all_to_all(outgoing, "date", split_axis=0, concat_axis=0, tiled=True)
    own = canonical(received, dates_dev)
    far, near = [
        lax.ppermute(
            own,
            "row",
            [
                pair
                for low in range(first, rows_count - 1, 2)
                for pair in ((low, low + 1), (low + 1, low))
            ],
        )
        for first in (1, 0)
    ]

    picks, population, row_sub, row_lane, col_lane = pl.pallas_call(
        prepare_kernel,
        out_shape=(
            jax.ShapeDtypeStruct((BLOCKS, 64, 256), HALF_FLOAT),
            jax.ShapeDtypeStruct((TILE, LANES), FLOAT),
            jax.ShapeDtypeStruct((TAP_COUNT, 64, LANES), FLOAT),
            jax.ShapeDtypeStruct((TAP_COUNT, TILE, LANES), FLOAT),
            jax.ShapeDtypeStruct((TAP_COUNT, TILE, LANES), FLOAT),
        ),
        in_specs=[pl.BlockSpec(memory_space=pltpu.SMEM)] + vmem(1),
        out_specs=tuple(vmem(5)),
        scratch_shapes=[pltpu.VMEM((LANES, LANES), jnp.int32)],
        compiler_params=small,
        cost_estimate=pl.CostEstimate(flops=4_000_000, bytes_accessed=1_000_000, transcendentals=0),
        name="prepare",
    )(offsets, masks)

    linked, eigen = pl.pallas_call(
        link_kernel,
        out_shape=(
            jax.ShapeDtypeStruct((2 * NDATE * TILE, LANES), FLOAT),
            jax.ShapeDtypeStruct((TILE, LANES), FLOAT),
        ),
        in_specs=vmem(8),
        out_specs=tuple(vmem(2)),
        scratch_shapes=[
            pltpu.VMEM((8, LANES, LANES), FLOAT),
            pltpu.VMEM((2 * LANES, LANES), FLOAT),
            pltpu.VMEM((8, LANES + 16, LANES), FLOAT),
            pltpu.VMEM((BLOCKS, 256, LANES), HALF_FLOAT),
            pltpu.VMEM((BLOCKS, 256, LANES), HALF_FLOAT),
            pltpu.VMEM((8, LANES, LANES), FLOAT),
        ],
        compiler_params=pltpu.CompilerParams(vmem_limit_bytes=16 * 1024 * 1024),
        cost_estimate=pl.CostEstimate(
            flops=1_000_000_000, bytes_accessed=2_000_000, transcendentals=0
        ),
        name="link",
    )(own, far, near, picks, population, row_sub, row_lane, col_lane)
    return linked.reshape(2, NDATE, TILE, LANES), eigen


def solution(mesh):
    in_specs = (P(None, "date", "row", None), P(), P(None, "row", "date"))
    out_specs = (P(None, None, "row", "date"), P("row", "date"))
    return jax.shard_map(
        on_device, mesh=mesh, in_specs=in_specs, out_specs=out_specs, check_vma=False
    )
```

```python
import functools

import jax
import jax.numpy as jnp
from jax import lax
from jax.experimental import pallas as pl
from jax.experimental.pallas import tpu as pltpu
from jax.sharding import PartitionSpec as P

NDATE = 32
SLOT_COLS = 9
EPSILON = 1e-06
LANES = 128
TILE = 8
GROUPS = 8
TAP_COUNT = 8
WINDOW_ROWS = 16
WINDOW_COLS = 136
BLOCKS = 16

FLOAT = jnp.float32
HALF_FLOAT = jnp.bfloat16


def lane_ids(shape):
    return lax.broadcasted_iota(jnp.int32, shape, len(shape) - 1)


def sublane_ids(shape):
    return lax.broadcasted_iota(jnp.int32, shape, len(shape) - 2)


def pack_kernel(slc_ref, send_ref):
    planes = slc_ref.shape[0]
    blocks = send_ref.shape[0]
    for block in range(blocks):
        for plane in range(planes):
            send_ref[block, pl.ds(plane, TILE, stride=planes), :] = slc_ref[
                plane, :, block * LANES : (block + 1) * LANES
            ]
    lanes = lane_ids((planes, LANES))
    rims = [jnp.zeros((planes, LANES), FLOAT) for _ in range(blocks)]
    for row in range(TILE):
        start = 16 * row
        turned = [
            pltpu.roll(
                send_ref[block, row * planes : (row + 1) * planes, :],
                (start + 8) % LANES,
                axis=1,
            )
            for block in range(blocks)
        ]
        left = (lanes >= start) & (lanes < start + 8)
        right = (lanes >= start + 8) & (lanes < start + 16)
        for block in range(blocks):
            if block > 0:
                rims[block] = jnp.where(left, turned[block - 1], rims[block])
            if block < blocks - 1:
                rims[block] = jnp.where(right, turned[block + 1], rims[block])
    for block in range(blocks):
        send_ref[block, TILE * planes : (TILE + 1) * planes, :] = rims[block]


def tap_weight(distance):
    spread = jnp.abs(2 * distance - 1)
    return jnp.where(spread == 1, 0.5625, jnp.where(spread == 3, -0.0625, 0.0)).astype(FLOAT)


def prepare_kernel(
    offsets_ref, masks_ref, picks_ref, population_ref, row_sub_ref, row_lane_ref, col_lane_ref, words_ref
):
    words = masks_ref.shape[0]
    below = near_is_below()
    total = jnp.zeros((TILE, LANES), jnp.int32)
    for word in range(words):
        bits = masks_ref[word]
        bits = bits - (lax.shift_right_logical(bits, 1) & 0x55555555)
        bits = (bits & 0x33333333) + (lax.shift_right_logical(bits, 2) & 0x33333333)
        bits = (bits + lax.shift_right_logical(bits, 4)) & 0x0F0F0F0F
        bits = bits + lax.shift_right_logical(bits, 8)
        bits = bits + lax.shift_right_logical(bits, 16)
        total = total + (bits & 0xFF)
    population_ref[...] = total.astype(FLOAT)

    lanes = lane_ids((TILE, LANES))
    subs = sublane_ids((TILE, LANES))
    lane_dates = ((lanes % 64) // 8) * 4 + lanes % 4
    row_shift = jnp.zeros((TILE, LANES), jnp.int32)
    col_shift = jnp.zeros((TILE, LANES), jnp.int32)
    for date in range(NDATE):
        here = lane_dates == date
        row_shift = jnp.where(here, offsets_ref[0, date], row_shift)
        col_shift = jnp.where(here, offsets_ref[1, date], col_shift)
    for tap in range(TAP_COUNT):
        row_lane_ref[tap] = tap_weight(tap - 3 - row_shift)
        col_lane_ref[tap] = tap_weight(tap - 3 - col_shift)
    for group in range(GROUPS):
        shift = jnp.zeros((TILE, LANES), jnp.int32)
        for date in range(4):
            shift = jnp.where(subs % 4 == date, offsets_ref[0, 4 * group + date], shift)
        for tap in range(TAP_COUNT):
            row_sub_ref[tap, group * TILE : (group + 1) * TILE, :] = tap_weight(tap - 3 - shift)

    flat = [masks_ref[word] for word in range(words)]
    flat = flat + [jnp.zeros((TILE, LANES), jnp.int32)] * (LANES // TILE - words)
    words_ref[...] = jnp.transpose(jnp.concatenate(flat, axis=0))

    def one_block(block, carry):
        packed = words_ref[pl.ds(pl.multiple_of(block * TILE, TILE), TILE), :]
        for row_pair in range(TILE // 2):
            spread = [[], []]
            for row in (2 * row_pair, 2 * row_pair + 1):
                row_words = [
                    jnp.broadcast_to(
                        packed[:, word * TILE + row : word * TILE + row + 1], (TILE, LANES)
                    )
                    for word in range(words)
                ]
                for half in range(2):
                    near = 8 * half + lanes // 16 - row
                    across = lanes % 16 - subs
                    inside = (near >= 0) & (near <= 8) & (across >= 0) & (across <= 8)
                    amount = jnp.where(inside, (near & 1) * SLOT_COLS + across, 31)
                    first = max(0, 8 * half - row) // 2
                    last = min(8, 8 * half + 7 - row) // 2
                    chosen = row_words[first]
                    for word in range(first + 1, last + 1):
                        chosen = jnp.where(near >= 2 * word, row_words[word], chosen)
                    bits = lax.shift_right_logical(chosen, amount) & 1
                    spread[half].append(bits.astype(FLOAT))
            low_half, high_half = [jnp.concatenate(half, axis=0) for half in spread]
            rows = slice(16 * row_pair, 16 * row_pair + 16)
            picks_ref[block, rows, :LANES] = jnp.where(below, high_half, low_half).astype(HALF_FLOAT)
            picks_ref[block, rows, LANES:] = jnp.where(below, low_half, high_half).astype(HALF_FLOAT)
        return carry

    lax.fori_loop(0, BLOCKS, one_block, 0)


def split_halves(values):
    high = values.astype(HALF_FLOAT)
    low = values - high.astype(FLOAT)
    return high, low


def dot(a, b, contract):
    return lax.dot_general(
        a, b, (((contract[0],), (contract[1],)), ((), ())), preferred_element_type=FLOAT
    )


def near_is_below():
    return (lax.axis_index("row") + lax.axis_index("date")) % 2 == 0


def resample_half(
    own_ref,
    other_ref,
    below,
    row_sub_ref,
    row_lane_ref,
    col_lane_ref,
    z_ref,
    y_ref,
    mixed_ref,
    rims_ref,
    turned_ref,
):
    row_at, row_count = lax.axis_index("row"), lax.axis_size("row")
    col_at, col_count = lax.axis_index("date"), lax.axis_size("date")

    def mix_group(group, carry):
        weights = [
            row_sub_ref[tap, pl.ds(pl.multiple_of(group * TILE, TILE), TILE), :]
            for tap in range(TAP_COUNT)
        ]
        own = [own_ref[group, row * TILE : (row + 1) * TILE, :] for row in range(TILE)]
        other = [other_ref[group, row * TILE : (row + 1) * TILE, :] for row in range(TILE)]
        raw = [jnp.where(below, a, b) for a, b in zip(own, other)]
        raw = raw + [jnp.where(below, b, a) for a, b in zip(own, other)]
        for row in range(8):
            mixed = weights[0] * raw[row + 1]
            for tap in range(1, TAP_COUNT):
                mixed = mixed + weights[tap] * raw[row + 1 + tap]
            start = pl.multiple_of((row // 4) * 64 + group * TILE, TILE)
            mixed_ref[row % 4, pl.ds(start, TILE), :] = mixed
        return carry

    lax.fori_loop(0, GROUPS, mix_group, 0, unroll=2)

    lanes = lane_ids((1, LANES))
    lower = lanes < 64
    own, other = [
        source[:, 8 * TILE : 9 * TILE, :].reshape(64, LANES) for source in (own_ref, other_ref)
    ]
    first, second = jnp.where(below, own, other), jnp.where(below, other, own)
    far_first, far_second = pltpu.roll(first, 64, axis=1), pltpu.roll(second, 64, axis=1)
    rims_ref[0:LANES, :] = jnp.transpose(
        jnp.concatenate([first, jnp.where(lower, far_first, far_second)], axis=0)
    )
    rims_ref[LANES : 2 * LANES, :] = jnp.transpose(jnp.concatenate([second, far_second], axis=0))
    row_weights = [row_lane_ref[tap, 0:1, :] for tap in range(TAP_COUNT)]
    for row in range(4):
        turned_ref[row, 8 : 8 + LANES, :] = jnp.transpose(mixed_ref[row])
        rim = row_weights[0] * rims_ref[(row + 1) * 16 : (row + 2) * 16, :]
        for tap in range(1, TAP_COUNT):
            rim = rim + row_weights[tap] * rims_ref[(row + 1 + tap) * 16 : (row + 2 + tap) * 16, :]
        turned_ref[row, 0:8, :] = rim[0:8]
        turned_ref[row, 8 + LANES : 16 + LANES, :] = rim[8:16]

    places = sublane_ids((WINDOW_COLS, LANES))
    inside = ((places >= 4) | (col_at > 0)) & ((places < 132) | (col_at < col_count - 1))
    row_inside = (lower & (below | (row_at > 0))) | (
        (lanes >= 64) & (jnp.logical_not(below) | (row_at < row_count - 1))
    )
    inside = inside & row_inside
    term = lax.broadcasted_iota(jnp.int32, (2 * LANES, 2 * LANES), 0) % LANES
    gives = lax.broadcasted_iota(jnp.int32, (2 * LANES, 2 * LANES), 1)
    same_part = ((term % 8) < 4) == (gives < LANES)
    sums = jnp.where(((term < 64) == ((gives % LANES) < 64)) & same_part, 1.0, 0.0).astype(HALF_FLOAT)

    def store_windows(target, row, values):
        high, low = split_halves(values)
        high = high.astype(FLOAT)
        rows = (
            jnp.where(lower, high, pltpu.roll(low, 64, axis=1)),
            jnp.where(lower, pltpu.roll(high, 64, axis=1), low),
        )
        for part in range(2):
            start = (row + 4 * part) * 16
            for block in range(BLOCKS):
                target[block, start : start + 16, :] = rows[part][
                    block * 8 : block * 8 + 16
                ].astype(HALF_FLOAT)

    for row in range(4):
        mixed = col_lane_ref[0, 0:1, :] * turned_ref[row, 1 : 1 + WINDOW_COLS, :]
        for tap in range(1, TAP_COUNT):
            mixed = mixed + col_lane_ref[tap, 0:1, :] * turned_ref[
                row, 1 + tap : 1 + tap + WINDOW_COLS, :
            ]
        z = jnp.where(inside, mixed, 0.0)
        high, low = split_halves(z)
        total = dot(jnp.concatenate([high, low.astype(HALF_FLOAT)], axis=1), sums, (1, 0))
        y = z * total[:, :LANES] + swapped(z) * total[:, LANES:]
        store_windows(z_ref, row, z)
        store_windows(y_ref, row, y)


def swapped(values):
    real = (lane_ids((1, LANES)) % 8) < 4
    return jnp.where(real, pltpu.roll(values, LANES - 4, axis=1), -pltpu.roll(values, 4, axis=1))


def near_kernel(own_ref, near_ref, row_sub_ref, row_lane_ref, col_lane_ref, *rest):
    resample_half(
        own_ref, near_ref, near_is_below(), row_sub_ref, row_lane_ref, col_lane_ref, *rest
    )


def link_kernel(
    own_ref,
    far_ref,
    row_sub_ref,
    row_lane_ref,
    col_lane_ref,
    near_z_ref,
    near_y_ref,
    picks_ref,
    population_ref,
    linked_ref,
    eigen_ref,
    far_z_ref,
    far_y_ref,
    mixed_ref,
    rims_ref,
    turned_ref,
    result_ref,
):
    resample_half(
        own_ref,
        far_ref,
        jnp.logical_not(near_is_below()),
        row_sub_ref,
        row_lane_ref,
        col_lane_ref,
        far_z_ref,
        far_y_ref,
        mixed_ref,
        rims_ref,
        turned_ref,
    )
    lower = lane_ids((1, LANES)) < 64

    for block in range(BLOCKS):
        z = jnp.concatenate([near_z_ref[block], far_z_ref[block]], axis=0)
        y = jnp.concatenate([near_y_ref[block], far_y_ref[block]], axis=0)
        picks = picks_ref[block]
        first = dot(picks, y, (1, 0))
        first = first + pltpu.roll(first, 64, axis=1)
        high, low = split_halves(jnp.concatenate([first, swapped(first)], axis=0))
        inner = dot(
            jnp.concatenate([high, low.astype(HALF_FLOAT)], axis=1),
            jnp.concatenate([z, z], axis=1),
            (1, 1),
        )
        high, low = split_halves(inner)
        chosen = jnp.concatenate([high, low.astype(HALF_FLOAT)], axis=0) * jnp.concatenate(
            [picks] * 4, axis=0
        )
        outer = dot(chosen, z, (1, 0))
        outer = outer[:128] + outer[128:]
        outer = outer + pltpu.roll(outer, 64, axis=1)
        second = outer[:64] - swapped(outer[64:])
        both = jnp.where(lower, second, first)
        for row in range(8):
            result_ref[row, block * 8 : block * 8 + 8, :] = both[row * 8 : row * 8 + 8]

    inverse = 1.0 / population_ref[...]
    for row in range(8):
        turned = jnp.transpose(result_ref[row])
        second, first = turned[:64], turned[64:]
        scale = inverse[row : row + 1]
        square = scale * scale
        norm_first = jnp.sqrt(jnp.sum(first * first, axis=0, keepdims=True) * square + EPSILON)
        norm_last = jnp.sqrt(
            jnp.sum(second * second, axis=0, keepdims=True) * (square * square) + EPSILON
        )
        eigen_ref[row : row + 1, :] = norm_last / norm_first
        linked = second * (square * (jnp.sqrt(jnp.float32(NDATE)) / norm_last))
        for group in range(GROUPS):
            for part in range(2):
                begin = ((part * NDATE + 4 * group) * 8) + row
                at = group * 8 + part * 4
                linked_ref[pl.ds(begin, 4, stride=8), :] = linked[at : at + 4]


def canonical(received, dates_dev):
    sources = received.shape[0]
    if dates_dev == 4:
        return received
    cells = received.reshape(sources, 9, 2, dates_dev, LANES)
    cells = jnp.transpose(cells, (1, 2, 0, 3, 4)).reshape(9, 2, GROUPS, 4, LANES)
    return jnp.transpose(cells, (2, 0, 1, 3, 4)).reshape(GROUPS, 9 * TILE, LANES)


def vmem(count):
    return [pl.BlockSpec(memory_space=pltpu.VMEM)] * count


def on_device(slc, offsets, masks):
    dates_dev = slc.shape[1]
    rows_dev = slc.shape[2]
    cols_all = slc.shape[3]
    rows_count = lax.axis_size("row")
    cols_count = lax.axis_size("date")
    planes_dev = 2 * dates_dev
    assert rows_dev == TILE and cols_all == cols_count * LANES

    small = pltpu.CompilerParams(vmem_limit_bytes=4 * 1024 * 1024)
    outgoing = pl.pallas_call(
        pack_kernel,
        out_shape=jax.ShapeDtypeStruct((cols_count, 9 * planes_dev, LANES), FLOAT),
        in_specs=vmem(1),
        out_specs=vmem(1)[0],
        compiler_params=small,
        cost_estimate=pl.CostEstimate(flops=0, bytes_accessed=600_000, transcendentals=0),
        name="pack",
    )(slc.reshape(planes_dev, rows_dev, cols_all))
    received = lax.all_to_all(outgoing, "date", split_axis=0, concat_axis=0, tiled=True)
    own = canonical(received, dates_dev)
    near, far = [
        lax.ppermute(
            own,
            ("date", "row"),
            [
                (date * rows_count + source, date * rows_count + target)
                for date in range(cols_count)
                for low in range((date + turn) % 2, rows_count - 1, 2)
                for source, target in ((low, low + 1), (low + 1, low))
            ],
        )
        for turn in range(2)
    ]
    picks, population, row_sub, row_lane, col_lane = pl.pallas_call(
        prepare_kernel,
        out_shape=(
            jax.ShapeDtypeStruct((BLOCKS, 64, 256), HALF_FLOAT),
            jax.ShapeDtypeStruct((TILE, LANES), FLOAT),
            jax.ShapeDtypeStruct((TAP_COUNT, 64, LANES), FLOAT),
            jax.ShapeDtypeStruct((TAP_COUNT, TILE, LANES), FLOAT),
            jax.ShapeDtypeStruct((TAP_COUNT, TILE, LANES), FLOAT),
        ),
        in_specs=[pl.BlockSpec(memory_space=pltpu.SMEM)] + vmem(1),
        out_specs=tuple(vmem(5)),
        scratch_shapes=[pltpu.VMEM((LANES, LANES), jnp.int32)],
        compiler_params=small,
        cost_estimate=pl.CostEstimate(flops=4_000_000, bytes_accessed=1_000_000, transcendentals=0),
        name="prepare",
    )(offsets, masks)

    half_scratch = [
        pltpu.VMEM((4, LANES, LANES), FLOAT),
        pltpu.VMEM((2 * LANES, LANES), FLOAT),
        pltpu.VMEM((4, LANES + 16, LANES), FLOAT),
    ]
    windows = jax.ShapeDtypeStruct((BLOCKS, LANES, LANES), HALF_FLOAT)
    near_z, near_y = pl.pallas_call(
        near_kernel,
        out_shape=(windows, windows),
        in_specs=vmem(5),
        out_specs=tuple(vmem(2)),
        scratch_shapes=half_scratch,
        compiler_params=small,
        cost_estimate=pl.CostEstimate(
            flops=200_000_000, bytes_accessed=2_000_000, transcendentals=0
        ),
        name="near",
    )(own, near, row_sub, row_lane, col_lane)
    linked, eigen = pl.pallas_call(
        link_kernel,
        out_shape=(
            jax.ShapeDtypeStruct((2 * NDATE * TILE, LANES), FLOAT),
            jax.ShapeDtypeStruct((TILE, LANES), FLOAT),
        ),
        in_specs=vmem(9),
        out_specs=tuple(vmem(2)),
        scratch_shapes=[
            pltpu.VMEM((BLOCKS, LANES, LANES), HALF_FLOAT),
            pltpu.VMEM((BLOCKS, LANES, LANES), HALF_FLOAT),
        ]
        + half_scratch
        + [pltpu.VMEM((8, LANES, LANES), FLOAT)],
        compiler_params=pltpu.CompilerParams(vmem_limit_bytes=16 * 1024 * 1024),
        cost_estimate=pl.CostEstimate(
            flops=1_000_000_000, bytes_accessed=2_000_000, transcendentals=0
        ),
        name="link",
    )(own, far, row_sub, row_lane, col_lane, near_z, near_y, picks, population)
    return linked.reshape(2, NDATE, TILE, LANES), eigen


def solution(mesh):
    in_specs = (P(None, "date", "row", None), P(), P(None, "row", "date"))
    out_specs = (P(None, None, "row", "date"), P("row", "date"))
    return jax.shard_map(
        on_device, mesh=mesh, in_specs=in_specs, out_specs=out_specs, check_vma=False
    )
```

```python
import functools

import jax
import jax.numpy as jnp
from jax import lax
from jax.experimental import pallas as pl
from jax.experimental.pallas import tpu as pltpu
from jax.sharding import PartitionSpec as P

NDATE = 32
SLOT_COLS = 9
EPSILON = 1e-06
LANES = 128
TILE = 8
GROUPS = 8
TAP_COUNT = 8
WINDOW_ROWS = 16
WINDOW_COLS = 136
BLOCKS = 16

FLOAT = jnp.float32
HALF_FLOAT = jnp.bfloat16


def lane_ids(shape):
    return lax.broadcasted_iota(jnp.int32, shape, len(shape) - 1)


def sublane_ids(shape):
    return lax.broadcasted_iota(jnp.int32, shape, len(shape) - 2)


def pack_kernel(slc_ref, send_ref):
    planes = slc_ref.shape[0]
    blocks = send_ref.shape[0]
    for block in range(blocks):
        for plane in range(planes):
            send_ref[block, pl.ds(plane, TILE, stride=planes), :] = slc_ref[
                plane, :, block * LANES : (block + 1) * LANES
            ]
    lanes = lane_ids((planes, LANES))
    rims = [jnp.zeros((planes, LANES), FLOAT) for _ in range(blocks)]
    for row in range(TILE):
        start = 16 * row
        turned = [
            pltpu.roll(
                send_ref[block, row * planes : (row + 1) * planes, :],
                (start + 8) % LANES,
                axis=1,
            )
            for block in range(blocks)
        ]
        left = (lanes >= start) & (lanes < start + 8)
        right = (lanes >= start + 8) & (lanes < start + 16)
        for block in range(blocks):
            if block > 0:
                rims[block] = jnp.where(left, turned[block - 1], rims[block])
            if block < blocks - 1:
                rims[block] = jnp.where(right, turned[block + 1], rims[block])
    for block in range(blocks):
        send_ref[block, TILE * planes : (TILE + 1) * planes, :] = rims[block]


def tap_weight(distance):
    spread = jnp.abs(2 * distance - 1)
    return jnp.where(spread == 1, 0.5625, jnp.where(spread == 3, -0.0625, 0.0)).astype(FLOAT)


def prepare_kernel(
    offsets_ref, masks_ref, picks_ref, population_ref, row_sub_ref, row_lane_ref, col_lane_ref, words_ref
):
    words = masks_ref.shape[0]
    below = near_is_below()
    total = jnp.zeros((TILE, LANES), jnp.int32)
    for word in range(words):
        bits = masks_ref[word]
        bits = bits - (lax.shift_right_logical(bits, 1) & 0x55555555)
        bits = (bits & 0x33333333) + (lax.shift_right_logical(bits, 2) & 0x33333333)
        bits = (bits + lax.shift_right_logical(bits, 4)) & 0x0F0F0F0F
        bits = bits + lax.shift_right_logical(bits, 8)
        bits = bits + lax.shift_right_logical(bits, 16)
        total = total + (bits & 0xFF)
    population_ref[...] = total.astype(FLOAT)

    lanes = lane_ids((TILE, LANES))
    subs = sublane_ids((TILE, LANES))
    lane_dates = ((lanes % 64) // 8) * 4 + lanes % 4
    row_shift = jnp.zeros((TILE, LANES), jnp.int32)
    col_shift = jnp.zeros((TILE, LANES), jnp.int32)
    for date in range(NDATE):
        here = lane_dates == date
        row_shift = jnp.where(here, offsets_ref[0, date], row_shift)
        col_shift = jnp.where(here, offsets_ref[1, date], col_shift)
    for tap in range(TAP_COUNT):
        row_lane_ref[tap] = tap_weight(tap - 3 - row_shift)
        col_lane_ref[tap] = tap_weight(tap - 3 - col_shift)
    for group in range(GROUPS):
        shift = jnp.zeros((TILE, LANES), jnp.int32)
        for date in range(4):
            shift = jnp.where(subs % 4 == date, offsets_ref[0, 4 * group + date], shift)
        for tap in range(TAP_COUNT):
            row_sub_ref[tap, group * TILE : (group + 1) * TILE, :] = tap_weight(tap - 3 - shift)

    flat = [masks_ref[word] for word in range(words)]
    flat = flat + [jnp.zeros((TILE, LANES), jnp.int32)] * (LANES // TILE - words)
    words_ref[...] = jnp.transpose(jnp.concatenate(flat, axis=0))

    def one_block(block, carry):
        packed = words_ref[pl.ds(pl.multiple_of(block * TILE, TILE), TILE), :]
        for row_pair in range(TILE // 2):
            spread = [[], []]
            for row in (2 * row_pair, 2 * row_pair + 1):
                row_words = [
                    jnp.broadcast_to(
                        packed[:, word * TILE + row : word * TILE + row + 1], (TILE, LANES)
                    )
                    for word in range(words)
                ]
                for half in range(2):
                    near = 8 * half + lanes // 16 - row
                    across = lanes % 16 - subs
                    inside = (near >= 0) & (near <= 8) & (across >= 0) & (across <= 8)
                    amount = jnp.where(inside, (near & 1) * SLOT_COLS + across, 31)
                    first = max(0, 8 * half - row) // 2
                    last = min(8, 8 * half + 7 - row) // 2
                    chosen = row_words[first]
                    for word in range(first + 1, last + 1):
                        chosen = jnp.where(near >= 2 * word, row_words[word], chosen)
                    bits = lax.shift_right_logical(chosen, amount) & 1
                    spread[half].append(bits.astype(FLOAT))
            low_half, high_half = [jnp.concatenate(half, axis=0) for half in spread]
            rows = slice(16 * row_pair, 16 * row_pair + 16)
            picks_ref[block, rows, :LANES] = jnp.where(below, high_half, low_half).astype(HALF_FLOAT)
            picks_ref[block, rows, LANES:] = jnp.where(below, low_half, high_half).astype(HALF_FLOAT)
        return carry

    lax.fori_loop(0, BLOCKS, one_block, 0)


def split_halves(values):
    high = values.astype(HALF_FLOAT)
    low = values - high.astype(FLOAT)
    return high, low


def dot(a, b, contract):
    return lax.dot_general(
        a, b, (((contract[0],), (contract[1],)), ((), ())), preferred_element_type=FLOAT
    )


def near_is_below():
    return (lax.axis_index("row") + lax.axis_index("date")) % 2 == 0


def resample_half(
    own_ref,
    other_ref,
    below,
    row_sub_ref,
    row_lane_ref,
    col_lane_ref,
    z_ref,
    y_ref,
    mixed_ref,
    rims_ref,
    turned_ref,
):
    row_at, row_count = lax.axis_index("row"), lax.axis_size("row")
    col_at, col_count = lax.axis_index("date"), lax.axis_size("date")

    exists = (below & (row_at < row_count - 1)) | (jnp.logical_not(below) & (row_at > 0))

    def mix_group(group, carry):
        weights = [
            row_sub_ref[tap, pl.ds(pl.multiple_of(group * TILE, TILE), TILE), :]
            for tap in range(TAP_COUNT)
        ]
        own = [own_ref[group, row * TILE : (row + 1) * TILE, :] for row in range(TILE)]
        other = [
            jnp.where(exists, other_ref[group, row * TILE : (row + 1) * TILE, :], 0.0)
            for row in range(TILE)
        ]
        raw = [jnp.where(below, a, b) for a, b in zip(own, other)]
        raw = raw + [jnp.where(below, b, a) for a, b in zip(own, other)]
        for row in range(8):
            mixed = weights[0] * raw[row + 1]
            for tap in range(1, TAP_COUNT):
                mixed = mixed + weights[tap] * raw[row + 1 + tap]
            start = pl.multiple_of((row // 4) * 64 + group * TILE, TILE)
            mixed_ref[row % 4, pl.ds(start, TILE), :] = mixed
        return carry

    lax.fori_loop(0, GROUPS, mix_group, 0, unroll=2)

    lanes = lane_ids((1, LANES))
    lower = lanes < 64
    own, other = [
        source[:, 8 * TILE : 9 * TILE, :].reshape(64, LANES) for source in (own_ref, other_ref)
    ]
    other = jnp.where(exists, other, 0.0)
    first, second = jnp.where(below, own, other), jnp.where(below, other, own)
    far_first, far_second = pltpu.roll(first, 64, axis=1), pltpu.roll(second, 64, axis=1)
    rims_ref[0:LANES, :] = jnp.transpose(
        jnp.concatenate([first, jnp.where(lower, far_first, far_second)], axis=0)
    )
    rims_ref[LANES : 2 * LANES, :] = jnp.transpose(jnp.concatenate([second, far_second], axis=0))
    row_weights = [row_lane_ref[tap, 0:1, :] for tap in range(TAP_COUNT)]
    for row in range(4):
        turned_ref[row, 8 : 8 + LANES, :] = jnp.transpose(mixed_ref[row])
        rim = row_weights[0] * rims_ref[(row + 1) * 16 : (row + 2) * 16, :]
        for tap in range(1, TAP_COUNT):
            rim = rim + row_weights[tap] * rims_ref[(row + 1 + tap) * 16 : (row + 2 + tap) * 16, :]
        turned_ref[row, 0:8, :] = rim[0:8]
        turned_ref[row, 8 + LANES : 16 + LANES, :] = rim[8:16]

    places = sublane_ids((WINDOW_COLS, LANES))
    inside = ((places >= 4) | (col_at > 0)) & ((places < 132) | (col_at < col_count - 1))
    row_inside = (lower & (below | (row_at > 0))) | (
        (lanes >= 64) & (jnp.logical_not(below) | (row_at < row_count - 1))
    )
    inside = inside & row_inside
    term = lax.broadcasted_iota(jnp.int32, (2 * LANES, 2 * LANES), 0) % LANES
    gives = lax.broadcasted_iota(jnp.int32, (2 * LANES, 2 * LANES), 1)
    same_part = ((term % 8) < 4) == (gives < LANES)
    sums = jnp.where(((term < 64) == ((gives % LANES) < 64)) & same_part, 1.0, 0.0).astype(HALF_FLOAT)

    def store_windows(target, row, values):
        high, low = split_halves(values)
        high = high.astype(FLOAT)
        rows = (
            jnp.where(lower, high, pltpu.roll(low, 64, axis=1)),
            jnp.where(lower, pltpu.roll(high, 64, axis=1), low),
        )
        for part in range(2):
            start = (row + 4 * part) * 16
            for block in range(BLOCKS):
                target[block, start : start + 16, :] = rows[part][
                    block * 8 : block * 8 + 16
                ].astype(HALF_FLOAT)

    for row in range(4):
        mixed = col_lane_ref[0, 0:1, :] * turned_ref[row, 1 : 1 + WINDOW_COLS, :]
        for tap in range(1, TAP_COUNT):
            mixed = mixed + col_lane_ref[tap, 0:1, :] * turned_ref[
                row, 1 + tap : 1 + tap + WINDOW_COLS, :
            ]
        z = jnp.where(inside, mixed, 0.0)
        high, low = split_halves(z)
        total = dot(jnp.concatenate([high, low.astype(HALF_FLOAT)], axis=1), sums, (1, 0))
        y = z * total[:, :LANES] + swapped(z) * total[:, LANES:]
        store_windows(z_ref, row, z)
        store_windows(y_ref, row, y)


def swapped(values):
    real = (lane_ids((1, LANES)) % 8) < 4
    return jnp.where(real, pltpu.roll(values, LANES - 4, axis=1), -pltpu.roll(values, 4, axis=1))


def near_kernel(own_ref, near_ref, row_sub_ref, row_lane_ref, col_lane_ref, *rest):
    resample_half(
        own_ref, near_ref, near_is_below(), row_sub_ref, row_lane_ref, col_lane_ref, *rest
    )


def link_kernel(
    own_ref,
    far_ref,
    row_sub_ref,
    row_lane_ref,
    col_lane_ref,
    near_z_ref,
    near_y_ref,
    picks_ref,
    population_ref,
    linked_ref,
    eigen_ref,
    far_z_ref,
    far_y_ref,
    mixed_ref,
    rims_ref,
    turned_ref,
    result_ref,
    first_ref,
    vectors_ref,
    chosen_ref,
):
    resample_half(
        own_ref,
        far_ref,
        jnp.logical_not(near_is_below()),
        row_sub_ref,
        row_lane_ref,
        col_lane_ref,
        far_z_ref,
        far_y_ref,
        mixed_ref,
        rims_ref,
        turned_ref,
    )
    lower = lane_ids((1, LANES)) < 64

    for block in range(BLOCKS):
        y = jnp.concatenate([near_y_ref[block], far_y_ref[block]], axis=0)
        first = dot(picks_ref[block], y, (1, 0))
        first = first + pltpu.roll(first, 64, axis=1)
        high, low = split_halves(jnp.concatenate([first, swapped(first)], axis=0))
        first_ref[block] = first
        vectors_ref[block, :, :LANES] = high
        vectors_ref[block, :, LANES:] = low.astype(HALF_FLOAT)

    for block in range(BLOCKS):
        z = jnp.concatenate([near_z_ref[block], far_z_ref[block]], axis=0)
        inner = dot(vectors_ref[block], jnp.concatenate([z, z], axis=1), (1, 1))
        high, low = split_halves(inner)
        picks = picks_ref[block]
        picks = jnp.concatenate([picks, picks], axis=0)
        chosen_ref[block, :128, :] = high * picks
        chosen_ref[block, 128:, :] = low.astype(HALF_FLOAT) * picks

    for block in range(BLOCKS):
        z = jnp.concatenate([near_z_ref[block], far_z_ref[block]], axis=0)
        outer = dot(chosen_ref[block], z, (1, 0))
        outer = outer[:128] + outer[128:]
        outer = outer + pltpu.roll(outer, 64, axis=1)
        second = outer[:64] - swapped(outer[64:])
        both = jnp.where(lower, second, first_ref[block])
        for row in range(8):
            result_ref[row, block * 8 : block * 8 + 8, :] = both[row * 8 : row * 8 + 8]

    inverse = 1.0 / population_ref[...]
    for row in range(8):
        turned = jnp.transpose(result_ref[row])
        second, first = turned[:64], turned[64:]
        scale = inverse[row : row + 1]
        square = scale * scale
        norm_first = jnp.sqrt(jnp.sum(first * first, axis=0, keepdims=True) * square + EPSILON)
        norm_last = jnp.sqrt(
            jnp.sum(second * second, axis=0, keepdims=True) * (square * square) + EPSILON
        )
        eigen_ref[row : row + 1, :] = norm_last / norm_first
        linked = second * (square * (jnp.sqrt(jnp.float32(NDATE)) / norm_last))
        for group in range(GROUPS):
            for part in range(2):
                begin = ((part * NDATE + 4 * group) * 8) + row
                at = group * 8 + part * 4
                linked_ref[pl.ds(begin, 4, stride=8), :] = linked[at : at + 4]


def canonical(received, dates_dev):
    sources = received.shape[0]
    if dates_dev == 4:
        return received
    cells = received.reshape(sources, 9, 2, dates_dev, LANES)
    cells = jnp.transpose(cells, (1, 2, 0, 3, 4)).reshape(9, 2, GROUPS, 4, LANES)
    return jnp.transpose(cells, (2, 0, 1, 3, 4)).reshape(GROUPS, 9 * TILE, LANES)


def partner(row, turn, rows_count):
    other = row + 1 if (row + turn) % 2 == 0 else row - 1
    return other if 0 <= other < rows_count else row


def vmem(count):
    return [pl.BlockSpec(memory_space=pltpu.VMEM)] * count


def on_device(slc, offsets, masks):
    dates_dev = slc.shape[1]
    rows_dev = slc.shape[2]
    cols_all = slc.shape[3]
    rows_count = lax.axis_size("row")
    cols_count = lax.axis_size("date")
    planes_dev = 2 * dates_dev
    assert rows_dev == TILE and cols_all == cols_count * LANES

    small = pltpu.CompilerParams(vmem_limit_bytes=4 * 1024 * 1024)
    outgoing = pl.pallas_call(
        pack_kernel,
        out_shape=jax.ShapeDtypeStruct((cols_count, 9 * planes_dev, LANES), FLOAT),
        in_specs=vmem(1),
        out_specs=vmem(1)[0],
        compiler_params=small,
        cost_estimate=pl.CostEstimate(flops=0, bytes_accessed=600_000, transcendentals=0),
        name="pack",
    )(slc.reshape(planes_dev, rows_dev, cols_all))
    received = lax.all_to_all(outgoing, "date", split_axis=0, concat_axis=0, tiled=True)
    own = canonical(received, dates_dev)
    near, far = [
        lax.ppermute(
            own,
            ("date", "row"),
            [
                (date * rows_count + row, date * rows_count + partner(row, date + turn, rows_count))
                for date in range(cols_count)
                for row in range(rows_count)
            ],
        )
        for turn in range(2)
    ]
    picks, population, row_sub, row_lane, col_lane = pl.pallas_call(
        prepare_kernel,
        out_shape=(
            jax.ShapeDtypeStruct((BLOCKS, 64, 256), HALF_FLOAT),
            jax.ShapeDtypeStruct((TILE, LANES), FLOAT),
            jax.ShapeDtypeStruct((TAP_COUNT, 64, LANES), FLOAT),
            jax.ShapeDtypeStruct((TAP_COUNT, TILE, LANES), FLOAT),
            jax.ShapeDtypeStruct((TAP_COUNT, TILE, LANES), FLOAT),
        ),
        in_specs=[pl.BlockSpec(memory_space=pltpu.SMEM)] + vmem(1),
        out_specs=tuple(vmem(5)),
        scratch_shapes=[pltpu.VMEM((LANES, LANES), jnp.int32)],
        compiler_params=small,
        cost_estimate=pl.CostEstimate(flops=4_000_000, bytes_accessed=1_000_000, transcendentals=0),
        name="prepare",
    )(offsets, masks)

    half_scratch = [
        pltpu.VMEM((4, LANES, LANES), FLOAT),
        pltpu.VMEM((2 * LANES, LANES), FLOAT),
        pltpu.VMEM((4, LANES + 16, LANES), FLOAT),
    ]
    windows = jax.ShapeDtypeStruct((BLOCKS, LANES, LANES), HALF_FLOAT)
    near_z, near_y = pl.pallas_call(
        near_kernel,
        out_shape=(windows, windows),
        in_specs=vmem(5),
        out_specs=tuple(vmem(2)),
        scratch_shapes=half_scratch,
        compiler_params=small,
        cost_estimate=pl.CostEstimate(
            flops=200_000_000, bytes_accessed=2_000_000, transcendentals=0
        ),
        name="near",
    )(own, near, row_sub, row_lane, col_lane)
    linked, eigen = pl.pallas_call(
        link_kernel,
        out_shape=(
            jax.ShapeDtypeStruct((2 * NDATE * TILE, LANES), FLOAT),
            jax.ShapeDtypeStruct((TILE, LANES), FLOAT),
        ),
        in_specs=vmem(9),
        out_specs=tuple(vmem(2)),
        scratch_shapes=[
            pltpu.VMEM((BLOCKS, LANES, LANES), HALF_FLOAT),
            pltpu.VMEM((BLOCKS, LANES, LANES), HALF_FLOAT),
        ]
        + half_scratch
        + [
            pltpu.VMEM((8, LANES, LANES), FLOAT),
            pltpu.VMEM((BLOCKS, 64, LANES), FLOAT),
            pltpu.VMEM((BLOCKS, 128, 256), HALF_FLOAT),
            pltpu.VMEM((BLOCKS, 256, 256), HALF_FLOAT),
        ],
        compiler_params=pltpu.CompilerParams(vmem_limit_bytes=16 * 1024 * 1024),
        cost_estimate=pl.CostEstimate(
            flops=1_000_000_000, bytes_accessed=2_000_000, transcendentals=0
        ),
        name="link",
    )(own, far, row_sub, row_lane, col_lane, near_z, near_y, picks, population)
    return linked.reshape(2, NDATE, TILE, LANES), eigen


def solution(mesh):
    in_specs = (P(None, "date", "row", None), P(), P(None, "row", "date"))
    out_specs = (P(None, None, "row", "date"), P("row", "date"))
    return jax.shard_map(
        on_device, mesh=mesh, in_specs=in_specs, out_specs=out_specs, check_vma=False
    )
```

```python
import functools

import jax
import jax.numpy as jnp
from jax import lax
from jax.experimental import pallas as pl
from jax.experimental.pallas import tpu as pltpu
from jax.sharding import PartitionSpec as P

NDATE = 32
SLOT_COLS = 9
EPSILON = 1e-06
LANES = 128
TILE = 8
GROUPS = 8
TAP_COUNT = 8
WINDOW_ROWS = 16
WINDOW_COLS = 136
BLOCKS = 16

FLOAT = jnp.float32
HALF_FLOAT = jnp.bfloat16


def lane_ids(shape):
    return lax.broadcasted_iota(jnp.int32, shape, len(shape) - 1)


def sublane_ids(shape):
    return lax.broadcasted_iota(jnp.int32, shape, len(shape) - 2)


def pack_kernel(slc_ref, send_ref):
    planes = slc_ref.shape[0]
    blocks = send_ref.shape[0]
    for block in range(blocks):
        for plane in range(planes):
            send_ref[block, pl.ds(plane, TILE, stride=planes), :] = slc_ref[
                plane, :, block * LANES : (block + 1) * LANES
            ]
    lanes = lane_ids((planes, LANES))
    rims = [jnp.zeros((planes, LANES), FLOAT) for _ in range(blocks)]
    for row in range(TILE):
        start = 16 * row
        turned = [
            pltpu.roll(
                send_ref[block, row * planes : (row + 1) * planes, :],
                (start + 8) % LANES,
                axis=1,
            )
            for block in range(blocks)
        ]
        left = (lanes >= start) & (lanes < start + 8)
        right = (lanes >= start + 8) & (lanes < start + 16)
        for block in range(blocks):
            if block > 0:
                rims[block] = jnp.where(left, turned[block - 1], rims[block])
            if block < blocks - 1:
                rims[block] = jnp.where(right, turned[block + 1], rims[block])
    for block in range(blocks):
        send_ref[block, TILE * planes : (TILE + 1) * planes, :] = rims[block]


def tap_weight(distance):
    spread = jnp.abs(2 * distance - 1)
    return jnp.where(spread == 1, 0.5625, jnp.where(spread == 3, -0.0625, 0.0)).astype(FLOAT)


def prepare_kernel(
    offsets_ref, masks_ref, picks_ref, population_ref, row_sub_ref, row_lane_ref, col_lane_ref, words_ref
):
    words = masks_ref.shape[0]
    below = near_is_below()
    total = jnp.zeros((TILE, LANES), jnp.int32)
    for word in range(words):
        bits = masks_ref[word]
        bits = bits - (lax.shift_right_logical(bits, 1) & 0x55555555)
        bits = (bits & 0x33333333) + (lax.shift_right_logical(bits, 2) & 0x33333333)
        bits = (bits + lax.shift_right_logical(bits, 4)) & 0x0F0F0F0F
        bits = bits + lax.shift_right_logical(bits, 8)
        bits = bits + lax.shift_right_logical(bits, 16)
        total = total + (bits & 0xFF)
    population_ref[...] = total.astype(FLOAT)

    lanes = lane_ids((TILE, LANES))
    subs = sublane_ids((TILE, LANES))
    lane_dates = ((lanes % 64) // 8) * 4 + lanes % 4
    row_shift = jnp.zeros((TILE, LANES), jnp.int32)
    col_shift = jnp.zeros((TILE, LANES), jnp.int32)
    for date in range(NDATE):
        here = lane_dates == date
        row_shift = jnp.where(here, offsets_ref[0, date], row_shift)
        col_shift = jnp.where(here, offsets_ref[1, date], col_shift)
    for tap in range(TAP_COUNT):
        row_lane_ref[tap] = tap_weight(tap - 3 - row_shift)
        col_lane_ref[tap] = tap_weight(tap - 3 - col_shift)
    for group in range(GROUPS):
        shift = jnp.zeros((TILE, LANES), jnp.int32)
        for date in range(4):
            shift = jnp.where(subs % 4 == date, offsets_ref[0, 4 * group + date], shift)
        for tap in range(TAP_COUNT):
            row_sub_ref[tap, group * TILE : (group + 1) * TILE, :] = tap_weight(tap - 3 - shift)

    flat = [masks_ref[word] for word in range(words)]
    flat = flat + [jnp.zeros((TILE, LANES), jnp.int32)] * (LANES // TILE - words)
    words_ref[...] = jnp.transpose(jnp.concatenate(flat, axis=0))

    def one_block(block, carry):
        packed = words_ref[pl.ds(pl.multiple_of(block * TILE, TILE), TILE), :]
        for row_pair in range(TILE // 2):
            spread = [[], []]
            for row in (2 * row_pair, 2 * row_pair + 1):
                row_words = [
                    jnp.broadcast_to(
                        packed[:, word * TILE + row : word * TILE + row + 1], (TILE, LANES)
                    )
                    for word in range(words)
                ]
                for half in range(2):
                    near = 8 * half + lanes // 16 - row
                    across = lanes % 16 - subs
                    inside = (near >= 0) & (near <= 8) & (across >= 0) & (across <= 8)
                    amount = jnp.where(inside, (near & 1) * SLOT_COLS + across, 31)
                    first = max(0, 8 * half - row) // 2
                    last = min(8, 8 * half + 7 - row) // 2
                    chosen = row_words[first]
                    for word in range(first + 1, last + 1):
                        chosen = jnp.where(near >= 2 * word, row_words[word], chosen)
                    bits = lax.shift_right_logical(chosen, amount) & 1
                    spread[half].append(bits.astype(FLOAT))
            low_half, high_half = [jnp.concatenate(half, axis=0) for half in spread]
            rows = slice(16 * row_pair, 16 * row_pair + 16)
            picks_ref[block, rows, :LANES] = jnp.where(below, high_half, low_half).astype(HALF_FLOAT)
            picks_ref[block, rows, LANES:] = jnp.where(below, low_half, high_half).astype(HALF_FLOAT)
        return carry

    lax.fori_loop(0, BLOCKS, one_block, 0)


def split_halves(values):
    high = values.astype(HALF_FLOAT)
    low = values - high.astype(FLOAT)
    return high, low


def dot(a, b, contract):
    return lax.dot_general(
        a, b, (((contract[0],), (contract[1],)), ((), ())), preferred_element_type=FLOAT
    )


def near_is_below():
    return (lax.axis_index("row") + lax.axis_index("date")) % 2 == 0


def resample_half(
    own_ref,
    other_ref,
    below,
    row_sub_ref,
    row_lane_ref,
    col_lane_ref,
    z_ref,
    y_ref,
    mixed_ref,
    rims_ref,
    turned_ref,
):
    row_at, row_count = lax.axis_index("row"), lax.axis_size("row")
    col_at, col_count = lax.axis_index("date"), lax.axis_size("date")

    exists = (below & (row_at < row_count - 1)) | (jnp.logical_not(below) & (row_at > 0))

    def mix_group(group, carry):
        weights = [
            row_sub_ref[tap, pl.ds(pl.multiple_of(group * TILE, TILE), TILE), :]
            for tap in range(TAP_COUNT)
        ]
        own = [own_ref[group, row * TILE : (row + 1) * TILE, :] for row in range(TILE)]
        other = [
            jnp.where(exists, other_ref[group, row * TILE : (row + 1) * TILE, :], 0.0)
            for row in range(TILE)
        ]
        raw = [jnp.where(below, a, b) for a, b in zip(own, other)]
        raw = raw + [jnp.where(below, b, a) for a, b in zip(own, other)]
        for row in range(8):
            mixed = weights[0] * raw[row + 1]
            for tap in range(1, TAP_COUNT):
                mixed = mixed + weights[tap] * raw[row + 1 + tap]
            start = pl.multiple_of((row // 4) * 64 + group * TILE, TILE)
            mixed_ref[row % 4, pl.ds(start, TILE), :] = mixed
        return carry

    lax.fori_loop(0, GROUPS, mix_group, 0, unroll=2)

    lanes = lane_ids((1, LANES))
    lower = lanes < 64
    own, other = [
        source[:, 8 * TILE : 9 * TILE, :].reshape(64, LANES) for source in (own_ref, other_ref)
    ]
    other = jnp.where(exists, other, 0.0)
    first, second = jnp.where(below, own, other), jnp.where(below, other, own)
    far_first, far_second = pltpu.roll(first, 64, axis=1), pltpu.roll(second, 64, axis=1)
    rims_ref[0:LANES, :] = jnp.transpose(
        jnp.concatenate([first, jnp.where(lower, far_first, far_second)], axis=0)
    )
    rims_ref[LANES : 2 * LANES, :] = jnp.transpose(jnp.concatenate([second, far_second], axis=0))
    row_weights = [row_lane_ref[tap, 0:1, :] for tap in range(TAP_COUNT)]
    for row in range(4):
        turned_ref[row, 8 : 8 + LANES, :] = jnp.transpose(mixed_ref[row])
        rim = row_weights[0] * rims_ref[(row + 1) * 16 : (row + 2) * 16, :]
        for tap in range(1, TAP_COUNT):
            rim = rim + row_weights[tap] * rims_ref[(row + 1 + tap) * 16 : (row + 2 + tap) * 16, :]
        turned_ref[row, 0:8, :] = rim[0:8]
        turned_ref[row, 8 + LANES : 16 + LANES, :] = rim[8:16]

    places = sublane_ids((WINDOW_COLS, LANES))
    inside = ((places >= 4) | (col_at > 0)) & ((places < 132) | (col_at < col_count - 1))
    row_inside = (lower & (below | (row_at > 0))) | (
        (lanes >= 64) & (jnp.logical_not(below) | (row_at < row_count - 1))
    )
    inside = inside & row_inside
    term = lax.broadcasted_iota(jnp.int32, (2 * LANES, 2 * LANES), 0) % LANES
    gives = lax.broadcasted_iota(jnp.int32, (2 * LANES, 2 * LANES), 1)
    same_part = ((term % 8) < 4) == (gives < LANES)
    sums = jnp.where(((term < 64) == ((gives % LANES) < 64)) & same_part, 1.0, 0.0).astype(HALF_FLOAT)

    def store_windows(target, row, values):
        high, low = split_halves(values)
        high = high.astype(FLOAT)
        rows = (
            jnp.where(lower, high, pltpu.roll(low, 64, axis=1)),
            jnp.where(lower, pltpu.roll(high, 64, axis=1), low),
        )
        for part in range(2):
            start = (row + 4 * part) * 16
            for block in range(BLOCKS):
                target[block, start : start + 16, :] = rows[part][
                    block * 8 : block * 8 + 16
                ].astype(HALF_FLOAT)

    for row in range(4):
        mixed = col_lane_ref[0, 0:1, :] * turned_ref[row, 1 : 1 + WINDOW_COLS, :]
        for tap in range(1, TAP_COUNT):
            mixed = mixed + col_lane_ref[tap, 0:1, :] * turned_ref[
                row, 1 + tap : 1 + tap + WINDOW_COLS, :
            ]
        z = jnp.where(inside, mixed, 0.0)
        high, low = split_halves(z)
        total = dot(jnp.concatenate([high, low.astype(HALF_FLOAT)], axis=1), sums, (1, 0))
        y = z * total[:, :LANES] + swapped(z) * total[:, LANES:]
        store_windows(z_ref, row, z)
        store_windows(y_ref, row, y)


def swapped(values):
    real = (lane_ids((1, LANES)) % 8) < 4
    return jnp.where(real, pltpu.roll(values, LANES - 4, axis=1), -pltpu.roll(values, 4, axis=1))


def near_kernel(own_ref, near_ref, row_sub_ref, row_lane_ref, col_lane_ref, *rest):
    resample_half(
        own_ref, near_ref, near_is_below(), row_sub_ref, row_lane_ref, col_lane_ref, *rest
    )


def link_kernel(
    own_ref,
    far_ref,
    row_sub_ref,
    row_lane_ref,
    col_lane_ref,
    near_z_ref,
    near_y_ref,
    picks_ref,
    population_ref,
    linked_ref,
    eigen_ref,
    far_z_ref,
    far_y_ref,
    mixed_ref,
    rims_ref,
    turned_ref,
    result_ref,
    first_ref,
    vectors_ref,
    chosen_ref,
):
    resample_half(
        own_ref,
        far_ref,
        jnp.logical_not(near_is_below()),
        row_sub_ref,
        row_lane_ref,
        col_lane_ref,
        far_z_ref,
        far_y_ref,
        mixed_ref,
        rims_ref,
        turned_ref,
    )
    lower = lane_ids((1, LANES)) < 64

    for block in range(BLOCKS):
        y = jnp.concatenate([near_y_ref[block], far_y_ref[block]], axis=0)
        first = dot(picks_ref[block], y, (1, 0))
        first = first + pltpu.roll(first, 64, axis=1)
        high, low = split_halves(jnp.concatenate([first, swapped(first)], axis=0))
        first_ref[block] = first
        vectors_ref[block, :, :LANES] = high
        vectors_ref[block, :, LANES:] = low.astype(HALF_FLOAT)

    for block in range(BLOCKS):
        z = jnp.concatenate([near_z_ref[block], far_z_ref[block]], axis=0)
        inner = dot(vectors_ref[block], jnp.concatenate([z, z], axis=1), (1, 1))
        high, low = split_halves(inner)
        picks = picks_ref[block]
        picks = jnp.concatenate([picks, picks], axis=0)
        chosen_ref[block, :128, :] = high * picks
        chosen_ref[block, 128:, :] = low.astype(HALF_FLOAT) * picks

    for block in range(BLOCKS):
        z = jnp.concatenate([near_z_ref[block], far_z_ref[block]], axis=0)
        outer = dot(chosen_ref[block], z, (1, 0))
        outer = outer[:128] + outer[128:]
        outer = outer + pltpu.roll(outer, 64, axis=1)
        second = outer[:64] - swapped(outer[64:])
        both = jnp.where(lower, second, first_ref[block])
        for row in range(8):
            result_ref[row, block * 8 : block * 8 + 8, :] = both[row * 8 : row * 8 + 8]

    inverse = 1.0 / population_ref[...]
    for row in range(8):
        turned = jnp.transpose(result_ref[row])
        second, first = turned[:64], turned[64:]
        scale = inverse[row : row + 1]
        square = scale * scale
        norm_first = jnp.sqrt(jnp.sum(first * first, axis=0, keepdims=True) * square + EPSILON)
        norm_last = jnp.sqrt(
            jnp.sum(second * second, axis=0, keepdims=True) * (square * square) + EPSILON
        )
        eigen_ref[row : row + 1, :] = norm_last / norm_first
        linked = second * (square * (jnp.sqrt(jnp.float32(NDATE)) / norm_last))
        for group in range(GROUPS):
            for part in range(2):
                begin = ((part * NDATE + 4 * group) * 8) + row
                at = group * 8 + part * 4
                linked_ref[pl.ds(begin, 4, stride=8), :] = linked[at : at + 4]


def canonical(received, dates_dev):
    sources = received.shape[0]
    if dates_dev == 4:
        return received
    cells = received.reshape(sources, 9, 2, dates_dev, LANES)
    cells = jnp.transpose(cells, (1, 2, 0, 3, 4)).reshape(9, 2, GROUPS, 4, LANES)
    return jnp.transpose(cells, (2, 0, 1, 3, 4)).reshape(GROUPS, 9 * TILE, LANES)


def partner(date, row, turn, rows_count):
    other = row + 1 if (row + date + turn) % 2 == 0 else row - 1
    if 0 <= other < rows_count:
        return date * rows_count + other
    return (date ^ 2) * rows_count + row


def vmem(count):
    return [pl.BlockSpec(memory_space=pltpu.VMEM)] * count


def on_device(slc, offsets, masks):
    dates_dev = slc.shape[1]
    rows_dev = slc.shape[2]
    cols_all = slc.shape[3]
    rows_count = lax.axis_size("row")
    cols_count = lax.axis_size("date")
    planes_dev = 2 * dates_dev
    assert rows_dev == TILE and cols_all == cols_count * LANES

    small = pltpu.CompilerParams(vmem_limit_bytes=4 * 1024 * 1024)
    outgoing = pl.pallas_call(
        pack_kernel,
        out_shape=jax.ShapeDtypeStruct((cols_count, 9 * planes_dev, LANES), FLOAT),
        in_specs=vmem(1),
        out_specs=vmem(1)[0],
        compiler_params=small,
        cost_estimate=pl.CostEstimate(flops=0, bytes_accessed=600_000, transcendentals=0),
        name="pack",
    )(slc.reshape(planes_dev, rows_dev, cols_all))
    received = lax.all_to_all(outgoing, "date", split_axis=0, concat_axis=0, tiled=True)
    own = canonical(received, dates_dev)
    near, far = [
        lax.ppermute(
            own,
            ("date", "row"),
            [
                (date * rows_count + row, partner(date, row, turn, rows_count))
                for date in range(cols_count)
                for row in range(rows_count)
            ],
        )
        for turn in range(2)
    ]
    picks, population, row_sub, row_lane, col_lane = pl.pallas_call(
        prepare_kernel,
        out_shape=(
            jax.ShapeDtypeStruct((BLOCKS, 64, 256), HALF_FLOAT),
            jax.ShapeDtypeStruct((TILE, LANES), FLOAT),
            jax.ShapeDtypeStruct((TAP_COUNT, 64, LANES), FLOAT),
            jax.ShapeDtypeStruct((TAP_COUNT, TILE, LANES), FLOAT),
            jax.ShapeDtypeStruct((TAP_COUNT, TILE, LANES), FLOAT),
        ),
        in_specs=[pl.BlockSpec(memory_space=pltpu.SMEM)] + vmem(1),
        out_specs=tuple(vmem(5)),
        scratch_shapes=[pltpu.VMEM((LANES, LANES), jnp.int32)],
        compiler_params=small,
        cost_estimate=pl.CostEstimate(flops=4_000_000, bytes_accessed=1_000_000, transcendentals=0),
        name="prepare",
    )(offsets, masks)

    half_scratch = [
        pltpu.VMEM((4, LANES, LANES), FLOAT),
        pltpu.VMEM((2 * LANES, LANES), FLOAT),
        pltpu.VMEM((4, LANES + 16, LANES), FLOAT),
    ]
    windows = jax.ShapeDtypeStruct((BLOCKS, LANES, LANES), HALF_FLOAT)
    near_z, near_y = pl.pallas_call(
        near_kernel,
        out_shape=(windows, windows),
        in_specs=vmem(5),
        out_specs=tuple(vmem(2)),
        scratch_shapes=half_scratch,
        compiler_params=small,
        cost_estimate=pl.CostEstimate(
            flops=200_000_000, bytes_accessed=2_000_000, transcendentals=0
        ),
        name="near",
    )(own, near, row_sub, row_lane, col_lane)
    linked, eigen = pl.pallas_call(
        link_kernel,
        out_shape=(
            jax.ShapeDtypeStruct((2 * NDATE * TILE, LANES), FLOAT),
            jax.ShapeDtypeStruct((TILE, LANES), FLOAT),
        ),
        in_specs=vmem(9),
        out_specs=tuple(vmem(2)),
        scratch_shapes=[
            pltpu.VMEM((BLOCKS, LANES, LANES), HALF_FLOAT),
            pltpu.VMEM((BLOCKS, LANES, LANES), HALF_FLOAT),
        ]
        + half_scratch
        + [
            pltpu.VMEM((8, LANES, LANES), FLOAT),
            pltpu.VMEM((BLOCKS, 64, LANES), FLOAT),
            pltpu.VMEM((BLOCKS, 128, 256), HALF_FLOAT),
            pltpu.VMEM((BLOCKS, 256, 256), HALF_FLOAT),
        ],
        compiler_params=pltpu.CompilerParams(vmem_limit_bytes=16 * 1024 * 1024),
        cost_estimate=pl.CostEstimate(
            flops=1_000_000_000, bytes_accessed=2_000_000, transcendentals=0
        ),
        name="link",
    )(own, far, row_sub, row_lane, col_lane, near_z, near_y, picks, population)
    return linked.reshape(2, NDATE, TILE, LANES), eigen


def solution(mesh):
    in_specs = (P(None, "date", "row", None), P(), P(None, "row", "date"))
    out_specs = (P(None, None, "row", "date"), P("row", "date"))
    return jax.shard_map(
        on_device, mesh=mesh, in_specs=in_specs, out_specs=out_specs, check_vma=False
    )
```

```python
import functools

import jax
import jax.numpy as jnp
from jax import lax
from jax.experimental import pallas as pl
from jax.experimental.pallas import tpu as pltpu
from jax.sharding import PartitionSpec as P

NDATE = 32
SLOT_COLS = 9
EPSILON = 1e-06
LANES = 128
TILE = 8
GROUPS = 8
TAP_COUNT = 8
WINDOW_ROWS = 16
WINDOW_COLS = 136
BLOCKS = 16

FLOAT = jnp.float32
HALF_FLOAT = jnp.bfloat16


def lane_ids(shape):
    return lax.broadcasted_iota(jnp.int32, shape, len(shape) - 1)


def sublane_ids(shape):
    return lax.broadcasted_iota(jnp.int32, shape, len(shape) - 2)


def pack_blocks(slc_ref, send_ref):
    planes = slc_ref.shape[0]
    blocks = send_ref.shape[0]
    for block in range(blocks):
        for plane in range(planes):
            send_ref[block, pl.ds(plane, TILE, stride=planes), :] = slc_ref[
                plane, :, block * LANES : (block + 1) * LANES
            ]
    lanes = lane_ids((planes, LANES))
    rims = [jnp.zeros((planes, LANES), FLOAT) for _ in range(blocks)]
    for row in range(TILE):
        start = 16 * row
        turned = [
            pltpu.roll(
                send_ref[block, row * planes : (row + 1) * planes, :],
                (start + 8) % LANES,
                axis=1,
            )
            for block in range(blocks)
        ]
        left = (lanes >= start) & (lanes < start + 8)
        right = (lanes >= start + 8) & (lanes < start + 16)
        for block in range(blocks):
            if block > 0:
                rims[block] = jnp.where(left, turned[block - 1], rims[block])
            if block < blocks - 1:
                rims[block] = jnp.where(right, turned[block + 1], rims[block])
    for block in range(blocks):
        send_ref[block, TILE * planes : (TILE + 1) * planes, :] = rims[block]


def pack_pieces(slc_ref, *rest):
    pieces, blocks_ref = rest[:-1], rest[-1]
    pack_blocks(slc_ref, blocks_ref)
    here = lax.axis_index("date")
    for turn, piece_ref in enumerate(pieces):
        piece_ref[...] = blocks_ref[here ^ turn]


def join_kernel(first, *rest):
    here = lax.axis_index("date")
    for turn, piece_ref in enumerate(rest[:-1]):
        rest[-1][(here ^ (first + turn)) % 4] = piece_ref[...]


def tap_weight(distance):
    spread = jnp.abs(2 * distance - 1)
    return jnp.where(spread == 1, 0.5625, jnp.where(spread == 3, -0.0625, 0.0)).astype(FLOAT)


def prepare_kernel(
    offsets_ref, masks_ref, picks_ref, population_ref, row_sub_ref, row_lane_ref, col_lane_ref, words_ref
):
    words = masks_ref.shape[0]
    below = near_is_below()
    total = jnp.zeros((TILE, LANES), jnp.int32)
    for word in range(words):
        bits = masks_ref[word]
        bits = bits - (lax.shift_right_logical(bits, 1) & 0x55555555)
        bits = (bits & 0x33333333) + (lax.shift_right_logical(bits, 2) & 0x33333333)
        bits = (bits + lax.shift_right_logical(bits, 4)) & 0x0F0F0F0F
        bits = bits + lax.shift_right_logical(bits, 8)
        bits = bits + lax.shift_right_logical(bits, 16)
        total = total + (bits & 0xFF)
    population_ref[...] = total.astype(FLOAT)

    lanes = lane_ids((TILE, LANES))
    subs = sublane_ids((TILE, LANES))
    lane_dates = ((lanes % 64) // 8) * 4 + lanes % 4
    row_shift = jnp.zeros((TILE, LANES), jnp.int32)
    col_shift = jnp.zeros((TILE, LANES), jnp.int32)
    for date in range(NDATE):
        here = lane_dates == date
        row_shift = jnp.where(here, offsets_ref[0, date], row_shift)
        col_shift = jnp.where(here, offsets_ref[1, date], col_shift)
    for tap in range(TAP_COUNT):
        row_lane_ref[tap] = tap_weight(tap - 3 - row_shift)
        col_lane_ref[tap] = tap_weight(tap - 3 - col_shift)
    for group in range(GROUPS):
        shift = jnp.zeros((TILE, LANES), jnp.int32)
        for date in range(4):
            shift = jnp.where(subs % 4 == date, offsets_ref[0, 4 * group + date], shift)
        for tap in range(TAP_COUNT):
            row_sub_ref[tap, group * TILE : (group + 1) * TILE, :] = tap_weight(tap - 3 - shift)

    flat = [masks_ref[word] for word in range(words)]
    flat = flat + [jnp.zeros((TILE, LANES), jnp.int32)] * (LANES // TILE - words)
    words_ref[...] = jnp.transpose(jnp.concatenate(flat, axis=0))

    def one_block(block, carry):
        packed = words_ref[pl.ds(pl.multiple_of(block * TILE, TILE), TILE), :]
        for row_pair in range(TILE // 2):
            spread = [[], []]
            for row in (2 * row_pair, 2 * row_pair + 1):
                row_words = [
                    jnp.broadcast_to(
                        packed[:, word * TILE + row : word * TILE + row + 1], (TILE, LANES)
                    )
                    for word in range(words)
                ]
                for half in range(2):
                    near = 8 * half + lanes // 16 - row
                    across = lanes % 16 - subs
                    inside = (near >= 0) & (near <= 8) & (across >= 0) & (across <= 8)
                    amount = jnp.where(inside, (near & 1) * SLOT_COLS + across, 31)
                    first = max(0, 8 * half - row) // 2
                    last = min(8, 8 * half + 7 - row) // 2
                    chosen = row_words[first]
                    for word in range(first + 1, last + 1):
                        chosen = jnp.where(near >= 2 * word, row_words[word], chosen)
                    bits = lax.shift_right_logical(chosen, amount) & 1
                    spread[half].append(bits.astype(FLOAT))
            low_half, high_half = [jnp.concatenate(half, axis=0) for half in spread]
            rows = slice(16 * row_pair, 16 * row_pair + 16)
            picks_ref[block, rows, :LANES] = jnp.where(below, high_half, low_half).astype(HALF_FLOAT)
            picks_ref[block, rows, LANES:] = jnp.where(below, low_half, high_half).astype(HALF_FLOAT)
        return carry

    lax.fori_loop(0, BLOCKS, one_block, 0)


def split_halves(values):
    high = values.astype(HALF_FLOAT)
    low = values - high.astype(FLOAT)
    return high, low


def dot(a, b, contract):
    return lax.dot_general(
        a, b, (((contract[0],), (contract[1],)), ((), ())), preferred_element_type=FLOAT
    )


def packed_rims(base, refs):
    halves = [ref[:, 8 * TILE : 9 * TILE, :].reshape(32, LANES) for ref in refs]
    return jnp.where(
        base == 0, jnp.concatenate(halves, axis=0), jnp.concatenate(halves[::-1], axis=0)
    )


def first_group():
    return lax.axis_index("date") & 4 if lax.axis_size("date") == GROUPS else 0


def near_is_below():
    return (lax.axis_index("row") + lax.axis_index("date")) % 2 == 0


def resample_half(
    base,
    own_refs,
    other_refs,
    below,
    row_sub_ref,
    row_lane_ref,
    col_lane_ref,
    z_ref,
    y_ref,
    mixed_ref,
    rims_ref,
    turned_ref,
):
    row_at, row_count = lax.axis_index("row"), lax.axis_size("row")
    col_at, col_count = lax.axis_index("date"), lax.axis_size("date")

    exists = (below & (row_at < row_count - 1)) | (jnp.logical_not(below) & (row_at > 0))

    def mix_group(own_ref, other_ref, base, slot):
        group = base + slot
        weights = [
            row_sub_ref[tap, pl.ds(pl.multiple_of(group * TILE, TILE), TILE), :]
            for tap in range(TAP_COUNT)
        ]
        own = [own_ref[slot, row * TILE : (row + 1) * TILE, :] for row in range(TILE)]
        other = [
            jnp.where(exists, other_ref[slot, row * TILE : (row + 1) * TILE, :], 0.0)
            for row in range(TILE)
        ]
        raw = [jnp.where(below, a, b) for a, b in zip(own, other)]
        raw = raw + [jnp.where(below, b, a) for a, b in zip(own, other)]
        for row in range(8):
            mixed = weights[0] * raw[row + 1]
            for tap in range(1, TAP_COUNT):
                mixed = mixed + weights[tap] * raw[row + 1 + tap]
            start = pl.multiple_of((row // 4) * 64 + group * TILE, TILE)
            mixed_ref[row % 4, pl.ds(start, TILE), :] = mixed

    def mix_slot(slot, carry):
        mix_group(own_refs[0], other_refs[0], base, slot)
        mix_group(own_refs[1], other_refs[1], 4 - base, slot)
        return carry

    lax.fori_loop(0, GROUPS // 2, mix_slot, 0)

    lanes = lane_ids((1, LANES))
    lower = lanes < 64
    own, other = [packed_rims(base, refs) for refs in (own_refs, other_refs)]
    other = jnp.where(exists, other, 0.0)
    first, second = jnp.where(below, own, other), jnp.where(below, other, own)
    far_first, far_second = pltpu.roll(first, 64, axis=1), pltpu.roll(second, 64, axis=1)
    rims_ref[0:LANES, :] = jnp.transpose(
        jnp.concatenate([first, jnp.where(lower, far_first, far_second)], axis=0)
    )
    rims_ref[LANES : 2 * LANES, :] = jnp.transpose(jnp.concatenate([second, far_second], axis=0))
    row_weights = [row_lane_ref[tap, 0:1, :] for tap in range(TAP_COUNT)]
    for row in range(4):
        turned_ref[row, 8 : 8 + LANES, :] = jnp.transpose(mixed_ref[row])
        rim = row_weights[0] * rims_ref[(row + 1) * 16 : (row + 2) * 16, :]
        for tap in range(1, TAP_COUNT):
            rim = rim + row_weights[tap] * rims_ref[(row + 1 + tap) * 16 : (row + 2 + tap) * 16, :]
        turned_ref[row, 0:8, :] = rim[0:8]
        turned_ref[row, 8 + LANES : 16 + LANES, :] = rim[8:16]

    places = sublane_ids((WINDOW_COLS, LANES))
    inside = ((places >= 4) | (col_at > 0)) & ((places < 132) | (col_at < col_count - 1))
    row_inside = (lower & (below | (row_at > 0))) | (
        (lanes >= 64) & (jnp.logical_not(below) | (row_at < row_count - 1))
    )
    inside = inside & row_inside
    term = lax.broadcasted_iota(jnp.int32, (2 * LANES, 2 * LANES), 0) % LANES
    gives = lax.broadcasted_iota(jnp.int32, (2 * LANES, 2 * LANES), 1)
    same_part = ((term % 8) < 4) == (gives < LANES)
    sums = jnp.where(((term < 64) == ((gives % LANES) < 64)) & same_part, 1.0, 0.0).astype(HALF_FLOAT)

    def store_windows(target, row, values):
        high, low = split_halves(values)
        high = high.astype(FLOAT)
        rows = (
            jnp.where(lower, high, pltpu.roll(low, 64, axis=1)),
            jnp.where(lower, pltpu.roll(high, 64, axis=1), low),
        )
        for part in range(2):
            start = (row + 4 * part) * 16
            for block in range(BLOCKS):
                target[block, start : start + 16, :] = rows[part][
                    block * 8 : block * 8 + 16
                ].astype(HALF_FLOAT)

    for row in range(4):
        mixed = col_lane_ref[0, 0:1, :] * turned_ref[row, 1 : 1 + WINDOW_COLS, :]
        for tap in range(1, TAP_COUNT):
            mixed = mixed + col_lane_ref[tap, 0:1, :] * turned_ref[
                row, 1 + tap : 1 + tap + WINDOW_COLS, :
            ]
        z = jnp.where(inside, mixed, 0.0)
        high, low = split_halves(z)
        total = dot(jnp.concatenate([high, low.astype(HALF_FLOAT)], axis=1), sums, (1, 0))
        y = z * total[:, :LANES] + swapped(z) * total[:, LANES:]
        store_windows(z_ref, row, z)
        store_windows(y_ref, row, y)


def swapped(values):
    real = (lane_ids((1, LANES)) % 8) < 4
    return jnp.where(real, pltpu.roll(values, LANES - 4, axis=1), -pltpu.roll(values, 4, axis=1))


def near_kernel(own_b, own_a, near_b, near_a, *rest):
    resample_half(first_group(), (own_a, own_b), (near_a, near_b), near_is_below(), *rest)


def link_kernel(
    own_b,
    own_a,
    far_b,
    far_a,
    row_sub_ref,
    row_lane_ref,
    col_lane_ref,
    near_z_ref,
    near_y_ref,
    picks_ref,
    population_ref,
    linked_ref,
    eigen_ref,
    far_z_ref,
    far_y_ref,
    mixed_ref,
    rims_ref,
    turned_ref,
    result_ref,
    first_ref,
    vectors_ref,
    chosen_ref,
):
    resample_half(
        first_group(),
        (own_a, own_b),
        (far_a, far_b),
        jnp.logical_not(near_is_below()),
        row_sub_ref,
        row_lane_ref,
        col_lane_ref,
        far_z_ref,
        far_y_ref,
        mixed_ref,
        rims_ref,
        turned_ref,
    )
    lower = lane_ids((1, LANES)) < 64

    for block in range(BLOCKS):
        y = jnp.concatenate([near_y_ref[block], far_y_ref[block]], axis=0)
        first = dot(picks_ref[block], y, (1, 0))
        first = first + pltpu.roll(first, 64, axis=1)
        high, low = split_halves(jnp.concatenate([first, swapped(first)], axis=0))
        first_ref[block] = first
        vectors_ref[block, :, :LANES] = high
        vectors_ref[block, :, LANES:] = low.astype(HALF_FLOAT)

    for block in range(BLOCKS):
        z = jnp.concatenate([near_z_ref[block], far_z_ref[block]], axis=0)
        inner = dot(vectors_ref[block], jnp.concatenate([z, z], axis=1), (1, 1))
        high, low = split_halves(inner)
        picks = picks_ref[block]
        picks = jnp.concatenate([picks, picks], axis=0)
        chosen_ref[block, :128, :] = high * picks
        chosen_ref[block, 128:, :] = low.astype(HALF_FLOAT) * picks

    for block in range(BLOCKS):
        z = jnp.concatenate([near_z_ref[block], far_z_ref[block]], axis=0)
        outer = dot(chosen_ref[block], z, (1, 0))
        outer = outer[:128] + outer[128:]
        outer = outer + pltpu.roll(outer, 64, axis=1)
        second = outer[:64] - swapped(outer[64:])
        both = jnp.where(lower, second, first_ref[block])
        for row in range(8):
            result_ref[row, block * 8 : block * 8 + 8, :] = both[row * 8 : row * 8 + 8]

    inverse = 1.0 / population_ref[...]
    for row in range(8):
        turned = jnp.transpose(result_ref[row])
        second, first = turned[:64], turned[64:]
        scale = inverse[row : row + 1]
        square = scale * scale
        norm_first = jnp.sqrt(jnp.sum(first * first, axis=0, keepdims=True) * square + EPSILON)
        norm_last = jnp.sqrt(
            jnp.sum(second * second, axis=0, keepdims=True) * (square * square) + EPSILON
        )
        eigen_ref[row : row + 1, :] = norm_last / norm_first
        linked = second * (square * (jnp.sqrt(jnp.float32(NDATE)) / norm_last))
        for group in range(GROUPS):
            for part in range(2):
                begin = ((part * NDATE + 4 * group) * 8) + row
                at = group * 8 + part * 4
                linked_ref[pl.ds(begin, 4, stride=8), :] = linked[at : at + 4]


def canonical(received, dates_dev):
    sources = received.shape[0]
    if dates_dev == 4:
        return received
    cells = received.reshape(sources, 9, 2, dates_dev, LANES)
    cells = jnp.transpose(cells, (1, 2, 0, 3, 4)).reshape(9, 2, GROUPS, 4, LANES)
    return jnp.transpose(cells, (2, 0, 1, 3, 4)).reshape(GROUPS, 9 * TILE, LANES)


def partner(date, row, turn, rows_count):
    other = row + 1 if (row + date + turn) % 2 == 0 else row - 1
    if 0 <= other < rows_count:
        return date * rows_count + other
    return (date ^ 2) * rows_count + row


def vmem(count):
    return [pl.BlockSpec(memory_space=pltpu.VMEM)] * count


def on_device(slc, offsets, masks):
    dates_dev = slc.shape[1]
    rows_dev = slc.shape[2]
    cols_all = slc.shape[3]
    rows_count = lax.axis_size("row")
    cols_count = lax.axis_size("date")
    planes_dev = 2 * dates_dev
    assert rows_dev == TILE and cols_all == cols_count * LANES

    small = pltpu.CompilerParams(vmem_limit_bytes=4 * 1024 * 1024)
    images = slc.reshape(planes_dev, rows_dev, cols_all)
    moves = pl.CostEstimate(flops=0, bytes_accessed=600_000, transcendentals=0)
    half_shape = jax.ShapeDtypeStruct((GROUPS // 2, 9 * TILE, LANES), FLOAT)

    def swap_rows(cells, turn):
        return lax.ppermute(
            cells,
            ("date", "row"),
            [
                (date * rows_count + row, partner(date, row, turn, rows_count))
                for date in range(cols_count)
                for row in range(rows_count)
            ],
        )

    if cols_count == GROUPS:
        pieces = pl.pallas_call(
            pack_pieces,
            out_shape=[jax.ShapeDtypeStruct((9 * TILE, LANES), FLOAT)] * GROUPS,
            in_specs=vmem(1),
            out_specs=vmem(GROUPS),
            scratch_shapes=[pltpu.VMEM((GROUPS, 9 * TILE, LANES), FLOAT)],
            compiler_params=small,
            cost_estimate=moves,
            name="pack",
        )(images)
        pieces = list(pieces[:1]) + [
            lax.ppermute(pieces[turn], "date", [(i, i ^ turn) for i in range(GROUPS)])
            for turn in range(1, GROUPS)
        ]
        own = [
            pl.pallas_call(
                functools.partial(join_kernel, first),
                out_shape=half_shape,
                in_specs=vmem(4),
                out_specs=vmem(1)[0],
                compiler_params=small,
                cost_estimate=moves,
                name="join",
            )(*pieces[first : first + 4])
            for first in (0, 4)
        ]
    else:
        outgoing = pl.pallas_call(
            pack_blocks,
            out_shape=jax.ShapeDtypeStruct((cols_count, 9 * planes_dev, LANES), FLOAT),
            in_specs=vmem(1),
            out_specs=vmem(1)[0],
            compiler_params=small,
            cost_estimate=moves,
            name="pack",
        )(images)
        received = lax.all_to_all(outgoing, "date", split_axis=0, concat_axis=0, tiled=True)
        received = canonical(received, dates_dev)
        own = [received[: GROUPS // 2], received[GROUPS // 2 :]]
    near_a, far_a, near_b, far_b = [swap_rows(half, turn) for half in own for turn in range(2)]

    picks, population, row_sub, row_lane, col_lane = pl.pallas_call(
        prepare_kernel,
        out_shape=(
            jax.ShapeDtypeStruct((BLOCKS, 64, 256), HALF_FLOAT),
            jax.ShapeDtypeStruct((TILE, LANES), FLOAT),
            jax.ShapeDtypeStruct((TAP_COUNT, 64, LANES), FLOAT),
            jax.ShapeDtypeStruct((TAP_COUNT, TILE, LANES), FLOAT),
            jax.ShapeDtypeStruct((TAP_COUNT, TILE, LANES), FLOAT),
        ),
        in_specs=[pl.BlockSpec(memory_space=pltpu.SMEM)] + vmem(1),
        out_specs=tuple(vmem(5)),
        scratch_shapes=[pltpu.VMEM((LANES, LANES), jnp.int32)],
        compiler_params=small,
        cost_estimate=pl.CostEstimate(flops=4_000_000, bytes_accessed=1_000_000, transcendentals=0),
        name="prepare",
    )(offsets, masks)

    half_scratch = [
        pltpu.VMEM((4, LANES, LANES), FLOAT),
        pltpu.VMEM((2 * LANES, LANES), FLOAT),
        pltpu.VMEM((4, LANES + 16, LANES), FLOAT),
    ]
    windows = jax.ShapeDtypeStruct((BLOCKS, LANES, LANES), HALF_FLOAT)
    near_z, near_y = pl.pallas_call(
        near_kernel,
        out_shape=(windows, windows),
        in_specs=vmem(7),
        out_specs=tuple(vmem(2)),
        scratch_shapes=half_scratch,
        compiler_params=small,
        cost_estimate=pl.CostEstimate(
            flops=200_000_000, bytes_accessed=2_000_000, transcendentals=0
        ),
        name="near",
    )(*own[::-1], near_b, near_a, row_sub, row_lane, col_lane)
    linked, eigen = pl.pallas_call(
        link_kernel,
        out_shape=(
            jax.ShapeDtypeStruct((2 * NDATE * TILE, LANES), FLOAT),
            jax.ShapeDtypeStruct((TILE, LANES), FLOAT),
        ),
        in_specs=vmem(11),
        out_specs=tuple(vmem(2)),
        scratch_shapes=[
            pltpu.VMEM((BLOCKS, LANES, LANES), HALF_FLOAT),
            pltpu.VMEM((BLOCKS, LANES, LANES), HALF_FLOAT),
        ]
        + half_scratch
        + [
            pltpu.VMEM((8, LANES, LANES), FLOAT),
            pltpu.VMEM((BLOCKS, 64, LANES), FLOAT),
            pltpu.VMEM((BLOCKS, 128, 256), HALF_FLOAT),
            pltpu.VMEM((BLOCKS, 256, 256), HALF_FLOAT),
        ],
        compiler_params=pltpu.CompilerParams(vmem_limit_bytes=16 * 1024 * 1024),
        cost_estimate=pl.CostEstimate(
            flops=1_000_000_000, bytes_accessed=2_000_000, transcendentals=0
        ),
        name="link",
    )(*own[::-1], far_b, far_a, row_sub, row_lane, col_lane, near_z, near_y, picks, population)
    return linked.reshape(2, NDATE, TILE, LANES), eigen


def solution(mesh):
    in_specs = (P(None, "date", "row", None), P(), P(None, "row", "date"))
    out_specs = (P(None, None, "row", "date"), P("row", "date"))
    return jax.shard_map(
        on_device, mesh=mesh, in_specs=in_specs, out_specs=out_specs, check_vma=False
    )
```

```python
import functools

import jax
import jax.numpy as jnp
from jax import lax
from jax.experimental import pallas as pl
from jax.experimental.pallas import tpu as pltpu
from jax.sharding import PartitionSpec as P

NDATE = 32
SLOT_COLS = 9
EPSILON = 1e-06
LANES = 128
TILE = 8
GROUPS = 8
TAP_COUNT = 8
WINDOW_ROWS = 16
WINDOW_COLS = 136
BLOCKS = 16

FLOAT = jnp.float32
HALF_FLOAT = jnp.bfloat16


def lane_ids(shape):
    return lax.broadcasted_iota(jnp.int32, shape, len(shape) - 1)


def sublane_ids(shape):
    return lax.broadcasted_iota(jnp.int32, shape, len(shape) - 2)


def pack_blocks(slc_ref, send_ref):
    planes = slc_ref.shape[0]
    blocks = send_ref.shape[0]
    for block in range(blocks):
        for plane in range(planes):
            send_ref[block, pl.ds(plane, TILE, stride=planes), :] = slc_ref[
                plane, :, block * LANES : (block + 1) * LANES
            ]
    lanes = lane_ids((planes, LANES))
    rims = [jnp.zeros((planes, LANES), FLOAT) for _ in range(blocks)]
    for row in range(TILE):
        start = 16 * row
        turned = [
            pltpu.roll(
                send_ref[block, row * planes : (row + 1) * planes, :],
                (start + 8) % LANES,
                axis=1,
            )
            for block in range(blocks)
        ]
        left = (lanes >= start) & (lanes < start + 8)
        right = (lanes >= start + 8) & (lanes < start + 16)
        for block in range(blocks):
            if block > 0:
                rims[block] = jnp.where(left, turned[block - 1], rims[block])
            if block < blocks - 1:
                rims[block] = jnp.where(right, turned[block + 1], rims[block])
    for block in range(blocks):
        send_ref[block, TILE * planes : (TILE + 1) * planes, :] = rims[block]


def pack_pieces(slc_ref, *rest):
    pieces, blocks_ref = rest[:-1], rest[-1]
    pack_blocks(slc_ref, blocks_ref)
    here = lax.axis_index("date")
    for turn, piece_ref in enumerate(pieces):
        piece_ref[...] = blocks_ref[here ^ turn]


def join_kernel(first, *rest):
    here = lax.axis_index("date")
    for turn, piece_ref in enumerate(rest[:4]):
        rest[-1][(here ^ (first + turn)) % 4] = piece_ref[...]


def tap_weight(distance):
    spread = jnp.abs(2 * distance - 1)
    return jnp.where(spread == 1, 0.5625, jnp.where(spread == 3, -0.0625, 0.0)).astype(FLOAT)


def prepare_kernel(
    offsets_ref, masks_ref, _, picks_ref, population_ref, row_sub_ref, row_lane_ref, col_lane_ref, words_ref
):
    words = masks_ref.shape[0]
    below = near_is_below()
    total = jnp.zeros((TILE, LANES), jnp.int32)
    for word in range(words):
        bits = masks_ref[word]
        bits = bits - (lax.shift_right_logical(bits, 1) & 0x55555555)
        bits = (bits & 0x33333333) + (lax.shift_right_logical(bits, 2) & 0x33333333)
        bits = (bits + lax.shift_right_logical(bits, 4)) & 0x0F0F0F0F
        bits = bits + lax.shift_right_logical(bits, 8)
        bits = bits + lax.shift_right_logical(bits, 16)
        total = total + (bits & 0xFF)
    population_ref[...] = total.astype(FLOAT)

    lanes = lane_ids((TILE, LANES))
    subs = sublane_ids((TILE, LANES))
    lane_dates = ((lanes % 64) // 8) * 4 + lanes % 4
    row_shift = jnp.zeros((TILE, LANES), jnp.int32)
    col_shift = jnp.zeros((TILE, LANES), jnp.int32)
    for date in range(NDATE):
        here = lane_dates == date
        row_shift = jnp.where(here, offsets_ref[0, date], row_shift)
        col_shift = jnp.where(here, offsets_ref[1, date], col_shift)
    for tap in range(TAP_COUNT):
        row_lane_ref[tap] = tap_weight(tap - 3 - row_shift)
        col_lane_ref[tap] = tap_weight(tap - 3 - col_shift)
    for group in range(GROUPS):
        shift = jnp.zeros((TILE, LANES), jnp.int32)
        for date in range(4):
            shift = jnp.where(subs % 4 == date, offsets_ref[0, 4 * group + date], shift)
        for tap in range(TAP_COUNT):
            row_sub_ref[tap, group * TILE : (group + 1) * TILE, :] = tap_weight(tap - 3 - shift)

    flat = [masks_ref[word] for word in range(words)]
    flat = flat + [jnp.zeros((TILE, LANES), jnp.int32)] * (LANES // TILE - words)
    words_ref[...] = jnp.transpose(jnp.concatenate(flat, axis=0))

    def one_block(block, carry):
        packed = words_ref[pl.ds(pl.multiple_of(block * TILE, TILE), TILE), :]
        for row_pair in range(TILE // 2):
            spread = [[], []]
            for row in (2 * row_pair, 2 * row_pair + 1):
                row_words = [
                    jnp.broadcast_to(
                        packed[:, word * TILE + row : word * TILE + row + 1], (TILE, LANES)
                    )
                    for word in range(words)
                ]
                for half in range(2):
                    near = 8 * half + lanes // 16 - row
                    across = lanes % 16 - subs
                    inside = (near >= 0) & (near <= 8) & (across >= 0) & (across <= 8)
                    amount = jnp.where(inside, (near & 1) * SLOT_COLS + across, 31)
                    first = max(0, 8 * half - row) // 2
                    last = min(8, 8 * half + 7 - row) // 2
                    chosen = row_words[first]
                    for word in range(first + 1, last + 1):
                        chosen = jnp.where(near >= 2 * word, row_words[word], chosen)
                    bits = lax.shift_right_logical(chosen, amount) & 1
                    spread[half].append(bits.astype(FLOAT))
            low_half, high_half = [jnp.concatenate(half, axis=0) for half in spread]
            rows = slice(16 * row_pair, 16 * row_pair + 16)
            picks_ref[block, rows, :LANES] = jnp.where(below, high_half, low_half).astype(HALF_FLOAT)
            picks_ref[block, rows, LANES:] = jnp.where(below, low_half, high_half).astype(HALF_FLOAT)
        return carry

    lax.fori_loop(0, BLOCKS, one_block, 0)


def split_halves(values):
    high = values.astype(HALF_FLOAT)
    low = values - high.astype(FLOAT)
    return high, low


def dot(a, b, contract):
    return lax.dot_general(
        a, b, (((contract[0],), (contract[1],)), ((), ())), preferred_element_type=FLOAT
    )


def packed_rims(base, refs):
    halves = [ref[:, 8 * TILE : 9 * TILE, :].reshape(32, LANES) for ref in refs]
    return jnp.where(
        base == 0, jnp.concatenate(halves, axis=0), jnp.concatenate(halves[::-1], axis=0)
    )


def first_group():
    return lax.axis_index("date") & 4 if lax.axis_size("date") == GROUPS else 0


def near_is_below():
    return (lax.axis_index("row") + lax.axis_index("date")) % 2 == 0


def resample_half(
    base,
    own_refs,
    other_refs,
    below,
    row_sub_ref,
    row_lane_ref,
    col_lane_ref,
    z_ref,
    y_ref,
    mixed_ref,
    rims_ref,
    turned_ref,
):
    row_at, row_count = lax.axis_index("row"), lax.axis_size("row")
    col_at, col_count = lax.axis_index("date"), lax.axis_size("date")

    exists = exists_at(below)

    def mix_group(own_ref, other_ref, base, slot):
        group = base + slot
        weights = [
            row_sub_ref[tap, pl.ds(pl.multiple_of(group * TILE, TILE), TILE), :]
            for tap in range(TAP_COUNT)
        ]
        own = [own_ref[slot, row * TILE : (row + 1) * TILE, :] for row in range(TILE)]
        other = [
            jnp.where(exists, other_ref[slot, row * TILE : (row + 1) * TILE, :], 0.0)
            for row in range(TILE)
        ]
        raw = [jnp.where(below, a, b) for a, b in zip(own, other)]
        raw = raw + [jnp.where(below, b, a) for a, b in zip(own, other)]
        for row in range(8):
            mixed = weights[0] * raw[row + 1]
            for tap in range(1, TAP_COUNT):
                mixed = mixed + weights[tap] * raw[row + 1 + tap]
            start = pl.multiple_of((row // 4) * 64 + group * TILE, TILE)
            mixed_ref[row % 4, pl.ds(start, TILE), :] = mixed

    def mix_slot(slot, carry):
        mix_group(own_refs[0], other_refs[0], base, slot)
        mix_group(own_refs[1], other_refs[1], 4 - base, slot)
        return carry

    lax.fori_loop(0, GROUPS // 2, mix_slot, 0)

    lanes = lane_ids((1, LANES))
    lower = lanes < 64
    own, other = [packed_rims(base, refs) for refs in (own_refs, other_refs)]
    other = jnp.where(exists, other, 0.0)
    first, second = jnp.where(below, own, other), jnp.where(below, other, own)
    far_first, far_second = pltpu.roll(first, 64, axis=1), pltpu.roll(second, 64, axis=1)
    rims_ref[0:LANES, :] = jnp.transpose(
        jnp.concatenate([first, jnp.where(lower, far_first, far_second)], axis=0)
    )
    rims_ref[LANES : 2 * LANES, :] = jnp.transpose(jnp.concatenate([second, far_second], axis=0))
    row_weights = [row_lane_ref[tap, 0:1, :] for tap in range(TAP_COUNT)]
    for row in range(4):
        turned_ref[row, 8 : 8 + LANES, :] = jnp.transpose(mixed_ref[row])
        rim = row_weights[0] * rims_ref[(row + 1) * 16 : (row + 2) * 16, :]
        for tap in range(1, TAP_COUNT):
            rim = rim + row_weights[tap] * rims_ref[(row + 1 + tap) * 16 : (row + 2 + tap) * 16, :]
        turned_ref[row, 0:8, :] = rim[0:8]
        turned_ref[row, 8 + LANES : 16 + LANES, :] = rim[8:16]

    places = sublane_ids((WINDOW_COLS, LANES))
    inside = ((places >= 4) | (col_at > 0)) & ((places < 132) | (col_at < col_count - 1))
    row_inside = (lower & (below | (row_at > 0))) | (
        (lanes >= 64) & (jnp.logical_not(below) | (row_at < row_count - 1))
    )
    inside = inside & row_inside
    term = lax.broadcasted_iota(jnp.int32, (2 * LANES, 2 * LANES), 0) % LANES
    gives = lax.broadcasted_iota(jnp.int32, (2 * LANES, 2 * LANES), 1)
    same_part = ((term % 8) < 4) == (gives < LANES)
    sums = jnp.where(((term < 64) == ((gives % LANES) < 64)) & same_part, 1.0, 0.0).astype(HALF_FLOAT)

    def store_windows(target, row, values):
        high, low = split_halves(values)
        high = high.astype(FLOAT)
        rows = (
            jnp.where(lower, high, pltpu.roll(low, 64, axis=1)),
            jnp.where(lower, pltpu.roll(high, 64, axis=1), low),
        )
        for part in range(2):
            start = (row + 4 * part) * 16
            for block in range(BLOCKS):
                target[block, start : start + 16, :] = rows[part][
                    block * 8 : block * 8 + 16
                ].astype(HALF_FLOAT)

    for row in range(4):
        mixed = col_lane_ref[0, 0:1, :] * turned_ref[row, 1 : 1 + WINDOW_COLS, :]
        for tap in range(1, TAP_COUNT):
            mixed = mixed + col_lane_ref[tap, 0:1, :] * turned_ref[
                row, 1 + tap : 1 + tap + WINDOW_COLS, :
            ]
        z = jnp.where(inside, mixed, 0.0)
        high, low = split_halves(z)
        total = dot(jnp.concatenate([high, low.astype(HALF_FLOAT)], axis=1), sums, (1, 0))
        y = z * total[:, :LANES] + swapped(z) * total[:, LANES:]
        store_windows(z_ref, row, z)
        store_windows(y_ref, row, y)


def swapped(values):
    real = (lane_ids((1, LANES)) % 8) < 4
    return jnp.where(real, pltpu.roll(values, LANES - 4, axis=1), -pltpu.roll(values, 4, axis=1))


def exists_at(below):
    row_at, row_count = lax.axis_index("row"), lax.axis_size("row")
    return (below & (row_at < row_count - 1)) | (jnp.logical_not(below) & (row_at > 0))


def screen_kernel(near_ref, far_ref, near_out_ref, far_out_ref):
    below = near_is_below()
    near_out_ref[...] = jnp.where(exists_at(below), near_ref[...], 0.0)
    far_out_ref[...] = jnp.where(exists_at(jnp.logical_not(below)), far_ref[...], 0.0)


def near_kernel(own_b, own_a, near_b, near_a, *rest):
    resample_half(first_group(), (own_a, own_b), (near_a, near_b), near_is_below(), *rest)


def link_kernel(
    own_b,
    own_a,
    far_b,
    far_a,
    row_sub_ref,
    row_lane_ref,
    col_lane_ref,
    near_z_ref,
    near_y_ref,
    picks_ref,
    population_ref,
    linked_ref,
    eigen_ref,
    far_z_ref,
    far_y_ref,
    mixed_ref,
    rims_ref,
    turned_ref,
    result_ref,
    first_ref,
    vectors_ref,
    chosen_ref,
):
    resample_half(
        first_group(),
        (own_a, own_b),
        (far_a, far_b),
        jnp.logical_not(near_is_below()),
        row_sub_ref,
        row_lane_ref,
        col_lane_ref,
        far_z_ref,
        far_y_ref,
        mixed_ref,
        rims_ref,
        turned_ref,
    )
    lower = lane_ids((1, LANES)) < 64

    for block in range(BLOCKS):
        y = jnp.concatenate([near_y_ref[block], far_y_ref[block]], axis=0)
        first = dot(picks_ref[block], y, (1, 0))
        first = first + pltpu.roll(first, 64, axis=1)
        high, low = split_halves(jnp.concatenate([first, swapped(first)], axis=0))
        first_ref[block] = first
        vectors_ref[block, :, :LANES] = high
        vectors_ref[block, :, LANES:] = low.astype(HALF_FLOAT)

    for block in range(BLOCKS):
        z = jnp.concatenate([near_z_ref[block], far_z_ref[block]], axis=0)
        inner = dot(vectors_ref[block], jnp.concatenate([z, z], axis=1), (1, 1))
        high, low = split_halves(inner)
        picks = picks_ref[block]
        picks = jnp.concatenate([picks, picks], axis=0)
        chosen_ref[block, :128, :] = high * picks
        chosen_ref[block, 128:, :] = low.astype(HALF_FLOAT) * picks

    for block in range(BLOCKS):
        z = jnp.concatenate([near_z_ref[block], far_z_ref[block]], axis=0)
        outer = dot(chosen_ref[block], z, (1, 0))
        outer = outer[:128] + outer[128:]
        outer = outer + pltpu.roll(outer, 64, axis=1)
        second = outer[:64] - swapped(outer[64:])
        both = jnp.where(lower, second, first_ref[block])
        for row in range(8):
            result_ref[row, block * 8 : block * 8 + 8, :] = both[row * 8 : row * 8 + 8]

    inverse = 1.0 / population_ref[...]
    for row in range(8):
        turned = jnp.transpose(result_ref[row])
        second, first = turned[:64], turned[64:]
        scale = inverse[row : row + 1]
        square = scale * scale
        norm_first = jnp.sqrt(jnp.sum(first * first, axis=0, keepdims=True) * square + EPSILON)
        norm_last = jnp.sqrt(
            jnp.sum(second * second, axis=0, keepdims=True) * (square * square) + EPSILON
        )
        eigen_ref[row : row + 1, :] = norm_last / norm_first
        linked = second * (square * (jnp.sqrt(jnp.float32(NDATE)) / norm_last))
        for group in range(GROUPS):
            for part in range(2):
                begin = ((part * NDATE + 4 * group) * 8) + row
                at = group * 8 + part * 4
                linked_ref[pl.ds(begin, 4, stride=8), :] = linked[at : at + 4]


def canonical(received, dates_dev):
    sources = received.shape[0]
    if dates_dev == 4:
        return received
    cells = received.reshape(sources, 9, 2, dates_dev, LANES)
    cells = jnp.transpose(cells, (1, 2, 0, 3, 4)).reshape(9, 2, GROUPS, 4, LANES)
    return jnp.transpose(cells, (2, 0, 1, 3, 4)).reshape(GROUPS, 9 * TILE, LANES)


def partner(date, row, turn, rows_count):
    other = row + 1 if (row + date + turn) % 2 == 0 else row - 1
    if 0 <= other < rows_count:
        return date * rows_count + other
    return (date ^ 2) * rows_count + row


def vmem(count):
    return [pl.BlockSpec(memory_space=pltpu.VMEM)] * count


def on_device(slc, offsets, masks):
    dates_dev = slc.shape[1]
    rows_dev = slc.shape[2]
    cols_all = slc.shape[3]
    rows_count = lax.axis_size("row")
    cols_count = lax.axis_size("date")
    planes_dev = 2 * dates_dev
    assert rows_dev == TILE and cols_all == cols_count * LANES

    small = pltpu.CompilerParams(vmem_limit_bytes=4 * 1024 * 1024)
    images = slc.reshape(planes_dev, rows_dev, cols_all)
    moves = pl.CostEstimate(flops=0, bytes_accessed=600_000, transcendentals=0)
    half_shape = jax.ShapeDtypeStruct((GROUPS // 2, 9 * TILE, LANES), FLOAT)

    def swap_rows(cells, turn):
        return lax.ppermute(
            cells,
            ("date", "row"),
            [
                (date * rows_count + row, partner(date, row, turn, rows_count))
                for date in range(cols_count)
                for row in range(rows_count)
            ],
        )

    prepare = pl.pallas_call(
        prepare_kernel,
        out_shape=(
            jax.ShapeDtypeStruct((BLOCKS, 64, 256), HALF_FLOAT),
            jax.ShapeDtypeStruct((TILE, LANES), FLOAT),
            jax.ShapeDtypeStruct((TAP_COUNT, 64, LANES), FLOAT),
            jax.ShapeDtypeStruct((TAP_COUNT, TILE, LANES), FLOAT),
            jax.ShapeDtypeStruct((TAP_COUNT, TILE, LANES), FLOAT),
        ),
        in_specs=[pl.BlockSpec(memory_space=pltpu.SMEM)] + vmem(2),
        out_specs=tuple(vmem(5)),
        scratch_shapes=[pltpu.VMEM((LANES, LANES), jnp.int32)],
        compiler_params=small,
        cost_estimate=pl.CostEstimate(flops=4_000_000, bytes_accessed=1_000_000, transcendentals=0),
        name="prepare",
    )

    if cols_count == GROUPS:
        pieces = pl.pallas_call(
            pack_pieces,
            out_shape=[jax.ShapeDtypeStruct((9 * TILE, LANES), FLOAT)] * GROUPS,
            in_specs=vmem(1),
            out_specs=vmem(GROUPS),
            scratch_shapes=[pltpu.VMEM((GROUPS, 9 * TILE, LANES), FLOAT)],
            compiler_params=small,
            cost_estimate=moves,
            name="pack",
        )(images)
        pieces = list(pieces[:1]) + [
            lax.ppermute(pieces[turn], "date", [(i, i ^ turn) for i in range(GROUPS)])
            for turn in range(1, GROUPS)
        ]

        def join(first, *after):
            return pl.pallas_call(
                functools.partial(join_kernel, first),
                out_shape=half_shape,
                in_specs=vmem(4 + len(after)),
                out_specs=vmem(1)[0],
                compiler_params=small,
                cost_estimate=moves,
                name="join",
            )(*pieces[first : first + 4], *after)

        own = [join(0)]
        near_a, far_a = swap_rows(own[0], 0), swap_rows(own[0], 1)
        prepared = prepare(offsets, masks, own[0])
        own.append(join(4, prepared[1]))
    else:
        outgoing = pl.pallas_call(
            pack_blocks,
            out_shape=jax.ShapeDtypeStruct((cols_count, 9 * planes_dev, LANES), FLOAT),
            in_specs=vmem(1),
            out_specs=vmem(1)[0],
            compiler_params=small,
            cost_estimate=moves,
            name="pack",
        )(images)
        received = lax.all_to_all(outgoing, "date", split_axis=0, concat_axis=0, tiled=True)
        received = canonical(received, dates_dev)
        own = [received[: GROUPS // 2], received[GROUPS // 2 :]]
        near_a, far_a = swap_rows(own[0], 0), swap_rows(own[0], 1)
        prepared = prepare(offsets, masks, own[0])
    picks, population, row_sub, row_lane, col_lane = prepared
    near_b, far_b = swap_rows(own[1], 0), swap_rows(own[1], 1)

    near_a, far_a = pl.pallas_call(
        screen_kernel,
        out_shape=(half_shape, half_shape),
        in_specs=vmem(2),
        out_specs=tuple(vmem(2)),
        compiler_params=small,
        cost_estimate=pl.CostEstimate(flops=0, bytes_accessed=600_000, transcendentals=0),
        name="screen",
    )(near_a, far_a)

    half_scratch = [
        pltpu.VMEM((4, LANES, LANES), FLOAT),
        pltpu.VMEM((2 * LANES, LANES), FLOAT),
        pltpu.VMEM((4, LANES + 16, LANES), FLOAT),
    ]
    windows = jax.ShapeDtypeStruct((BLOCKS, LANES, LANES), HALF_FLOAT)
    near_z, near_y = pl.pallas_call(
        near_kernel,
        out_shape=(windows, windows),
        in_specs=vmem(7),
        out_specs=tuple(vmem(2)),
        scratch_shapes=half_scratch,
        compiler_params=small,
        cost_estimate=pl.CostEstimate(
            flops=200_000_000, bytes_accessed=2_000_000, transcendentals=0
        ),
        name="near",
    )(*own[::-1], near_b, near_a, row_sub, row_lane, col_lane)
    linked, eigen = pl.pallas_call(
        link_kernel,
        out_shape=(
            jax.ShapeDtypeStruct((2 * NDATE * TILE, LANES), FLOAT),
            jax.ShapeDtypeStruct((TILE, LANES), FLOAT),
        ),
        in_specs=vmem(11),
        out_specs=tuple(vmem(2)),
        scratch_shapes=[
            pltpu.VMEM((BLOCKS, LANES, LANES), HALF_FLOAT),
            pltpu.VMEM((BLOCKS, LANES, LANES), HALF_FLOAT),
        ]
        + half_scratch
        + [
            pltpu.VMEM((8, LANES, LANES), FLOAT),
            pltpu.VMEM((BLOCKS, 64, LANES), FLOAT),
            pltpu.VMEM((BLOCKS, 128, 256), HALF_FLOAT),
            pltpu.VMEM((BLOCKS, 256, 256), HALF_FLOAT),
        ],
        compiler_params=pltpu.CompilerParams(vmem_limit_bytes=16 * 1024 * 1024),
        cost_estimate=pl.CostEstimate(
            flops=1_000_000_000, bytes_accessed=2_000_000, transcendentals=0
        ),
        name="link",
    )(*own[::-1], far_b, far_a, row_sub, row_lane, col_lane, near_z, near_y, picks, population)
    return linked.reshape(2, NDATE, TILE, LANES), eigen


def solution(mesh):
    in_specs = (P(None, "date", "row", None), P(), P(None, "row", "date"))
    out_specs = (P(None, None, "row", "date"), P("row", "date"))
    return jax.shard_map(
        on_device, mesh=mesh, in_specs=in_specs, out_specs=out_specs, check_vma=False
    )
```

```python
import functools

import jax
import jax.numpy as jnp
from jax import lax
from jax.experimental import pallas as pl
from jax.experimental.pallas import tpu as pltpu
from jax.sharding import PartitionSpec as P

NDATE = 32
SLOT_COLS = 9
EPSILON = 1e-06
LANES = 128
TILE = 8
GROUPS = 8
TAP_COUNT = 8
WINDOW_ROWS = 16
WINDOW_COLS = 136
BLOCKS = 16

FLOAT = jnp.float32
HALF_FLOAT = jnp.bfloat16


def lane_ids(shape):
    return lax.broadcasted_iota(jnp.int32, shape, len(shape) - 1)


def sublane_ids(shape):
    return lax.broadcasted_iota(jnp.int32, shape, len(shape) - 2)


def pack_blocks(slc_ref, send_ref):
    planes = slc_ref.shape[0]
    blocks = send_ref.shape[0]
    for block in range(blocks):
        for plane in range(planes):
            send_ref[block, pl.ds(plane, TILE, stride=planes), :] = slc_ref[
                plane, :, block * LANES : (block + 1) * LANES
            ]
    lanes = lane_ids((planes, LANES))
    rims = [jnp.zeros((planes, LANES), FLOAT) for _ in range(blocks)]
    for row in range(TILE):
        start = 16 * row
        turned = [
            pltpu.roll(
                send_ref[block, row * planes : (row + 1) * planes, :],
                (start + 8) % LANES,
                axis=1,
            )
            for block in range(blocks)
        ]
        left = (lanes >= start) & (lanes < start + 8)
        right = (lanes >= start + 8) & (lanes < start + 16)
        for block in range(blocks):
            if block > 0:
                rims[block] = jnp.where(left, turned[block - 1], rims[block])
            if block < blocks - 1:
                rims[block] = jnp.where(right, turned[block + 1], rims[block])
    for block in range(blocks):
        send_ref[block, TILE * planes : (TILE + 1) * planes, :] = rims[block]


def pack_pieces(slc_ref, *rest):
    pieces, blocks_ref = rest[:-1], rest[-1]
    pack_blocks(slc_ref, blocks_ref)
    here = lax.axis_index("date")
    for turn, piece_ref in enumerate(pieces):
        piece_ref[...] = blocks_ref[here ^ turn]


def join_kernel(turns, *rest):
    here = lax.axis_index("date")
    for turn, piece_ref in zip(turns, rest[:-1]):
        rest[-1][(here ^ turn) % 4] = piece_ref[...]


def tap_weight(distance):
    spread = jnp.abs(2 * distance - 1)
    return jnp.where(spread == 1, 0.5625, jnp.where(spread == 3, -0.0625, 0.0)).astype(FLOAT)


def prepare_kernel(
    offsets_ref, masks_ref, picks_ref, population_ref, row_sub_ref, row_lane_ref, col_lane_ref, words_ref
):
    words = masks_ref.shape[0]
    below = near_is_below()
    total = jnp.zeros((TILE, LANES), jnp.int32)
    for word in range(words):
        bits = masks_ref[word]
        bits = bits - (lax.shift_right_logical(bits, 1) & 0x55555555)
        bits = (bits & 0x33333333) + (lax.shift_right_logical(bits, 2) & 0x33333333)
        bits = (bits + lax.shift_right_logical(bits, 4)) & 0x0F0F0F0F
        bits = bits + lax.shift_right_logical(bits, 8)
        bits = bits + lax.shift_right_logical(bits, 16)
        total = total + (bits & 0xFF)
    population_ref[...] = total.astype(FLOAT)

    lanes = lane_ids((TILE, LANES))
    subs = sublane_ids((TILE, LANES))
    lane_dates = ((lanes % 64) // 8) * 4 + lanes % 4
    row_shift = jnp.zeros((TILE, LANES), jnp.int32)
    col_shift = jnp.zeros((TILE, LANES), jnp.int32)
    for date in range(NDATE):
        here = lane_dates == date
        row_shift = jnp.where(here, offsets_ref[0, date], row_shift)
        col_shift = jnp.where(here, offsets_ref[1, date], col_shift)
    for tap in range(TAP_COUNT):
        row_lane_ref[tap] = tap_weight(tap - 3 - row_shift)
        col_lane_ref[tap] = tap_weight(tap - 3 - col_shift)
    for group in range(GROUPS):
        shift = jnp.zeros((TILE, LANES), jnp.int32)
        for date in range(4):
            shift = jnp.where(subs % 4 == date, offsets_ref[0, 4 * group + date], shift)
        for tap in range(TAP_COUNT):
            row_sub_ref[tap, group * TILE : (group + 1) * TILE, :] = tap_weight(tap - 3 - shift)

    flat = [masks_ref[word] for word in range(words)]
    flat = flat + [jnp.zeros((TILE, LANES), jnp.int32)] * (LANES // TILE - words)
    words_ref[...] = jnp.transpose(jnp.concatenate(flat, axis=0))

    def one_block(block, carry):
        packed = words_ref[pl.ds(pl.multiple_of(block * TILE, TILE), TILE), :]
        for row_pair in range(TILE // 2):
            spread = [[], []]
            for row in (2 * row_pair, 2 * row_pair + 1):
                row_words = [
                    jnp.broadcast_to(
                        packed[:, word * TILE + row : word * TILE + row + 1], (TILE, LANES)
                    )
                    for word in range(words)
                ]
                for half in range(2):
                    near = 8 * half + lanes // 16 - row
                    across = lanes % 16 - subs
                    inside = (near >= 0) & (near <= 8) & (across >= 0) & (across <= 8)
                    amount = jnp.where(inside, (near & 1) * SLOT_COLS + across, 31)
                    first = max(0, 8 * half - row) // 2
                    last = min(8, 8 * half + 7 - row) // 2
                    chosen = row_words[first]
                    for word in range(first + 1, last + 1):
                        chosen = jnp.where(near >= 2 * word, row_words[word], chosen)
                    bits = lax.shift_right_logical(chosen, amount) & 1
                    spread[half].append(bits.astype(FLOAT))
            low_half, high_half = [jnp.concatenate(half, axis=0) for half in spread]
            rows = slice(16 * row_pair, 16 * row_pair + 16)
            picks_ref[block, rows, :LANES] = jnp.where(below, high_half, low_half).astype(HALF_FLOAT)
            picks_ref[block, rows, LANES:] = jnp.where(below, low_half, high_half).astype(HALF_FLOAT)
        return carry

    lax.fori_loop(0, BLOCKS, one_block, 0)


def split_halves(values):
    high = values.astype(HALF_FLOAT)
    low = values - high.astype(FLOAT)
    return high, low


def dot(a, b, contract):
    return lax.dot_general(
        a, b, (((contract[0],), (contract[1],)), ((), ())), preferred_element_type=FLOAT
    )


def packed_rims(base, refs):
    halves = [ref[:, 8 * TILE : 9 * TILE, :].reshape(32, LANES) for ref in refs]
    return jnp.where(
        base == 0, jnp.concatenate(halves, axis=0), jnp.concatenate(halves[::-1], axis=0)
    )


def first_group():
    return (lax.axis_index("date") ^ 4) & 4 if lax.axis_size("date") == GROUPS else 0


def near_is_below():
    return (lax.axis_index("row") + lax.axis_index("date")) % 2 == 0


def resample_half(
    base,
    own_refs,
    other_refs,
    below,
    row_sub_ref,
    row_lane_ref,
    col_lane_ref,
    z_ref,
    y_ref,
    mixed_ref,
    rims_ref,
    turned_ref,
):
    row_at, row_count = lax.axis_index("row"), lax.axis_size("row")
    col_at, col_count = lax.axis_index("date"), lax.axis_size("date")

    exists = (below & (row_at < row_count - 1)) | (jnp.logical_not(below) & (row_at > 0))

    def mix_group(own_ref, other_ref, base, slot):
        group = base + slot
        weights = [
            row_sub_ref[tap, pl.ds(pl.multiple_of(group * TILE, TILE), TILE), :]
            for tap in range(TAP_COUNT)
        ]
        own = [own_ref[slot, row * TILE : (row + 1) * TILE, :] for row in range(TILE)]
        other = [
            jnp.where(exists, other_ref[slot, row * TILE : (row + 1) * TILE, :], 0.0)
            for row in range(TILE)
        ]
        raw = [jnp.where(below, a, b) for a, b in zip(own, other)]
        raw = raw + [jnp.where(below, b, a) for a, b in zip(own, other)]
        for row in range(8):
            mixed = weights[0] * raw[row + 1]
            for tap in range(1, TAP_COUNT):
                mixed = mixed + weights[tap] * raw[row + 1 + tap]
            start = pl.multiple_of((row // 4) * 64 + group * TILE, TILE)
            mixed_ref[row % 4, pl.ds(start, TILE), :] = mixed

    def mix_slot(slot, carry):
        mix_group(own_refs[0], other_refs[0], base, slot)
        mix_group(own_refs[1], other_refs[1], 4 - base, slot)
        return carry

    lax.fori_loop(0, GROUPS // 2, mix_slot, 0)

    lanes = lane_ids((1, LANES))
    lower = lanes < 64
    own, other = [packed_rims(base, refs) for refs in (own_refs, other_refs)]
    other = jnp.where(exists, other, 0.0)
    first, second = jnp.where(below, own, other), jnp.where(below, other, own)
    far_first, far_second = pltpu.roll(first, 64, axis=1), pltpu.roll(second, 64, axis=1)
    rims_ref[0:LANES, :] = jnp.transpose(
        jnp.concatenate([first, jnp.where(lower, far_first, far_second)], axis=0)
    )
    rims_ref[LANES : 2 * LANES, :] = jnp.transpose(jnp.concatenate([second, far_second], axis=0))
    row_weights = [row_lane_ref[tap, 0:1, :] for tap in range(TAP_COUNT)]
    for row in range(4):
        turned_ref[row, 8 : 8 + LANES, :] = jnp.transpose(mixed_ref[row])
        rim = row_weights[0] * rims_ref[(row + 1) * 16 : (row + 2) * 16, :]
        for tap in range(1, TAP_COUNT):
            rim = rim + row_weights[tap] * rims_ref[(row + 1 + tap) * 16 : (row + 2 + tap) * 16, :]
        turned_ref[row, 0:8, :] = rim[0:8]
        turned_ref[row, 8 + LANES : 16 + LANES, :] = rim[8:16]

    places = sublane_ids((WINDOW_COLS, LANES))
    inside = ((places >= 4) | (col_at > 0)) & ((places < 132) | (col_at < col_count - 1))
    row_inside = (lower & (below | (row_at > 0))) | (
        (lanes >= 64) & (jnp.logical_not(below) | (row_at < row_count - 1))
    )
    inside = inside & row_inside
    term = lax.broadcasted_iota(jnp.int32, (2 * LANES, 2 * LANES), 0) % LANES
    gives = lax.broadcasted_iota(jnp.int32, (2 * LANES, 2 * LANES), 1)
    same_part = ((term % 8) < 4) == (gives < LANES)
    sums = jnp.where(((term < 64) == ((gives % LANES) < 64)) & same_part, 1.0, 0.0).astype(HALF_FLOAT)

    def store_windows(target, row, values):
        high, low = split_halves(values)
        high = high.astype(FLOAT)
        rows = (
            jnp.where(lower, high, pltpu.roll(low, 64, axis=1)),
            jnp.where(lower, pltpu.roll(high, 64, axis=1), low),
        )
        for part in range(2):
            start = (row + 4 * part) * 16
            for block in range(BLOCKS):
                target[block, start : start + 16, :] = rows[part][
                    block * 8 : block * 8 + 16
                ].astype(HALF_FLOAT)

    for row in range(4):
        mixed = col_lane_ref[0, 0:1, :] * turned_ref[row, 1 : 1 + WINDOW_COLS, :]
        for tap in range(1, TAP_COUNT):
            mixed = mixed + col_lane_ref[tap, 0:1, :] * turned_ref[
                row, 1 + tap : 1 + tap + WINDOW_COLS, :
            ]
        z = jnp.where(inside, mixed, 0.0)
        high, low = split_halves(z)
        total = dot(jnp.concatenate([high, low.astype(HALF_FLOAT)], axis=1), sums, (1, 0))
        y = z * total[:, :LANES] + swapped(z) * total[:, LANES:]
        store_windows(z_ref, row, z)
        store_windows(y_ref, row, y)


def swapped(values):
    real = (lane_ids((1, LANES)) % 8) < 4
    return jnp.where(real, pltpu.roll(values, LANES - 4, axis=1), -pltpu.roll(values, 4, axis=1))


def near_kernel(own_b, own_a, near_b, near_a, *rest):
    resample_half(first_group(), (own_a, own_b), (near_a, near_b), near_is_below(), *rest)


def link_kernel(
    own_b,
    own_a,
    far_b,
    far_a,
    row_sub_ref,
    row_lane_ref,
    col_lane_ref,
    near_z_ref,
    near_y_ref,
    picks_ref,
    population_ref,
    linked_ref,
    eigen_ref,
    far_z_ref,
    far_y_ref,
    mixed_ref,
    rims_ref,
    turned_ref,
    result_ref,
    first_ref,
    vectors_ref,
    chosen_ref,
):
    resample_half(
        first_group(),
        (own_a, own_b),
        (far_a, far_b),
        jnp.logical_not(near_is_below()),
        row_sub_ref,
        row_lane_ref,
        col_lane_ref,
        far_z_ref,
        far_y_ref,
        mixed_ref,
        rims_ref,
        turned_ref,
    )
    lower = lane_ids((1, LANES)) < 64

    for block in range(BLOCKS):
        y = jnp.concatenate([near_y_ref[block], far_y_ref[block]], axis=0)
        first = dot(picks_ref[block], y, (1, 0))
        first = first + pltpu.roll(first, 64, axis=1)
        high, low = split_halves(jnp.concatenate([first, swapped(first)], axis=0))
        first_ref[block] = first
        vectors_ref[block, :, :LANES] = high
        vectors_ref[block, :, LANES:] = low.astype(HALF_FLOAT)

    for block in range(BLOCKS):
        z = jnp.concatenate([near_z_ref[block], far_z_ref[block]], axis=0)
        inner = dot(vectors_ref[block], jnp.concatenate([z, z], axis=1), (1, 1))
        high, low = split_halves(inner)
        picks = picks_ref[block]
        picks = jnp.concatenate([picks, picks], axis=0)
        chosen_ref[block, :128, :] = high * picks
        chosen_ref[block, 128:, :] = low.astype(HALF_FLOAT) * picks

    for block in range(BLOCKS):
        z = jnp.concatenate([near_z_ref[block], far_z_ref[block]], axis=0)
        outer = dot(chosen_ref[block], z, (1, 0))
        outer = outer[:128] + outer[128:]
        outer = outer + pltpu.roll(outer, 64, axis=1)
        second = outer[:64] - swapped(outer[64:])
        both = jnp.where(lower, second, first_ref[block])
        for row in range(8):
            result_ref[row, block * 8 : block * 8 + 8, :] = both[row * 8 : row * 8 + 8]

    inverse = 1.0 / population_ref[...]
    for row in range(8):
        turned = jnp.transpose(result_ref[row])
        second, first = turned[:64], turned[64:]
        scale = inverse[row : row + 1]
        square = scale * scale
        norm_first = jnp.sqrt(jnp.sum(first * first, axis=0, keepdims=True) * square + EPSILON)
        norm_last = jnp.sqrt(
            jnp.sum(second * second, axis=0, keepdims=True) * (square * square) + EPSILON
        )
        eigen_ref[row : row + 1, :] = norm_last / norm_first
        linked = second * (square * (jnp.sqrt(jnp.float32(NDATE)) / norm_last))
        for group in range(GROUPS):
            for part in range(2):
                begin = ((part * NDATE + 4 * group) * 8) + row
                at = group * 8 + part * 4
                linked_ref[pl.ds(begin, 4, stride=8), :] = linked[at : at + 4]


def canonical(received, dates_dev):
    sources = received.shape[0]
    if dates_dev == 4:
        return received
    cells = received.reshape(sources, 9, 2, dates_dev, LANES)
    cells = jnp.transpose(cells, (1, 2, 0, 3, 4)).reshape(9, 2, GROUPS, 4, LANES)
    return jnp.transpose(cells, (2, 0, 1, 3, 4)).reshape(GROUPS, 9 * TILE, LANES)


def partner(date, row, turn, rows_count):
    other = row + 1 if (row + date + turn) % 2 == 0 else row - 1
    if 0 <= other < rows_count:
        return date * rows_count + other
    return (date ^ 2) * rows_count + row


def vmem(count):
    return [pl.BlockSpec(memory_space=pltpu.VMEM)] * count


def on_device(slc, offsets, masks):
    dates_dev = slc.shape[1]
    rows_dev = slc.shape[2]
    cols_all = slc.shape[3]
    rows_count = lax.axis_size("row")
    cols_count = lax.axis_size("date")
    planes_dev = 2 * dates_dev
    assert rows_dev == TILE and cols_all == cols_count * LANES

    small = pltpu.CompilerParams(vmem_limit_bytes=4 * 1024 * 1024)
    images = slc.reshape(planes_dev, rows_dev, cols_all)
    moves = pl.CostEstimate(flops=0, bytes_accessed=600_000, transcendentals=0)
    half_shape = jax.ShapeDtypeStruct((GROUPS // 2, 9 * TILE, LANES), FLOAT)

    def swap_rows(cells, turn):
        return lax.ppermute(
            cells,
            ("date", "row"),
            [
                (date * rows_count + row, partner(date, row, turn, rows_count))
                for date in range(cols_count)
                for row in range(rows_count)
            ],
        )

    if cols_count == GROUPS:
        pieces = pl.pallas_call(
            pack_pieces,
            out_shape=[jax.ShapeDtypeStruct((9 * TILE, LANES), FLOAT)] * GROUPS,
            in_specs=vmem(1),
            out_specs=vmem(GROUPS),
            scratch_shapes=[pltpu.VMEM((GROUPS, 9 * TILE, LANES), FLOAT)],
            compiler_params=small,
            cost_estimate=moves,
            name="pack",
        )(images)
        pieces = list(pieces[:1]) + [
            lax.ppermute(pieces[turn], "date", [(i, i ^ turn) for i in range(GROUPS)])
            for turn in range(1, GROUPS)
        ]
        own = [
            pl.pallas_call(
                functools.partial(join_kernel, turns),
                out_shape=half_shape,
                in_specs=vmem(4),
                out_specs=vmem(1)[0],
                compiler_params=small,
                cost_estimate=moves,
                name="join",
            )(*[pieces[turn] for turn in turns])
            for turns in ((6, 7, 4, 5), (2, 3, 1, 0))
        ]
    else:
        outgoing = pl.pallas_call(
            pack_blocks,
            out_shape=jax.ShapeDtypeStruct((cols_count, 9 * planes_dev, LANES), FLOAT),
            in_specs=vmem(1),
            out_specs=vmem(1)[0],
            compiler_params=small,
            cost_estimate=moves,
            name="pack",
        )(images)
        received = lax.all_to_all(outgoing, "date", split_axis=0, concat_axis=0, tiled=True)
        received = canonical(received, dates_dev)
        own = [received[: GROUPS // 2], received[GROUPS // 2 :]]
    near_a, far_a, near_b, far_b = [swap_rows(half, turn) for half in own for turn in range(2)]

    picks, population, row_sub, row_lane, col_lane = pl.pallas_call(
        prepare_kernel,
        out_shape=(
            jax.ShapeDtypeStruct((BLOCKS, 64, 256), HALF_FLOAT),
            jax.ShapeDtypeStruct((TILE, LANES), FLOAT),
            jax.ShapeDtypeStruct((TAP_COUNT, 64, LANES), FLOAT),
            jax.ShapeDtypeStruct((TAP_COUNT, TILE, LANES), FLOAT),
            jax.ShapeDtypeStruct((TAP_COUNT, TILE, LANES), FLOAT),
        ),
        in_specs=[pl.BlockSpec(memory_space=pltpu.SMEM)] + vmem(1),
        out_specs=tuple(vmem(5)),
        scratch_shapes=[pltpu.VMEM((LANES, LANES), jnp.int32)],
        compiler_params=small,
        cost_estimate=pl.CostEstimate(flops=4_000_000, bytes_accessed=1_000_000, transcendentals=0),
        name="prepare",
    )(offsets, masks)

    half_scratch = [
        pltpu.VMEM((4, LANES, LANES), FLOAT),
        pltpu.VMEM((2 * LANES, LANES), FLOAT),
        pltpu.VMEM((4, LANES + 16, LANES), FLOAT),
    ]
    windows = jax.ShapeDtypeStruct((BLOCKS, LANES, LANES), HALF_FLOAT)
    near_z, near_y = pl.pallas_call(
        near_kernel,
        out_shape=(windows, windows),
        in_specs=vmem(7),
        out_specs=tuple(vmem(2)),
        scratch_shapes=half_scratch,
        compiler_params=small,
        cost_estimate=pl.CostEstimate(
            flops=200_000_000, bytes_accessed=2_000_000, transcendentals=0
        ),
        name="near",
    )(*own[::-1], near_b, near_a, row_sub, row_lane, col_lane)
    linked, eigen = pl.pallas_call(
        link_kernel,
        out_shape=(
            jax.ShapeDtypeStruct((2 * NDATE * TILE, LANES), FLOAT),
            jax.ShapeDtypeStruct((TILE, LANES), FLOAT),
        ),
        in_specs=vmem(11),
        out_specs=tuple(vmem(2)),
        scratch_shapes=[
            pltpu.VMEM((BLOCKS, LANES, LANES), HALF_FLOAT),
            pltpu.VMEM((BLOCKS, LANES, LANES), HALF_FLOAT),
        ]
        + half_scratch
        + [
            pltpu.VMEM((8, LANES, LANES), FLOAT),
            pltpu.VMEM((BLOCKS, 64, LANES), FLOAT),
            pltpu.VMEM((BLOCKS, 128, 256), HALF_FLOAT),
            pltpu.VMEM((BLOCKS, 256, 256), HALF_FLOAT),
        ],
        compiler_params=pltpu.CompilerParams(vmem_limit_bytes=16 * 1024 * 1024),
        cost_estimate=pl.CostEstimate(
            flops=1_000_000_000, bytes_accessed=2_000_000, transcendentals=0
        ),
        name="link",
    )(*own[::-1], far_b, far_a, row_sub, row_lane, col_lane, near_z, near_y, picks, population)
    return linked.reshape(2, NDATE, TILE, LANES), eigen


def solution(mesh):
    in_specs = (P(None, "date", "row", None), P(), P(None, "row", "date"))
    out_specs = (P(None, None, "row", "date"), P("row", "date"))
    return jax.shard_map(
        on_device, mesh=mesh, in_specs=in_specs, out_specs=out_specs, check_vma=False
    )
```

```python
import functools

import jax
import jax.numpy as jnp
from jax import lax
from jax.experimental import pallas as pl
from jax.experimental.pallas import tpu as pltpu
from jax.sharding import PartitionSpec as P

NDATE = 32
SLOT_COLS = 9
EPSILON = 1e-06
LANES = 128
TILE = 8
GROUPS = 8
TAP_COUNT = 8
WINDOW_ROWS = 16
WINDOW_COLS = 136
BLOCKS = 16

FLOAT = jnp.float32
HALF_FLOAT = jnp.bfloat16


def lane_ids(shape):
    return lax.broadcasted_iota(jnp.int32, shape, len(shape) - 1)


def sublane_ids(shape):
    return lax.broadcasted_iota(jnp.int32, shape, len(shape) - 2)


def pack_blocks(slc_ref, send_ref):
    planes = slc_ref.shape[0]
    blocks = send_ref.shape[0]
    for block in range(blocks):
        for plane in range(planes):
            send_ref[block, pl.ds(plane, TILE, stride=planes), :] = slc_ref[
                plane, :, block * LANES : (block + 1) * LANES
            ]
    lanes = lane_ids((planes, LANES))
    rims = [jnp.zeros((planes, LANES), FLOAT) for _ in range(blocks)]
    for row in range(TILE):
        start = 16 * row
        turned = [
            pltpu.roll(
                send_ref[block, row * planes : (row + 1) * planes, :],
                (start + 8) % LANES,
                axis=1,
            )
            for block in range(blocks)
        ]
        left = (lanes >= start) & (lanes < start + 8)
        right = (lanes >= start + 8) & (lanes < start + 16)
        for block in range(blocks):
            if block > 0:
                rims[block] = jnp.where(left, turned[block - 1], rims[block])
            if block < blocks - 1:
                rims[block] = jnp.where(right, turned[block + 1], rims[block])
    for block in range(blocks):
        send_ref[block, TILE * planes : (TILE + 1) * planes, :] = rims[block]


def pack_pieces(slc_ref, kept_ref, passed_ref, blocks_ref):
    pack_blocks(slc_ref, blocks_ref)
    here = lax.axis_index("date")
    for chip in range(GROUPS // 2):
        kept_ref[chip] = blocks_ref[here ^ (2 * chip)]
        passed_ref[chip] = blocks_ref[here ^ (2 * chip + 1)]


def pair_kernel(kept_ref, passed_ref, *pairs):
    core = lax.axis_index("date") & 1
    for chip, pair_ref in enumerate(pairs):
        pair_ref[core] = kept_ref[chip]
        pair_ref[1 - core] = passed_ref[chip]


def join_kernel(chips, *rest):
    here = lax.axis_index("date")
    for chip, pair_ref in zip(chips, rest[:-1]):
        start = (here ^ (2 * chip)) & 2
        rest[-1][start] = pair_ref[0]
        rest[-1][start + 1] = pair_ref[1]


def tap_weight(distance):
    spread = jnp.abs(2 * distance - 1)
    return jnp.where(spread == 1, 0.5625, jnp.where(spread == 3, -0.0625, 0.0)).astype(FLOAT)


def prepare_kernel(
    offsets_ref, masks_ref, picks_ref, population_ref, row_sub_ref, row_lane_ref, col_lane_ref, words_ref
):
    words = masks_ref.shape[0]
    below = near_is_below()
    total = jnp.zeros((TILE, LANES), jnp.int32)
    for word in range(words):
        bits = masks_ref[word]
        bits = bits - (lax.shift_right_logical(bits, 1) & 0x55555555)
        bits = (bits & 0x33333333) + (lax.shift_right_logical(bits, 2) & 0x33333333)
        bits = (bits + lax.shift_right_logical(bits, 4)) & 0x0F0F0F0F
        bits = bits + lax.shift_right_logical(bits, 8)
        bits = bits + lax.shift_right_logical(bits, 16)
        total = total + (bits & 0xFF)
    population_ref[...] = total.astype(FLOAT)

    lanes = lane_ids((TILE, LANES))
    subs = sublane_ids((TILE, LANES))
    lane_dates = ((lanes % 64) // 8) * 4 + lanes % 4
    row_shift = jnp.zeros((TILE, LANES), jnp.int32)
    col_shift = jnp.zeros((TILE, LANES), jnp.int32)
    for date in range(NDATE):
        here = lane_dates == date
        row_shift = jnp.where(here, offsets_ref[0, date], row_shift)
        col_shift = jnp.where(here, offsets_ref[1, date], col_shift)
    for tap in range(TAP_COUNT):
        row_lane_ref[tap] = tap_weight(tap - 3 - row_shift)
        col_lane_ref[tap] = tap_weight(tap - 3 - col_shift)
    for group in range(GROUPS):
        shift = jnp.zeros((TILE, LANES), jnp.int32)
        for date in range(4):
            shift = jnp.where(subs % 4 == date, offsets_ref[0, 4 * group + date], shift)
        for tap in range(TAP_COUNT):
            row_sub_ref[tap, group * TILE : (group + 1) * TILE, :] = tap_weight(tap - 3 - shift)

    flat = [masks_ref[word] for word in range(words)]
    flat = flat + [jnp.zeros((TILE, LANES), jnp.int32)] * (LANES // TILE - words)
    words_ref[...] = jnp.transpose(jnp.concatenate(flat, axis=0))

    def one_block(block, carry):
        packed = words_ref[pl.ds(pl.multiple_of(block * TILE, TILE), TILE), :]
        for row_pair in range(TILE // 2):
            spread = [[], []]
            for row in (2 * row_pair, 2 * row_pair + 1):
                row_words = [
                    jnp.broadcast_to(
                        packed[:, word * TILE + row : word * TILE + row + 1], (TILE, LANES)
                    )
                    for word in range(words)
                ]
                for half in range(2):
                    near = 8 * half + lanes // 16 - row
                    across = lanes % 16 - subs
                    inside = (near >= 0) & (near <= 8) & (across >= 0) & (across <= 8)
                    amount = jnp.where(inside, (near & 1) * SLOT_COLS + across, 31)
                    first = max(0, 8 * half - row) // 2
                    last = min(8, 8 * half + 7 - row) // 2
                    chosen = row_words[first]
                    for word in range(first + 1, last + 1):
                        chosen = jnp.where(near >= 2 * word, row_words[word], chosen)
                    bits = lax.shift_right_logical(chosen, amount) & 1
                    spread[half].append(bits.astype(FLOAT))
            low_half, high_half = [jnp.concatenate(half, axis=0) for half in spread]
            rows = slice(16 * row_pair, 16 * row_pair + 16)
            picks_ref[block, rows, :LANES] = jnp.where(below, high_half, low_half).astype(HALF_FLOAT)
            picks_ref[block, rows, LANES:] = jnp.where(below, low_half, high_half).astype(HALF_FLOAT)
        return carry

    lax.fori_loop(0, BLOCKS, one_block, 0)


def split_halves(values):
    high = values.astype(HALF_FLOAT)
    low = values - high.astype(FLOAT)
    return high, low


def dot(a, b, contract):
    return lax.dot_general(
        a, b, (((contract[0],), (contract[1],)), ((), ())), preferred_element_type=FLOAT
    )


def packed_rims(base, refs):
    halves = [ref[:, 8 * TILE : 9 * TILE, :].reshape(32, LANES) for ref in refs]
    return jnp.where(
        base == 0, jnp.concatenate(halves, axis=0), jnp.concatenate(halves[::-1], axis=0)
    )


def first_group():
    return (lax.axis_index("date") ^ 4) & 4 if lax.axis_size("date") == GROUPS else 0


def near_is_below():
    return (lax.axis_index("row") + lax.axis_index("date")) % 2 == 0


def resample_half(
    base,
    own_refs,
    other_refs,
    below,
    row_sub_ref,
    row_lane_ref,
    col_lane_ref,
    z_ref,
    y_ref,
    mixed_ref,
    rims_ref,
    turned_ref,
):
    row_at, row_count = lax.axis_index("row"), lax.axis_size("row")
    col_at, col_count = lax.axis_index("date"), lax.axis_size("date")

    exists = (below & (row_at < row_count - 1)) | (jnp.logical_not(below) & (row_at > 0))

    def mix_group(own_ref, other_ref, base, slot):
        group = base + slot
        weights = [
            row_sub_ref[tap, pl.ds(pl.multiple_of(group * TILE, TILE), TILE), :]
            for tap in range(TAP_COUNT)
        ]
        own = [own_ref[slot, row * TILE : (row + 1) * TILE, :] for row in range(TILE)]
        other = [
            jnp.where(exists, other_ref[slot, row * TILE : (row + 1) * TILE, :], 0.0)
            for row in range(TILE)
        ]
        raw = [jnp.where(below, a, b) for a, b in zip(own, other)]
        raw = raw + [jnp.where(below, b, a) for a, b in zip(own, other)]
        for row in range(8):
            mixed = weights[0] * raw[row + 1]
            for tap in range(1, TAP_COUNT):
                mixed = mixed + weights[tap] * raw[row + 1 + tap]
            start = pl.multiple_of((row // 4) * 64 + group * TILE, TILE)
            mixed_ref[row % 4, pl.ds(start, TILE), :] = mixed

    def mix_slot(slot, carry):
        mix_group(own_refs[0], other_refs[0], base, slot)
        mix_group(own_refs[1], other_refs[1], 4 - base, slot)
        return carry

    lax.fori_loop(0, GROUPS // 2, mix_slot, 0)

    lanes = lane_ids((1, LANES))
    lower = lanes < 64
    own, other = [packed_rims(base, refs) for refs in (own_refs, other_refs)]
    other = jnp.where(exists, other, 0.0)
    first, second = jnp.where(below, own, other), jnp.where(below, other, own)
    far_first, far_second = pltpu.roll(first, 64, axis=1), pltpu.roll(second, 64, axis=1)
    rims_ref[0:LANES, :] = jnp.transpose(
        jnp.concatenate([first, jnp.where(lower, far_first, far_second)], axis=0)
    )
    rims_ref[LANES : 2 * LANES, :] = jnp.transpose(jnp.concatenate([second, far_second], axis=0))
    row_weights = [row_lane_ref[tap, 0:1, :] for tap in range(TAP_COUNT)]
    for row in range(4):
        turned_ref[row, 8 : 8 + LANES, :] = jnp.transpose(mixed_ref[row])
        rim = row_weights[0] * rims_ref[(row + 1) * 16 : (row + 2) * 16, :]
        for tap in range(1, TAP_COUNT):
            rim = rim + row_weights[tap] * rims_ref[(row + 1 + tap) * 16 : (row + 2 + tap) * 16, :]
        turned_ref[row, 0:8, :] = rim[0:8]
        turned_ref[row, 8 + LANES : 16 + LANES, :] = rim[8:16]

    places = sublane_ids((WINDOW_COLS, LANES))
    inside = ((places >= 4) | (col_at > 0)) & ((places < 132) | (col_at < col_count - 1))
    row_inside = (lower & (below | (row_at > 0))) | (
        (lanes >= 64) & (jnp.logical_not(below) | (row_at < row_count - 1))
    )
    inside = inside & row_inside
    term = lax.broadcasted_iota(jnp.int32, (2 * LANES, 2 * LANES), 0) % LANES
    gives = lax.broadcasted_iota(jnp.int32, (2 * LANES, 2 * LANES), 1)
    same_part = ((term % 8) < 4) == (gives < LANES)
    sums = jnp.where(((term < 64) == ((gives % LANES) < 64)) & same_part, 1.0, 0.0).astype(HALF_FLOAT)

    def store_windows(target, row, values):
        high, low = split_halves(values)
        high = high.astype(FLOAT)
        rows = (
            jnp.where(lower, high, pltpu.roll(low, 64, axis=1)),
            jnp.where(lower, pltpu.roll(high, 64, axis=1), low),
        )
        for part in range(2):
            start = (row + 4 * part) * 16
            for block in range(BLOCKS):
                target[block, start : start + 16, :] = rows[part][
                    block * 8 : block * 8 + 16
                ].astype(HALF_FLOAT)

    for row in range(4):
        mixed = col_lane_ref[0, 0:1, :] * turned_ref[row, 1 : 1 + WINDOW_COLS, :]
        for tap in range(1, TAP_COUNT):
            mixed = mixed + col_lane_ref[tap, 0:1, :] * turned_ref[
                row, 1 + tap : 1 + tap + WINDOW_COLS, :
            ]
        z = jnp.where(inside, mixed, 0.0)
        high, low = split_halves(z)
        total = dot(jnp.concatenate([high, low.astype(HALF_FLOAT)], axis=1), sums, (1, 0))
        y = z * total[:, :LANES] + swapped(z) * total[:, LANES:]
        store_windows(z_ref, row, z)
        store_windows(y_ref, row, y)


def swapped(values):
    real = (lane_ids((1, LANES)) % 8) < 4
    return jnp.where(real, pltpu.roll(values, LANES - 4, axis=1), -pltpu.roll(values, 4, axis=1))


def near_kernel(own_b, own_a, near_b, near_a, *rest):
    resample_half(first_group(), (own_a, own_b), (near_a, near_b), near_is_below(), *rest)


def link_kernel(
    own_b,
    own_a,
    far_b,
    far_a,
    row_sub_ref,
    row_lane_ref,
    col_lane_ref,
    near_z_ref,
    near_y_ref,
    picks_ref,
    population_ref,
    linked_ref,
    eigen_ref,
    far_z_ref,
    far_y_ref,
    mixed_ref,
    rims_ref,
    turned_ref,
    result_ref,
    first_ref,
    vectors_ref,
    chosen_ref,
):
    resample_half(
        first_group(),
        (own_a, own_b),
        (far_a, far_b),
        jnp.logical_not(near_is_below()),
        row_sub_ref,
        row_lane_ref,
        col_lane_ref,
        far_z_ref,
        far_y_ref,
        mixed_ref,
        rims_ref,
        turned_ref,
    )
    lower = lane_ids((1, LANES)) < 64

    for block in range(BLOCKS):
        y = jnp.concatenate([near_y_ref[block], far_y_ref[block]], axis=0)
        first = dot(picks_ref[block], y, (1, 0))
        first = first + pltpu.roll(first, 64, axis=1)
        high, low = split_halves(jnp.concatenate([first, swapped(first)], axis=0))
        first_ref[block] = first
        vectors_ref[block, :, :LANES] = high
        vectors_ref[block, :, LANES:] = low.astype(HALF_FLOAT)

    for block in range(BLOCKS):
        z = jnp.concatenate([near_z_ref[block], far_z_ref[block]], axis=0)
        inner = dot(vectors_ref[block], jnp.concatenate([z, z], axis=1), (1, 1))
        high, low = split_halves(inner)
        picks = picks_ref[block]
        picks = jnp.concatenate([picks, picks], axis=0)
        chosen_ref[block, :128, :] = high * picks
        chosen_ref[block, 128:, :] = low.astype(HALF_FLOAT) * picks

    for block in range(BLOCKS):
        z = jnp.concatenate([near_z_ref[block], far_z_ref[block]], axis=0)
        outer = dot(chosen_ref[block], z, (1, 0))
        outer = outer[:128] + outer[128:]
        outer = outer + pltpu.roll(outer, 64, axis=1)
        second = outer[:64] - swapped(outer[64:])
        both = jnp.where(lower, second, first_ref[block])
        for row in range(8):
            result_ref[row, block * 8 : block * 8 + 8, :] = both[row * 8 : row * 8 + 8]

    inverse = 1.0 / population_ref[...]
    for row in range(8):
        turned = jnp.transpose(result_ref[row])
        second, first = turned[:64], turned[64:]
        scale = inverse[row : row + 1]
        square = scale * scale
        norm_first = jnp.sqrt(jnp.sum(first * first, axis=0, keepdims=True) * square + EPSILON)
        norm_last = jnp.sqrt(
            jnp.sum(second * second, axis=0, keepdims=True) * (square * square) + EPSILON
        )
        eigen_ref[row : row + 1, :] = norm_last / norm_first
        linked = second * (square * (jnp.sqrt(jnp.float32(NDATE)) / norm_last))
        for group in range(GROUPS):
            for part in range(2):
                begin = ((part * NDATE + 4 * group) * 8) + row
                at = group * 8 + part * 4
                linked_ref[pl.ds(begin, 4, stride=8), :] = linked[at : at + 4]


def canonical(received, dates_dev):
    sources = received.shape[0]
    if dates_dev == 4:
        return received
    cells = received.reshape(sources, 9, 2, dates_dev, LANES)
    cells = jnp.transpose(cells, (1, 2, 0, 3, 4)).reshape(9, 2, GROUPS, 4, LANES)
    return jnp.transpose(cells, (2, 0, 1, 3, 4)).reshape(GROUPS, 9 * TILE, LANES)


def partner(date, row, turn, rows_count):
    other = row + 1 if (row + date + turn) % 2 == 0 else row - 1
    if 0 <= other < rows_count:
        return date * rows_count + other
    return (date ^ 2) * rows_count + row


def vmem(count):
    return [pl.BlockSpec(memory_space=pltpu.VMEM)] * count


def on_device(slc, offsets, masks):
    dates_dev = slc.shape[1]
    rows_dev = slc.shape[2]
    cols_all = slc.shape[3]
    rows_count = lax.axis_size("row")
    cols_count = lax.axis_size("date")
    planes_dev = 2 * dates_dev
    assert rows_dev == TILE and cols_all == cols_count * LANES

    small = pltpu.CompilerParams(vmem_limit_bytes=4 * 1024 * 1024)
    images = slc.reshape(planes_dev, rows_dev, cols_all)
    moves = pl.CostEstimate(flops=0, bytes_accessed=600_000, transcendentals=0)
    half_shape = jax.ShapeDtypeStruct((GROUPS // 2, 9 * TILE, LANES), FLOAT)

    def swap_rows(cells, turn):
        return lax.ppermute(
            cells,
            ("date", "row"),
            [
                (date * rows_count + row, partner(date, row, turn, rows_count))
                for date in range(cols_count)
                for row in range(rows_count)
            ],
        )

    if cols_count == GROUPS:
        kept, passed = pl.pallas_call(
            pack_pieces,
            out_shape=(half_shape, half_shape),
            in_specs=vmem(1),
            out_specs=tuple(vmem(2)),
            scratch_shapes=[pltpu.VMEM((GROUPS, 9 * TILE, LANES), FLOAT)],
            compiler_params=small,
            cost_estimate=moves,
            name="pack",
        )(images)
        passed = lax.ppermute(passed, "date", [(i, i ^ 1) for i in range(GROUPS)])
        pairs = pl.pallas_call(
            pair_kernel,
            out_shape=[jax.ShapeDtypeStruct((2, 9 * TILE, LANES), FLOAT)] * (GROUPS // 2),
            in_specs=vmem(2),
            out_specs=vmem(GROUPS // 2),
            compiler_params=small,
            cost_estimate=moves,
            name="pair",
        )(kept, passed)
        pairs = list(pairs[:1]) + [
            lax.ppermute(pairs[chip], "date", [(i, i ^ (2 * chip)) for i in range(GROUPS)])
            for chip in range(1, GROUPS // 2)
        ]
        own = [
            pl.pallas_call(
                functools.partial(join_kernel, chips),
                out_shape=half_shape,
                in_specs=vmem(2),
                out_specs=vmem(1)[0],
                compiler_params=small,
                cost_estimate=moves,
                name="join",
            )(*[pairs[chip] for chip in chips])
            for chips in ((3, 2), (1, 0))
        ]
    else:
        outgoing = pl.pallas_call(
            pack_blocks,
            out_shape=jax.ShapeDtypeStruct((cols_count, 9 * planes_dev, LANES), FLOAT),
            in_specs=vmem(1),
            out_specs=vmem(1)[0],
            compiler_params=small,
            cost_estimate=moves,
            name="pack",
        )(images)
        received = lax.all_to_all(outgoing, "date", split_axis=0, concat_axis=0, tiled=True)
        received = canonical(received, dates_dev)
        own = [received[: GROUPS // 2], received[GROUPS // 2 :]]
    near_a, far_a, near_b, far_b = [swap_rows(half, turn) for half in own for turn in range(2)]

    picks, population, row_sub, row_lane, col_lane = pl.pallas_call(
        prepare_kernel,
        out_shape=(
            jax.ShapeDtypeStruct((BLOCKS, 64, 256), HALF_FLOAT),
            jax.ShapeDtypeStruct((TILE, LANES), FLOAT),
            jax.ShapeDtypeStruct((TAP_COUNT, 64, LANES), FLOAT),
            jax.ShapeDtypeStruct((TAP_COUNT, TILE, LANES), FLOAT),
            jax.ShapeDtypeStruct((TAP_COUNT, TILE, LANES), FLOAT),
        ),
        in_specs=[pl.BlockSpec(memory_space=pltpu.SMEM)] + vmem(1),
        out_specs=tuple(vmem(5)),
        scratch_shapes=[pltpu.VMEM((LANES, LANES), jnp.int32)],
        compiler_params=small,
        cost_estimate=pl.CostEstimate(flops=4_000_000, bytes_accessed=1_000_000, transcendentals=0),
        name="prepare",
    )(offsets, masks)

    half_scratch = [
        pltpu.VMEM((4, LANES, LANES), FLOAT),
        pltpu.VMEM((2 * LANES, LANES), FLOAT),
        pltpu.VMEM((4, LANES + 16, LANES), FLOAT),
    ]
    windows = jax.ShapeDtypeStruct((BLOCKS, LANES, LANES), HALF_FLOAT)
    near_z, near_y = pl.pallas_call(
        near_kernel,
        out_shape=(windows, windows),
        in_specs=vmem(7),
        out_specs=tuple(vmem(2)),
        scratch_shapes=half_scratch,
        compiler_params=small,
        cost_estimate=pl.CostEstimate(
            flops=200_000_000, bytes_accessed=2_000_000, transcendentals=0
        ),
        name="near",
    )(*own[::-1], near_b, near_a, row_sub, row_lane, col_lane)
    linked, eigen = pl.pallas_call(
        link_kernel,
        out_shape=(
            jax.ShapeDtypeStruct((2 * NDATE * TILE, LANES), FLOAT),
            jax.ShapeDtypeStruct((TILE, LANES), FLOAT),
        ),
        in_specs=vmem(11),
        out_specs=tuple(vmem(2)),
        scratch_shapes=[
            pltpu.VMEM((BLOCKS, LANES, LANES), HALF_FLOAT),
            pltpu.VMEM((BLOCKS, LANES, LANES), HALF_FLOAT),
        ]
        + half_scratch
        + [
            pltpu.VMEM((8, LANES, LANES), FLOAT),
            pltpu.VMEM((BLOCKS, 64, LANES), FLOAT),
            pltpu.VMEM((BLOCKS, 128, 256), HALF_FLOAT),
            pltpu.VMEM((BLOCKS, 256, 256), HALF_FLOAT),
        ],
        compiler_params=pltpu.CompilerParams(vmem_limit_bytes=16 * 1024 * 1024),
        cost_estimate=pl.CostEstimate(
            flops=1_000_000_000, bytes_accessed=2_000_000, transcendentals=0
        ),
        name="link",
    )(*own[::-1], far_b, far_a, row_sub, row_lane, col_lane, near_z, near_y, picks, population)
    return linked.reshape(2, NDATE, TILE, LANES), eigen


def solution(mesh):
    in_specs = (P(None, "date", "row", None), P(), P(None, "row", "date"))
    out_specs = (P(None, None, "row", "date"), P("row", "date"))
    return jax.shard_map(
        on_device, mesh=mesh, in_specs=in_specs, out_specs=out_specs, check_vma=False
    )
```

```python
import functools

import jax
import jax.numpy as jnp
from jax import lax
from jax.experimental import pallas as pl
from jax.experimental.pallas import tpu as pltpu
from jax.sharding import PartitionSpec as P

NDATE = 32
SLOT_COLS = 9
EPSILON = 1e-06
LANES = 128
TILE = 8
GROUPS = 8
TAP_COUNT = 8
WINDOW_ROWS = 16
WINDOW_COLS = 136
CHUNKS = 4
BLOCKS = 16

FLOAT = jnp.float32
HALF_FLOAT = jnp.bfloat16


def lane_ids(shape):
    return lax.broadcasted_iota(jnp.int32, shape, len(shape) - 1)


def sublane_ids(shape):
    return lax.broadcasted_iota(jnp.int32, shape, len(shape) - 2)


def pack_blocks(slc_ref, send_ref, images_ref, arrived):
    planes = slc_ref.shape[0]
    blocks = send_ref.shape[0]
    copies = [
        pltpu.make_async_copy(slc_ref.at[plane], images_ref.at[plane], arrived.at[plane])
        for plane in range(planes)
    ]
    for copy in copies:
        copy.start()
    for plane, copy in enumerate(copies):
        copy.wait()
        for block in range(blocks):
            send_ref[block, pl.ds(plane, TILE, stride=planes), :] = images_ref[
                plane, :, block * LANES : (block + 1) * LANES
            ]
    lanes = lane_ids((planes, LANES))
    rims = [jnp.zeros((planes, LANES), FLOAT) for _ in range(blocks)]
    for row in range(TILE):
        start = 16 * row
        turned = [
            pltpu.roll(
                send_ref[block, row * planes : (row + 1) * planes, :],
                (start + 8) % LANES,
                axis=1,
            )
            for block in range(blocks)
        ]
        left = (lanes >= start) & (lanes < start + 8)
        right = (lanes >= start + 8) & (lanes < start + 16)
        for block in range(blocks):
            if block > 0:
                rims[block] = jnp.where(left, turned[block - 1], rims[block])
            if block < blocks - 1:
                rims[block] = jnp.where(right, turned[block + 1], rims[block])
    for block in range(blocks):
        send_ref[block, TILE * planes : (TILE + 1) * planes, :] = rims[block]


def pack_pieces(slc_ref, *rest):
    pieces, blocks_ref = rest[:-3], rest[-3]
    pack_blocks(slc_ref, *rest[-3:])
    here = lax.axis_index("date")
    for turn, piece_ref in enumerate(pieces):
        piece_ref[...] = blocks_ref[here ^ turn]


def join_kernel(turns, *rest):
    here = lax.axis_index("date")
    for turn, piece_ref in zip(turns, rest[:-1]):
        rest[-1][(here ^ turn) % 4] = piece_ref[...]


def tap_weight(distance):
    spread = jnp.abs(2 * distance - 1)
    return jnp.where(spread == 1, 0.5625, jnp.where(spread == 3, -0.0625, 0.0)).astype(FLOAT)


def prepare_kernel(
    offsets_ref, masks_ref, picks_ref, population_ref, row_sub_ref, row_lane_ref, col_lane_ref, words_ref
):
    words = masks_ref.shape[0]
    below = near_is_below()
    total = jnp.zeros((TILE, LANES), jnp.int32)
    for word in range(words):
        bits = masks_ref[word]
        bits = bits - (lax.shift_right_logical(bits, 1) & 0x55555555)
        bits = (bits & 0x33333333) + (lax.shift_right_logical(bits, 2) & 0x33333333)
        bits = (bits + lax.shift_right_logical(bits, 4)) & 0x0F0F0F0F
        bits = bits + lax.shift_right_logical(bits, 8)
        bits = bits + lax.shift_right_logical(bits, 16)
        total = total + (bits & 0xFF)
    population_ref[...] = total.astype(FLOAT)

    lanes = lane_ids((TILE, LANES))
    subs = sublane_ids((TILE, LANES))
    lane_dates = ((lanes % 64) // 8) * 4 + lanes % 4
    row_shift = jnp.zeros((TILE, LANES), jnp.int32)
    col_shift = jnp.zeros((TILE, LANES), jnp.int32)
    for date in range(NDATE):
        here = lane_dates == date
        row_shift = jnp.where(here, offsets_ref[0, date], row_shift)
        col_shift = jnp.where(here, offsets_ref[1, date], col_shift)
    for tap in range(TAP_COUNT):
        row_lane_ref[tap] = tap_weight(tap - 3 - row_shift)
        col_lane_ref[tap] = tap_weight(tap - 3 - col_shift)
    for group in range(GROUPS):
        shift = jnp.zeros((TILE, LANES), jnp.int32)
        for date in range(4):
            shift = jnp.where(subs % 4 == date, offsets_ref[0, 4 * group + date], shift)
        for tap in range(TAP_COUNT):
            row_sub_ref[tap, group * TILE : (group + 1) * TILE, :] = tap_weight(tap - 3 - shift)

    flat = [masks_ref[word] for word in range(words)]
    flat = flat + [jnp.zeros((TILE, LANES), jnp.int32)] * (LANES // TILE - words)
    words_ref[...] = jnp.transpose(jnp.concatenate(flat, axis=0))

    def one_block(block, carry):
        packed = words_ref[pl.ds(pl.multiple_of(block * TILE, TILE), TILE), :]
        for row_pair in range(TILE // 2):
            spread = [[], []]
            for row in (2 * row_pair, 2 * row_pair + 1):
                row_words = [
                    jnp.broadcast_to(
                        packed[:, word * TILE + row : word * TILE + row + 1], (TILE, LANES)
                    )
                    for word in range(words)
                ]
                for half in range(2):
                    near = 8 * half + lanes // 16 - row
                    across = lanes % 16 - subs
                    inside = (near >= 0) & (near <= 8) & (across >= 0) & (across <= 8)
                    amount = jnp.where(inside, (near & 1) * SLOT_COLS + across, 31)
                    first = max(0, 8 * half - row) // 2
                    last = min(8, 8 * half + 7 - row) // 2
                    chosen = row_words[first]
                    for word in range(first + 1, last + 1):
                        chosen = jnp.where(near >= 2 * word, row_words[word], chosen)
                    bits = lax.shift_right_logical(chosen, amount) & 1
                    spread[half].append(bits.astype(FLOAT))
            low_half, high_half = [jnp.concatenate(half, axis=0) for half in spread]
            rows = slice(16 * row_pair, 16 * row_pair + 16)
            picks_ref[block, rows, :LANES] = jnp.where(below, high_half, low_half).astype(HALF_FLOAT)
            picks_ref[block, rows, LANES:] = jnp.where(below, low_half, high_half).astype(HALF_FLOAT)
        return carry

    lax.fori_loop(0, BLOCKS, one_block, 0)


def split_halves(values):
    high = values.astype(HALF_FLOAT)
    low = values - high.astype(FLOAT)
    return high, low


def dot(a, b, contract):
    return lax.dot_general(
        a, b, (((contract[0],), (contract[1],)), ((), ())), preferred_element_type=FLOAT
    )


def packed_rims(base, refs):
    halves = [ref[:, 8 * TILE : 9 * TILE, :].reshape(32, LANES) for ref in refs]
    return jnp.where(
        base == 0, jnp.concatenate(halves, axis=0), jnp.concatenate(halves[::-1], axis=0)
    )


def first_group():
    return (lax.axis_index("date") ^ 4) & 4 if lax.axis_size("date") == GROUPS else 0


def near_is_below():
    return (lax.axis_index("row") + lax.axis_index("date")) % 2 == 0


def resample_half(
    base,
    own_refs,
    other_refs,
    below,
    row_sub_ref,
    row_lane_ref,
    col_lane_ref,
    z_ref,
    y_ref,
    mixed_ref,
    rims_ref,
    turned_ref,
):
    row_at, row_count = lax.axis_index("row"), lax.axis_size("row")
    col_at, col_count = lax.axis_index("date"), lax.axis_size("date")

    exists = (below & (row_at < row_count - 1)) | (jnp.logical_not(below) & (row_at > 0))

    def mix_group(own_ref, other_ref, base, slot):
        group = base + slot
        weights = [
            row_sub_ref[tap, pl.ds(pl.multiple_of(group * TILE, TILE), TILE), :]
            for tap in range(TAP_COUNT)
        ]
        own = [own_ref[slot, row * TILE : (row + 1) * TILE, :] for row in range(TILE)]
        other = [
            jnp.where(exists, other_ref[slot, row * TILE : (row + 1) * TILE, :], 0.0)
            for row in range(TILE)
        ]
        raw = [jnp.where(below, a, b) for a, b in zip(own, other)]
        raw = raw + [jnp.where(below, b, a) for a, b in zip(own, other)]
        for row in range(8):
            mixed = weights[0] * raw[row + 1]
            for tap in range(1, TAP_COUNT):
                mixed = mixed + weights[tap] * raw[row + 1 + tap]
            start = pl.multiple_of((row // 4) * 64 + group * TILE, TILE)
            mixed_ref[row % 4, pl.ds(start, TILE), :] = mixed

    def mix_slot(slot, carry):
        mix_group(own_refs[0], other_refs[0], base, slot)
        mix_group(own_refs[1], other_refs[1], 4 - base, slot)
        return carry

    lax.fori_loop(0, GROUPS // 2, mix_slot, 0)

    lanes = lane_ids((1, LANES))
    lower = lanes < 64
    own, other = [packed_rims(base, refs) for refs in (own_refs, other_refs)]
    other = jnp.where(exists, other, 0.0)
    first, second = jnp.where(below, own, other), jnp.where(below, other, own)
    far_first, far_second = pltpu.roll(first, 64, axis=1), pltpu.roll(second, 64, axis=1)
    rims_ref[0:LANES, :] = jnp.transpose(
        jnp.concatenate([first, jnp.where(lower, far_first, far_second)], axis=0)
    )
    rims_ref[LANES : 2 * LANES, :] = jnp.transpose(jnp.concatenate([second, far_second], axis=0))
    row_weights = [row_lane_ref[tap, 0:1, :] for tap in range(TAP_COUNT)]
    for row in range(4):
        turned_ref[row, 8 : 8 + LANES, :] = jnp.transpose(mixed_ref[row])
        rim = row_weights[0] * rims_ref[(row + 1) * 16 : (row + 2) * 16, :]
        for tap in range(1, TAP_COUNT):
            rim = rim + row_weights[tap] * rims_ref[(row + 1 + tap) * 16 : (row + 2 + tap) * 16, :]
        turned_ref[row, 0:8, :] = rim[0:8]
        turned_ref[row, 8 + LANES : 16 + LANES, :] = rim[8:16]

    places = sublane_ids((WINDOW_COLS, LANES))
    inside = ((places >= 4) | (col_at > 0)) & ((places < 132) | (col_at < col_count - 1))
    row_inside = (lower & (below | (row_at > 0))) | (
        (lanes >= 64) & (jnp.logical_not(below) | (row_at < row_count - 1))
    )
    inside = inside & row_inside
    term = lax.broadcasted_iota(jnp.int32, (2 * LANES, 2 * LANES), 0) % LANES
    gives = lax.broadcasted_iota(jnp.int32, (2 * LANES, 2 * LANES), 1)
    same_part = ((term % 8) < 4) == (gives < LANES)
    sums = jnp.where(((term < 64) == ((gives % LANES) < 64)) & same_part, 1.0, 0.0).astype(HALF_FLOAT)

    def store_windows(target, row, values):
        high, low = split_halves(values)
        high = high.astype(FLOAT)
        rows = (
            jnp.where(lower, high, pltpu.roll(low, 64, axis=1)),
            jnp.where(lower, pltpu.roll(high, 64, axis=1), low),
        )
        for part in range(2):
            start = (row + 4 * part) * 16
            for block in range(BLOCKS):
                target[block, start : start + 16, :] = rows[part][
                    block * 8 : block * 8 + 16
                ].astype(HALF_FLOAT)

    for row in range(4):
        mixed = col_lane_ref[0, 0:1, :] * turned_ref[row, 1 : 1 + WINDOW_COLS, :]
        for tap in range(1, TAP_COUNT):
            mixed = mixed + col_lane_ref[tap, 0:1, :] * turned_ref[
                row, 1 + tap : 1 + tap + WINDOW_COLS, :
            ]
        z = jnp.where(inside, mixed, 0.0)
        high, low = split_halves(z)
        total = dot(jnp.concatenate([high, low.astype(HALF_FLOAT)], axis=1), sums, (1, 0))
        y = z * total[:, :LANES] + swapped(z) * total[:, LANES:]
        store_windows(z_ref, row, z)
        store_windows(y_ref, row, y)


def swapped(values):
    real = (lane_ids((1, LANES)) % 8) < 4
    return jnp.where(real, pltpu.roll(values, LANES - 4, axis=1), -pltpu.roll(values, 4, axis=1))


def near_kernel(own_b, own_a, near_b, near_a, *rest):
    resample_half(first_group(), (own_a, own_b), (near_a, near_b), near_is_below(), *rest)


def link_kernel(
    own_b,
    own_a,
    far_b,
    far_a,
    row_sub_ref,
    row_lane_ref,
    col_lane_ref,
    near_z_ref,
    near_y_ref,
    picks_ref,
    population_ref,
    linked_ref,
    eigen_ref,
    far_z_ref,
    far_y_ref,
    mixed_ref,
    rims_ref,
    turned_ref,
    result_ref,
    first_ref,
    vectors_ref,
    chosen_ref,
    spectra_ref,
    norms_ref,
    staged_ref,
    written,
):
    resample_half(
        first_group(),
        (own_a, own_b),
        (far_a, far_b),
        jnp.logical_not(near_is_below()),
        row_sub_ref,
        row_lane_ref,
        col_lane_ref,
        far_z_ref,
        far_y_ref,
        mixed_ref,
        rims_ref,
        turned_ref,
    )
    lower = lane_ids((1, LANES)) < 64

    for block in range(BLOCKS):
        y = jnp.concatenate([near_y_ref[block], far_y_ref[block]], axis=0)
        first = dot(picks_ref[block], y, (1, 0))
        first = first + pltpu.roll(first, 64, axis=1)
        high, low = split_halves(jnp.concatenate([first, swapped(first)], axis=0))
        first_ref[block] = first
        vectors_ref[block, :, :LANES] = high
        vectors_ref[block, :, LANES:] = low.astype(HALF_FLOAT)

    for block in range(BLOCKS):
        z = jnp.concatenate([near_z_ref[block], far_z_ref[block]], axis=0)
        inner = dot(vectors_ref[block], jnp.concatenate([z, z], axis=1), (1, 1))
        high, low = split_halves(inner)
        picks = picks_ref[block]
        picks = jnp.concatenate([picks, picks], axis=0)
        chosen_ref[block, :128, :] = high * picks
        chosen_ref[block, 128:, :] = low.astype(HALF_FLOAT) * picks

    for block in range(BLOCKS):
        z = jnp.concatenate([near_z_ref[block], far_z_ref[block]], axis=0)
        outer = dot(chosen_ref[block], z, (1, 0))
        outer = outer[:128] + outer[128:]
        outer = outer + pltpu.roll(outer, 64, axis=1)
        second = outer[:64] - swapped(outer[64:])
        both = jnp.where(lower, second, first_ref[block])
        for row in range(8):
            result_ref[row, block * 8 : block * 8 + 8, :] = both[row * 8 : row * 8 + 8]

    for row in range(8):
        turned = jnp.transpose(result_ref[row])
        spectra_ref[row * LANES : (row + 1) * LANES, :] = turned
        squares = turned * turned
        norms_ref[0, row : row + 1, :] = jnp.sum(squares[64:], axis=0, keepdims=True)
        norms_ref[1, row : row + 1, :] = jnp.sum(squares[:64], axis=0, keepdims=True)
    scale = 1.0 / population_ref[...]
    square = scale * scale
    norm_first = jnp.sqrt(norms_ref[0] * square + EPSILON)
    norm_last = jnp.sqrt(norms_ref[1] * (square * square) + EPSILON)
    eigen_ref[...] = norm_last / norm_first
    factor = square * (jnp.sqrt(jnp.float32(NDATE)) / norm_last)
    copies = []
    for chunk in range(CHUNKS):
        size = 2 * NDATE // CHUNKS
        for plane in range(chunk * size, (chunk + 1) * size):
            part, date = plane // NDATE, plane % NDATE
            at = (date // 4) * 8 + part * 4 + date % 4
            staged_ref[plane * TILE : (plane + 1) * TILE, :] = (
                spectra_ref[pl.ds(at, TILE, stride=LANES), :] * factor
            )
        rows = pl.ds(chunk * size * TILE, size * TILE)
        copies.append(
            pltpu.make_async_copy(staged_ref.at[rows], linked_ref.at[rows], written.at[chunk])
        )
        copies[-1].start()
    for copy in copies:
        copy.wait()


def canonical(received, dates_dev):
    sources = received.shape[0]
    if dates_dev == 4:
        return received
    cells = received.reshape(sources, 9, 2, dates_dev, LANES)
    cells = jnp.transpose(cells, (1, 2, 0, 3, 4)).reshape(9, 2, GROUPS, 4, LANES)
    return jnp.transpose(cells, (2, 0, 1, 3, 4)).reshape(GROUPS, 9 * TILE, LANES)


def partner(date, row, turn, rows_count):
    other = row + 1 if (row + date + turn) % 2 == 0 else row - 1
    if 0 <= other < rows_count:
        return date * rows_count + other
    return (date ^ 2) * rows_count + row


def vmem(count):
    return [pl.BlockSpec(memory_space=pltpu.VMEM)] * count


def on_device(slc, offsets, masks):
    dates_dev = slc.shape[1]
    rows_dev = slc.shape[2]
    cols_all = slc.shape[3]
    rows_count = lax.axis_size("row")
    cols_count = lax.axis_size("date")
    planes_dev = 2 * dates_dev
    assert rows_dev == TILE and cols_all == cols_count * LANES

    small = pltpu.CompilerParams(vmem_limit_bytes=4 * 1024 * 1024)
    images = pltpu.with_memory_space_constraint(
        slc.reshape(planes_dev, rows_dev, cols_all), pltpu.HBM
    )
    images_scratch = [
        pltpu.VMEM(images.shape, FLOAT),
        pltpu.SemaphoreType.DMA((planes_dev,)),
    ]
    moves = pl.CostEstimate(flops=0, bytes_accessed=600_000, transcendentals=0)
    half_shape = jax.ShapeDtypeStruct((GROUPS // 2, 9 * TILE, LANES), FLOAT)

    def swap_rows(cells, turn):
        return lax.ppermute(
            cells,
            ("date", "row"),
            [
                (date * rows_count + row, partner(date, row, turn, rows_count))
                for date in range(cols_count)
                for row in range(rows_count)
            ],
        )

    if cols_count == GROUPS:
        pieces = pl.pallas_call(
            pack_pieces,
            out_shape=[jax.ShapeDtypeStruct((9 * TILE, LANES), FLOAT)] * GROUPS,
            in_specs=[pl.BlockSpec(memory_space=pltpu.HBM)],
            out_specs=vmem(GROUPS),
            scratch_shapes=[pltpu.VMEM((GROUPS, 9 * TILE, LANES), FLOAT)] + images_scratch,
            compiler_params=small,
            cost_estimate=moves,
            name="pack",
        )(images)
        pieces = list(pieces[:1]) + [
            lax.ppermute(pieces[turn], "date", [(i, i ^ turn) for i in range(GROUPS)])
            for turn in range(1, GROUPS)
        ]
        own = [
            pl.pallas_call(
                functools.partial(join_kernel, turns),
                out_shape=half_shape,
                in_specs=vmem(4),
                out_specs=vmem(1)[0],
                compiler_params=small,
                cost_estimate=moves,
                name="join",
            )(*[pieces[turn] for turn in turns])
            for turns in ((6, 7, 4, 5), (2, 3, 1, 0))
        ]
    else:
        outgoing = pl.pallas_call(
            pack_blocks,
            out_shape=jax.ShapeDtypeStruct((cols_count, 9 * planes_dev, LANES), FLOAT),
            in_specs=[pl.BlockSpec(memory_space=pltpu.HBM)],
            out_specs=vmem(1)[0],
            scratch_shapes=images_scratch,
            compiler_params=small,
            cost_estimate=moves,
            name="pack",
        )(images)
        received = lax.all_to_all(outgoing, "date", split_axis=0, concat_axis=0, tiled=True)
        received = canonical(received, dates_dev)
        own = [received[: GROUPS // 2], received[GROUPS // 2 :]]
    near_a, far_a, near_b, far_b = [swap_rows(half, turn) for half in own for turn in range(2)]

    picks, population, row_sub, row_lane, col_lane = pl.pallas_call(
        prepare_kernel,
        out_shape=(
            jax.ShapeDtypeStruct((BLOCKS, 64, 256), HALF_FLOAT),
            jax.ShapeDtypeStruct((TILE, LANES), FLOAT),
            jax.ShapeDtypeStruct((TAP_COUNT, 64, LANES), FLOAT),
            jax.ShapeDtypeStruct((TAP_COUNT, TILE, LANES), FLOAT),
            jax.ShapeDtypeStruct((TAP_COUNT, TILE, LANES), FLOAT),
        ),
        in_specs=[pl.BlockSpec(memory_space=pltpu.SMEM)] + vmem(1),
        out_specs=tuple(vmem(5)),
        scratch_shapes=[pltpu.VMEM((LANES, LANES), jnp.int32)],
        compiler_params=small,
        cost_estimate=pl.CostEstimate(flops=4_000_000, bytes_accessed=1_000_000, transcendentals=0),
        name="prepare",
    )(offsets, masks)

    half_scratch = [
        pltpu.VMEM((4, LANES, LANES), FLOAT),
        pltpu.VMEM((2 * LANES, LANES), FLOAT),
        pltpu.VMEM((4, LANES + 16, LANES), FLOAT),
    ]
    windows = jax.ShapeDtypeStruct((BLOCKS, LANES, LANES), HALF_FLOAT)
    near_z, near_y = pl.pallas_call(
        near_kernel,
        out_shape=(windows, windows),
        in_specs=vmem(7),
        out_specs=tuple(vmem(2)),
        scratch_shapes=half_scratch,
        compiler_params=small,
        cost_estimate=pl.CostEstimate(
            flops=200_000_000, bytes_accessed=2_000_000, transcendentals=0
        ),
        name="near",
    )(*own[::-1], near_b, near_a, row_sub, row_lane, col_lane)
    linked, eigen = pl.pallas_call(
        link_kernel,
        out_shape=(
            jax.ShapeDtypeStruct((2 * NDATE * TILE, LANES), FLOAT),
            jax.ShapeDtypeStruct((TILE, LANES), FLOAT),
        ),
        in_specs=vmem(11),
        out_specs=(pl.BlockSpec(memory_space=pltpu.HBM), vmem(1)[0]),
        scratch_shapes=[
            pltpu.VMEM((BLOCKS, LANES, LANES), HALF_FLOAT),
            pltpu.VMEM((BLOCKS, LANES, LANES), HALF_FLOAT),
        ]
        + half_scratch
        + [
            pltpu.VMEM((8, LANES, LANES), FLOAT),
            pltpu.VMEM((BLOCKS, 64, LANES), FLOAT),
            pltpu.VMEM((BLOCKS, 128, 256), HALF_FLOAT),
            pltpu.VMEM((BLOCKS, 256, 256), HALF_FLOAT),
            pltpu.VMEM((TILE * LANES, LANES), FLOAT),
            pltpu.VMEM((2, TILE, LANES), FLOAT),
            pltpu.VMEM((2 * NDATE * TILE, LANES), FLOAT),
            pltpu.SemaphoreType.DMA((CHUNKS,)),
        ],
        compiler_params=pltpu.CompilerParams(vmem_limit_bytes=16 * 1024 * 1024),
        cost_estimate=pl.CostEstimate(
            flops=1_000_000_000, bytes_accessed=2_000_000, transcendentals=0
        ),
        name="link",
    )(*own[::-1], far_b, far_a, row_sub, row_lane, col_lane, near_z, near_y, picks, population)
    return linked.reshape(2, NDATE, TILE, LANES), eigen


def solution(mesh):
    in_specs = (P(None, "date", "row", None), P(), P(None, "row", "date"))
    out_specs = (P(None, None, "row", "date"), P("row", "date"))
    return jax.shard_map(
        on_device, mesh=mesh, in_specs=in_specs, out_specs=out_specs, check_vma=False
    )
```

```python
import functools

import jax
import jax.numpy as jnp
from jax import lax
from jax.experimental import pallas as pl
from jax.experimental.pallas import tpu as pltpu
from jax.sharding import PartitionSpec as P

NDATE = 32
SLOT_COLS = 9
EPSILON = 1e-06
LANES = 128
TILE = 8
GROUPS = 8
TAP_COUNT = 8
WINDOW_ROWS = 16
WINDOW_COLS = 136
BLOCKS = 16

FLOAT = jnp.float32
HALF_FLOAT = jnp.bfloat16


def lane_ids(shape):
    return lax.broadcasted_iota(jnp.int32, shape, len(shape) - 1)


def sublane_ids(shape):
    return lax.broadcasted_iota(jnp.int32, shape, len(shape) - 2)


def pack_blocks(slc_ref, send_ref):
    planes = slc_ref.shape[0]
    blocks = send_ref.shape[0]
    for block in range(blocks):
        for plane in range(planes):
            send_ref[block, pl.ds(plane, TILE, stride=planes), :] = slc_ref[
                plane, :, block * LANES : (block + 1) * LANES
            ]
    lanes = lane_ids((planes, LANES))
    rims = [jnp.zeros((planes, LANES), FLOAT) for _ in range(blocks)]
    for row in range(TILE):
        start = 16 * row
        turned = [
            pltpu.roll(
                send_ref[block, row * planes : (row + 1) * planes, :],
                (start + 8) % LANES,
                axis=1,
            )
            for block in range(blocks)
        ]
        left = (lanes >= start) & (lanes < start + 8)
        right = (lanes >= start + 8) & (lanes < start + 16)
        for block in range(blocks):
            if block > 0:
                rims[block] = jnp.where(left, turned[block - 1], rims[block])
            if block < blocks - 1:
                rims[block] = jnp.where(right, turned[block + 1], rims[block])
    for block in range(blocks):
        send_ref[block, TILE * planes : (TILE + 1) * planes, :] = rims[block]


def pack_pieces(slc_ref, *rest):
    pieces, blocks_ref = rest[:-1], rest[-1]
    pack_blocks(slc_ref, blocks_ref)
    here = lax.axis_index("date")
    for turn, piece_ref in enumerate(pieces):
        piece_ref[...] = blocks_ref[here ^ turn]


def join_kernel(turns, *rest):
    here = lax.axis_index("date")
    for turn, piece_ref in zip(turns, rest[:-1]):
        rest[-1][(here ^ turn) % 4] = piece_ref[...]


def tap_weight(distance):
    spread = jnp.abs(2 * distance - 1)
    return jnp.where(spread == 1, 0.5625, jnp.where(spread == 3, -0.0625, 0.0)).astype(FLOAT)


def prepare_kernel(
    offsets_ref, masks_ref, picks_ref, population_ref, row_sub_ref, row_lane_ref, col_lane_ref, words_ref
):
    words = masks_ref.shape[0]
    below = near_is_below()
    total = jnp.zeros((TILE, LANES), jnp.int32)
    for word in range(words):
        bits = masks_ref[word]
        bits = bits - (lax.shift_right_logical(bits, 1) & 0x55555555)
        bits = (bits & 0x33333333) + (lax.shift_right_logical(bits, 2) & 0x33333333)
        bits = (bits + lax.shift_right_logical(bits, 4)) & 0x0F0F0F0F
        bits = bits + lax.shift_right_logical(bits, 8)
        bits = bits + lax.shift_right_logical(bits, 16)
        total = total + (bits & 0xFF)
    population_ref[...] = total.astype(FLOAT)

    lanes = lane_ids((TILE, LANES))
    subs = sublane_ids((TILE, LANES))
    lane_dates = ((lanes % 64) // 8) * 4 + lanes % 4
    row_shift = jnp.zeros((TILE, LANES), jnp.int32)
    col_shift = jnp.zeros((TILE, LANES), jnp.int32)
    for date in range(NDATE):
        here = lane_dates == date
        row_shift = jnp.where(here, offsets_ref[0, date], row_shift)
        col_shift = jnp.where(here, offsets_ref[1, date], col_shift)
    for tap in range(TAP_COUNT):
        row_lane_ref[tap] = tap_weight(tap - 3 - row_shift)
        col_lane_ref[tap] = tap_weight(tap - 3 - col_shift)
    for group in range(GROUPS):
        shift = jnp.zeros((TILE, LANES), jnp.int32)
        for date in range(4):
            shift = jnp.where(subs % 4 == date, offsets_ref[0, 4 * group + date], shift)
        for tap in range(TAP_COUNT):
            row_sub_ref[tap, group * TILE : (group + 1) * TILE, :] = tap_weight(tap - 3 - shift)

    flat = [masks_ref[word] for word in range(words)]
    flat = flat + [jnp.zeros((TILE, LANES), jnp.int32)] * (LANES // TILE - words)
    words_ref[...] = jnp.transpose(jnp.concatenate(flat, axis=0))

    def one_block(block, carry):
        packed = words_ref[pl.ds(pl.multiple_of(block * TILE, TILE), TILE), :]
        for row_pair in range(TILE // 2):
            spread = [[], []]
            for row in (2 * row_pair, 2 * row_pair + 1):
                row_words = [
                    jnp.broadcast_to(
                        packed[:, word * TILE + row : word * TILE + row + 1], (TILE, LANES)
                    )
                    for word in range(words)
                ]
                for half in range(2):
                    near = 8 * half + lanes // 16 - row
                    across = lanes % 16 - subs
                    inside = (near >= 0) & (near <= 8) & (across >= 0) & (across <= 8)
                    amount = jnp.where(inside, (near & 1) * SLOT_COLS + across, 31)
                    first = max(0, 8 * half - row) // 2
                    last = min(8, 8 * half + 7 - row) // 2
                    chosen = row_words[first]
                    for word in range(first + 1, last + 1):
                        chosen = jnp.where(near >= 2 * word, row_words[word], chosen)
                    bits = lax.shift_right_logical(chosen, amount) & 1
                    spread[half].append(bits.astype(FLOAT))
            low_half, high_half = [jnp.concatenate(half, axis=0) for half in spread]
            rows = slice(16 * row_pair, 16 * row_pair + 16)
            picks_ref[block, rows, :LANES] = jnp.where(below, high_half, low_half).astype(HALF_FLOAT)
            picks_ref[block, rows, LANES:] = jnp.where(below, low_half, high_half).astype(HALF_FLOAT)
        return carry

    lax.fori_loop(0, BLOCKS, one_block, 0)


def split_halves(values):
    high = values.astype(HALF_FLOAT)
    low = values - high.astype(FLOAT)
    return high, low


def dot(a, b, contract):
    return lax.dot_general(
        a, b, (((contract[0],), (contract[1],)), ((), ())), preferred_element_type=FLOAT
    )


def packed_rims(base, refs):
    halves = [ref[:, 8 * TILE : 9 * TILE, :].reshape(32, LANES) for ref in refs]
    return jnp.where(
        base == 0, jnp.concatenate(halves, axis=0), jnp.concatenate(halves[::-1], axis=0)
    )


def first_group():
    return (lax.axis_index("date") ^ 4) & 4 if lax.axis_size("date") == GROUPS else 0


def near_is_below():
    return (lax.axis_index("row") + lax.axis_index("date")) % 2 == 0


def resample_rows(
    base,
    own_refs,
    other_refs,
    below,
    row_sub_ref,
    row_lane_ref,
    mixed_ref,
    rims_ref,
    turned_ref,
):
    row_at, row_count = lax.axis_index("row"), lax.axis_size("row")

    exists = (below & (row_at < row_count - 1)) | (jnp.logical_not(below) & (row_at > 0))

    def mix_group(own_ref, other_ref, base, slot):
        group = base + slot
        weights = [
            row_sub_ref[tap, pl.ds(pl.multiple_of(group * TILE, TILE), TILE), :]
            for tap in range(TAP_COUNT)
        ]
        own = [own_ref[slot, row * TILE : (row + 1) * TILE, :] for row in range(TILE)]
        other = [
            jnp.where(exists, other_ref[slot, row * TILE : (row + 1) * TILE, :], 0.0)
            for row in range(TILE)
        ]
        raw = [jnp.where(below, a, b) for a, b in zip(own, other)]
        raw = raw + [jnp.where(below, b, a) for a, b in zip(own, other)]
        for row in range(8):
            mixed = weights[0] * raw[row + 1]
            for tap in range(1, TAP_COUNT):
                mixed = mixed + weights[tap] * raw[row + 1 + tap]
            start = pl.multiple_of((row // 4) * 64 + group * TILE, TILE)
            mixed_ref[row % 4, pl.ds(start, TILE), :] = mixed

    def mix_slot(slot, carry):
        mix_group(own_refs[0], other_refs[0], base, slot)
        mix_group(own_refs[1], other_refs[1], 4 - base, slot)
        return carry

    lax.fori_loop(0, GROUPS // 2, mix_slot, 0)

    lanes = lane_ids((1, LANES))
    lower = lanes < 64
    own, other = [packed_rims(base, refs) for refs in (own_refs, other_refs)]
    other = jnp.where(exists, other, 0.0)
    first, second = jnp.where(below, own, other), jnp.where(below, other, own)
    far_first, far_second = pltpu.roll(first, 64, axis=1), pltpu.roll(second, 64, axis=1)
    rims_ref[0:LANES, :] = jnp.transpose(
        jnp.concatenate([first, jnp.where(lower, far_first, far_second)], axis=0)
    )
    rims_ref[LANES : 2 * LANES, :] = jnp.transpose(jnp.concatenate([second, far_second], axis=0))
    row_weights = [row_lane_ref[tap, 0:1, :] for tap in range(TAP_COUNT)]
    for row in range(4):
        turned_ref[row, 8 : 8 + LANES, :] = jnp.transpose(mixed_ref[row])
        rim = row_weights[0] * rims_ref[(row + 1) * 16 : (row + 2) * 16, :]
        for tap in range(1, TAP_COUNT):
            rim = rim + row_weights[tap] * rims_ref[(row + 1 + tap) * 16 : (row + 2 + tap) * 16, :]
        turned_ref[row, 0:8, :] = rim[0:8]
        turned_ref[row, 8 + LANES : 16 + LANES, :] = rim[8:16]


def resample_columns(below, col_lane_ref, z_ref, y_ref, turned_ref, first, count):
    row_at, row_count = lax.axis_index("row"), lax.axis_size("row")
    col_at, col_count = lax.axis_index("date"), lax.axis_size("date")
    lanes = lane_ids((1, LANES))
    lower = lanes < 64
    width = count * 8 + 8
    places = sublane_ids((width, LANES)) + first * 8
    inside = ((places >= 4) | (col_at > 0)) & ((places < 132) | (col_at < col_count - 1))
    row_inside = (lower & (below | (row_at > 0))) | (
        (lanes >= 64) & (jnp.logical_not(below) | (row_at < row_count - 1))
    )
    inside = inside & row_inside
    term = lax.broadcasted_iota(jnp.int32, (2 * LANES, 2 * LANES), 0) % LANES
    gives = lax.broadcasted_iota(jnp.int32, (2 * LANES, 2 * LANES), 1)
    same_part = ((term % 8) < 4) == (gives < LANES)
    sums = jnp.where(((term < 64) == ((gives % LANES) < 64)) & same_part, 1.0, 0.0).astype(HALF_FLOAT)

    def store_windows(target, row, values):
        high, low = split_halves(values)
        high = high.astype(FLOAT)
        rows = (
            jnp.where(lower, high, pltpu.roll(low, 64, axis=1)),
            jnp.where(lower, pltpu.roll(high, 64, axis=1), low),
        )
        for part in range(2):
            start = (row + 4 * part) * 16
            for block in range(count):
                target[first + block, start : start + 16, :] = rows[part][
                    block * 8 : block * 8 + 16
                ].astype(HALF_FLOAT)

    for row in range(4):
        begin = 1 + first * 8
        mixed = col_lane_ref[0, 0:1, :] * turned_ref[row, begin : begin + width, :]
        for tap in range(1, TAP_COUNT):
            mixed = mixed + col_lane_ref[tap, 0:1, :] * turned_ref[
                row, begin + tap : begin + tap + width, :
            ]
        z = jnp.where(inside, mixed, 0.0)
        high, low = split_halves(z)
        total = dot(jnp.concatenate([high, low.astype(HALF_FLOAT)], axis=1), sums, (1, 0))
        y = z * total[:, :LANES] + swapped(z) * total[:, LANES:]
        store_windows(z_ref, row, z)
        store_windows(y_ref, row, y)


def swapped(values):
    real = (lane_ids((1, LANES)) % 8) < 4
    return jnp.where(real, pltpu.roll(values, LANES - 4, axis=1), -pltpu.roll(values, 4, axis=1))


def near_kernel(
    own_b,
    own_a,
    near_b,
    near_a,
    row_sub_ref,
    row_lane_ref,
    col_lane_ref,
    z_ref,
    y_ref,
    mixed_ref,
    rims_ref,
    turned_ref,
):
    below = near_is_below()
    resample_rows(
        first_group(),
        (own_a, own_b),
        (near_a, near_b),
        below,
        row_sub_ref,
        row_lane_ref,
        mixed_ref,
        rims_ref,
        turned_ref,
    )
    resample_columns(below, col_lane_ref, z_ref, y_ref, turned_ref, 0, BLOCKS)


def link_kernel(
    own_b,
    own_a,
    far_b,
    far_a,
    row_sub_ref,
    row_lane_ref,
    col_lane_ref,
    near_z_ref,
    near_y_ref,
    picks_ref,
    population_ref,
    linked_ref,
    eigen_ref,
    far_z_ref,
    far_y_ref,
    mixed_ref,
    rims_ref,
    turned_ref,
    result_ref,
    first_ref,
    vectors_ref,
    chosen_ref,
):
    below = jnp.logical_not(near_is_below())
    resample_rows(
        first_group(),
        (own_a, own_b),
        (far_a, far_b),
        below,
        row_sub_ref,
        row_lane_ref,
        mixed_ref,
        rims_ref,
        turned_ref,
    )
    lower = lane_ids((1, LANES)) < 64

    def columns(first, count):
        resample_columns(below, col_lane_ref, far_z_ref, far_y_ref, turned_ref, first, count)

    def first_phase(first, count):
        for block in range(first, first + count):
            y = jnp.concatenate([near_y_ref[block], far_y_ref[block]], axis=0)
            vector = dot(picks_ref[block], y, (1, 0))
            vector = vector + pltpu.roll(vector, 64, axis=1)
            high, low = split_halves(jnp.concatenate([vector, swapped(vector)], axis=0))
            first_ref[block] = vector
            vectors_ref[block, :, :LANES] = high
            vectors_ref[block, :, LANES:] = low.astype(HALF_FLOAT)

    def inner_phase(first, count):
        for block in range(first, first + count):
            z = jnp.concatenate([near_z_ref[block], far_z_ref[block]], axis=0)
            inner = dot(vectors_ref[block], jnp.concatenate([z, z], axis=1), (1, 1))
            high, low = split_halves(inner)
            picks = picks_ref[block]
            picks = jnp.concatenate([picks, picks], axis=0)
            chosen_ref[block, :128, :] = high * picks
            chosen_ref[block, 128:, :] = low.astype(HALF_FLOAT) * picks

    def outer_phase(first, count):
        for block in range(first, first + count):
            z = jnp.concatenate([near_z_ref[block], far_z_ref[block]], axis=0)
            outer = dot(chosen_ref[block], z, (1, 0))
            outer = outer[:128] + outer[128:]
            outer = outer + pltpu.roll(outer, 64, axis=1)
            second = outer[:64] - swapped(outer[64:])
            both = jnp.where(lower, second, first_ref[block])
            for row in range(8):
                result_ref[row, block * 8 : block * 8 + 8, :] = both[row * 8 : row * 8 + 8]

    half = BLOCKS // 2
    columns(0, half)
    first_phase(0, half)
    columns(half, half)
    inner_phase(0, half)
    first_phase(half, half)
    outer_phase(0, half)
    inner_phase(half, half)
    outer_phase(half, half)

    inverse = 1.0 / population_ref[...]
    for row in range(8):
        turned = jnp.transpose(result_ref[row])
        second, first = turned[:64], turned[64:]
        scale = inverse[row : row + 1]
        square = scale * scale
        norm_first = jnp.sqrt(jnp.sum(first * first, axis=0, keepdims=True) * square + EPSILON)
        norm_last = jnp.sqrt(
            jnp.sum(second * second, axis=0, keepdims=True) * (square * square) + EPSILON
        )
        eigen_ref[row : row + 1, :] = norm_last / norm_first
        linked = second * (square * (jnp.sqrt(jnp.float32(NDATE)) / norm_last))
        for group in range(GROUPS):
            for part in range(2):
                begin = ((part * NDATE + 4 * group) * 8) + row
                at = group * 8 + part * 4
                linked_ref[pl.ds(begin, 4, stride=8), :] = linked[at : at + 4]


def canonical(received, dates_dev):
    sources = received.shape[0]
    if dates_dev == 4:
        return received
    cells = received.reshape(sources, 9, 2, dates_dev, LANES)
    cells = jnp.transpose(cells, (1, 2, 0, 3, 4)).reshape(9, 2, GROUPS, 4, LANES)
    return jnp.transpose(cells, (2, 0, 1, 3, 4)).reshape(GROUPS, 9 * TILE, LANES)


def partner(date, row, turn, rows_count):
    other = row + 1 if (row + date + turn) % 2 == 0 else row - 1
    if 0 <= other < rows_count:
        return date * rows_count + other
    return (date ^ 2) * rows_count + row


def vmem(count):
    return [pl.BlockSpec(memory_space=pltpu.VMEM)] * count


def on_device(slc, offsets, masks):
    dates_dev = slc.shape[1]
    rows_dev = slc.shape[2]
    cols_all = slc.shape[3]
    rows_count = lax.axis_size("row")
    cols_count = lax.axis_size("date")
    planes_dev = 2 * dates_dev
    assert rows_dev == TILE and cols_all == cols_count * LANES

    small = pltpu.CompilerParams(vmem_limit_bytes=4 * 1024 * 1024)
    images = slc.reshape(planes_dev, rows_dev, cols_all)
    moves = pl.CostEstimate(flops=0, bytes_accessed=600_000, transcendentals=0)
    half_shape = jax.ShapeDtypeStruct((GROUPS // 2, 9 * TILE, LANES), FLOAT)

    def swap_rows(cells, turn):
        return lax.ppermute(
            cells,
            ("date", "row"),
            [
                (date * rows_count + row, partner(date, row, turn, rows_count))
                for date in range(cols_count)
                for row in range(rows_count)
            ],
        )

    if cols_count == GROUPS:
        pieces = pl.pallas_call(
            pack_pieces,
            out_shape=[jax.ShapeDtypeStruct((9 * TILE, LANES), FLOAT)] * GROUPS,
            in_specs=vmem(1),
            out_specs=vmem(GROUPS),
            scratch_shapes=[pltpu.VMEM((GROUPS, 9 * TILE, LANES), FLOAT)],
            compiler_params=small,
            cost_estimate=moves,
            name="pack",
        )(images)
        pieces = list(pieces[:1]) + [
            lax.ppermute(pieces[turn], "date", [(i, i ^ turn) for i in range(GROUPS)])
            for turn in range(1, GROUPS)
        ]
        own = [
            pl.pallas_call(
                functools.partial(join_kernel, turns),
                out_shape=half_shape,
                in_specs=vmem(4),
                out_specs=vmem(1)[0],
                compiler_params=small,
                cost_estimate=moves,
                name="join",
            )(*[pieces[turn] for turn in turns])
            for turns in ((6, 7, 4, 5), (2, 3, 1, 0))
        ]
    else:
        outgoing = pl.pallas_call(
            pack_blocks,
            out_shape=jax.ShapeDtypeStruct((cols_count, 9 * planes_dev, LANES), FLOAT),
            in_specs=vmem(1),
            out_specs=vmem(1)[0],
            compiler_params=small,
            cost_estimate=moves,
            name="pack",
        )(images)
        received = lax.all_to_all(outgoing, "date", split_axis=0, concat_axis=0, tiled=True)
        received = canonical(received, dates_dev)
        own = [received[: GROUPS // 2], received[GROUPS // 2 :]]
    near_a, far_a, near_b, far_b = [swap_rows(half, turn) for half in own for turn in range(2)]

    picks, population, row_sub, row_lane, col_lane = pl.pallas_call(
        prepare_kernel,
        out_shape=(
            jax.ShapeDtypeStruct((BLOCKS, 64, 256), HALF_FLOAT),
            jax.ShapeDtypeStruct((TILE, LANES), FLOAT),
            jax.ShapeDtypeStruct((TAP_COUNT, 64, LANES), FLOAT),
            jax.ShapeDtypeStruct((TAP_COUNT, TILE, LANES), FLOAT),
            jax.ShapeDtypeStruct((TAP_COUNT, TILE, LANES), FLOAT),
        ),
        in_specs=[pl.BlockSpec(memory_space=pltpu.SMEM)] + vmem(1),
        out_specs=tuple(vmem(5)),
        scratch_shapes=[pltpu.VMEM((LANES, LANES), jnp.int32)],
        compiler_params=small,
        cost_estimate=pl.CostEstimate(flops=4_000_000, bytes_accessed=1_000_000, transcendentals=0),
        name="prepare",
    )(offsets, masks)

    half_scratch = [
        pltpu.VMEM((4, LANES, LANES), FLOAT),
        pltpu.VMEM((2 * LANES, LANES), FLOAT),
        pltpu.VMEM((4, LANES + 16, LANES), FLOAT),
    ]
    windows = jax.ShapeDtypeStruct((BLOCKS, LANES, LANES), HALF_FLOAT)
    near_z, near_y = pl.pallas_call(
        near_kernel,
        out_shape=(windows, windows),
        in_specs=vmem(7),
        out_specs=tuple(vmem(2)),
        scratch_shapes=half_scratch,
        compiler_params=small,
        cost_estimate=pl.CostEstimate(
            flops=200_000_000, bytes_accessed=2_000_000, transcendentals=0
        ),
        name="near",
    )(*own[::-1], near_b, near_a, row_sub, row_lane, col_lane)
    linked, eigen = pl.pallas_call(
        link_kernel,
        out_shape=(
            jax.ShapeDtypeStruct((2 * NDATE * TILE, LANES), FLOAT),
            jax.ShapeDtypeStruct((TILE, LANES), FLOAT),
        ),
        in_specs=vmem(11),
        out_specs=tuple(vmem(2)),
        scratch_shapes=[
            pltpu.VMEM((BLOCKS, LANES, LANES), HALF_FLOAT),
            pltpu.VMEM((BLOCKS, LANES, LANES), HALF_FLOAT),
        ]
        + half_scratch
        + [
            pltpu.VMEM((8, LANES, LANES), FLOAT),
            pltpu.VMEM((BLOCKS, 64, LANES), FLOAT),
            pltpu.VMEM((BLOCKS, 128, 256), HALF_FLOAT),
            pltpu.VMEM((BLOCKS, 256, 256), HALF_FLOAT),
        ],
        compiler_params=pltpu.CompilerParams(vmem_limit_bytes=16 * 1024 * 1024),
        cost_estimate=pl.CostEstimate(
            flops=1_000_000_000, bytes_accessed=2_000_000, transcendentals=0
        ),
        name="link",
    )(*own[::-1], far_b, far_a, row_sub, row_lane, col_lane, near_z, near_y, picks, population)
    return linked.reshape(2, NDATE, TILE, LANES), eigen


def solution(mesh):
    in_specs = (P(None, "date", "row", None), P(), P(None, "row", "date"))
    out_specs = (P(None, None, "row", "date"), P("row", "date"))
    return jax.shard_map(
        on_device, mesh=mesh, in_specs=in_specs, out_specs=out_specs, check_vma=False
    )
```

```python
import functools

import jax
import jax.numpy as jnp
from jax import lax
from jax.experimental import pallas as pl
from jax.experimental.pallas import tpu as pltpu
from jax.sharding import PartitionSpec as P

NDATE = 32
SLOT_COLS = 9
EPSILON = 1e-06
LANES = 128
TILE = 8
GROUPS = 8
TAP_COUNT = 8
WINDOW_ROWS = 16
WINDOW_COLS = 136
BLOCKS = 16

FLOAT = jnp.float32
HALF_FLOAT = jnp.bfloat16


def lane_ids(shape):
    return lax.broadcasted_iota(jnp.int32, shape, len(shape) - 1)


def sublane_ids(shape):
    return lax.broadcasted_iota(jnp.int32, shape, len(shape) - 2)


def pack_blocks(slc_ref, send_ref):
    planes = slc_ref.shape[0]
    blocks = send_ref.shape[0]
    for block in range(blocks):
        for plane in range(planes):
            send_ref[block, pl.ds(plane, TILE, stride=planes), :] = slc_ref[
                plane, :, block * LANES : (block + 1) * LANES
            ]
    lanes = lane_ids((planes, LANES))
    rims = [jnp.zeros((planes, LANES), FLOAT) for _ in range(blocks)]
    for row in range(TILE):
        start = 16 * row
        turned = [
            pltpu.roll(
                send_ref[block, row * planes : (row + 1) * planes, :],
                (start + 8) % LANES,
                axis=1,
            )
            for block in range(blocks)
        ]
        left = (lanes >= start) & (lanes < start + 8)
        right = (lanes >= start + 8) & (lanes < start + 16)
        for block in range(blocks):
            if block > 0:
                rims[block] = jnp.where(left, turned[block - 1], rims[block])
            if block < blocks - 1:
                rims[block] = jnp.where(right, turned[block + 1], rims[block])
    for block in range(blocks):
        send_ref[block, TILE * planes : (TILE + 1) * planes, :] = rims[block]


def pack_pieces(slc_ref, *rest):
    pieces, blocks_ref = rest[:-1], rest[-1]
    pack_blocks(slc_ref, blocks_ref)
    here = lax.axis_index("date")
    for turn, piece_ref in enumerate(pieces):
        piece_ref[...] = blocks_ref[here ^ turn]


def join_kernel(turns, *rest):
    here = lax.axis_index("date")
    for turn, piece_ref in zip(turns, rest[:-1]):
        rest[-1][(here ^ turn) % 4] = piece_ref[...]


def tap_weight(distance):
    spread = jnp.abs(2 * distance - 1)
    return jnp.where(spread == 1, 0.5625, jnp.where(spread == 3, -0.0625, 0.0)).astype(FLOAT)


def prepare_kernel(
    offsets_ref, masks_ref, picks_ref, population_ref, row_sub_ref, row_lane_ref, col_lane_ref, words_ref
):
    words = masks_ref.shape[0]
    below = near_is_below()
    total = jnp.zeros((TILE, LANES), jnp.int32)
    for word in range(words):
        bits = masks_ref[word]
        bits = bits - (lax.shift_right_logical(bits, 1) & 0x55555555)
        bits = (bits & 0x33333333) + (lax.shift_right_logical(bits, 2) & 0x33333333)
        bits = (bits + lax.shift_right_logical(bits, 4)) & 0x0F0F0F0F
        bits = bits + lax.shift_right_logical(bits, 8)
        bits = bits + lax.shift_right_logical(bits, 16)
        total = total + (bits & 0xFF)
    population_ref[...] = total.astype(FLOAT)

    lanes = lane_ids((TILE, LANES))
    subs = sublane_ids((TILE, LANES))
    lane_dates = ((lanes % 64) // 8) * 4 + lanes % 4
    row_shift = jnp.zeros((TILE, LANES), jnp.int32)
    col_shift = jnp.zeros((TILE, LANES), jnp.int32)
    for date in range(NDATE):
        here = lane_dates == date
        row_shift = jnp.where(here, offsets_ref[0, date], row_shift)
        col_shift = jnp.where(here, offsets_ref[1, date], col_shift)
    for tap in range(TAP_COUNT):
        row_lane_ref[tap] = tap_weight(tap - 3 - row_shift)
        col_lane_ref[tap] = tap_weight(tap - 3 - col_shift)
    for group in range(GROUPS):
        shift = jnp.zeros((TILE, LANES), jnp.int32)
        for date in range(4):
            shift = jnp.where(subs % 4 == date, offsets_ref[0, 4 * group + date], shift)
        for tap in range(TAP_COUNT):
            row_sub_ref[tap, group * TILE : (group + 1) * TILE, :] = tap_weight(tap - 3 - shift)

    flat = [masks_ref[word] for word in range(words)]
    flat = flat + [jnp.zeros((TILE, LANES), jnp.int32)] * (LANES // TILE - words)
    words_ref[...] = jnp.transpose(jnp.concatenate(flat, axis=0))

    def one_block(block, carry):
        packed = words_ref[pl.ds(pl.multiple_of(block * TILE, TILE), TILE), :]
        for row_pair in range(TILE // 2):
            spread = [[], []]
            for row in (2 * row_pair, 2 * row_pair + 1):
                row_words = [
                    jnp.broadcast_to(
                        packed[:, word * TILE + row : word * TILE + row + 1], (TILE, LANES)
                    )
                    for word in range(words)
                ]
                for half in range(2):
                    near = 8 * half + lanes // 16 - row
                    across = lanes % 16 - subs
                    inside = (near >= 0) & (near <= 8) & (across >= 0) & (across <= 8)
                    amount = jnp.where(inside, (near & 1) * SLOT_COLS + across, 31)
                    first = max(0, 8 * half - row) // 2
                    last = min(8, 8 * half + 7 - row) // 2
                    chosen = row_words[first]
                    for word in range(first + 1, last + 1):
                        chosen = jnp.where(near >= 2 * word, row_words[word], chosen)
                    bits = lax.shift_right_logical(chosen, amount) & 1
                    spread[half].append(bits.astype(FLOAT))
            low_half, high_half = [jnp.concatenate(half, axis=0) for half in spread]
            rows = slice(16 * row_pair, 16 * row_pair + 16)
            picks_ref[block, rows, :LANES] = jnp.where(below, high_half, low_half).astype(HALF_FLOAT)
            picks_ref[block, rows, LANES:] = jnp.where(below, low_half, high_half).astype(HALF_FLOAT)
        return carry

    lax.fori_loop(0, BLOCKS, one_block, 0)


def split_halves(values):
    high = values.astype(HALF_FLOAT)
    low = values - high.astype(FLOAT)
    return high, low


def dot(a, b, contract):
    return lax.dot_general(
        a, b, (((contract[0],), (contract[1],)), ((), ())), preferred_element_type=FLOAT
    )


def packed_rims(base, refs):
    halves = [ref[:, 8 * TILE : 9 * TILE, :].reshape(32, LANES) for ref in refs]
    return jnp.where(
        base == 0, jnp.concatenate(halves, axis=0), jnp.concatenate(halves[::-1], axis=0)
    )


def first_group():
    return (lax.axis_index("date") ^ 4) & 4 if lax.axis_size("date") == GROUPS else 0


def near_is_below():
    return (lax.axis_index("row") + lax.axis_index("date")) % 2 == 0


def resample_rows(
    base,
    own_refs,
    other_refs,
    below,
    row_sub_ref,
    row_lane_ref,
    mixed_ref,
    rims_ref,
    turned_ref,
):
    row_at, row_count = lax.axis_index("row"), lax.axis_size("row")

    exists = exists_at(below)

    def mix_group(own_ref, other_ref, base, slot):
        group = base + slot
        weights = [
            row_sub_ref[tap, pl.ds(pl.multiple_of(group * TILE, TILE), TILE), :]
            for tap in range(TAP_COUNT)
        ]
        own = [own_ref[slot, row * TILE : (row + 1) * TILE, :] for row in range(TILE)]
        other = [
            jnp.where(exists, other_ref[slot, row * TILE : (row + 1) * TILE, :], 0.0)
            for row in range(TILE)
        ]
        raw = [jnp.where(below, a, b) for a, b in zip(own, other)]
        raw = raw + [jnp.where(below, b, a) for a, b in zip(own, other)]
        for row in range(8):
            mixed = weights[0] * raw[row + 1]
            for tap in range(1, TAP_COUNT):
                mixed = mixed + weights[tap] * raw[row + 1 + tap]
            start = pl.multiple_of((row // 4) * 64 + group * TILE, TILE)
            mixed_ref[row % 4, pl.ds(start, TILE), :] = mixed

    def mix_slot(slot, carry):
        mix_group(own_refs[0], other_refs[0], base, slot)
        mix_group(own_refs[1], other_refs[1], 4 - base, slot)
        return carry

    lax.fori_loop(0, GROUPS // 2, mix_slot, 0)

    lanes = lane_ids((1, LANES))
    lower = lanes < 64
    own, other = [packed_rims(base, refs) for refs in (own_refs, other_refs)]
    other = jnp.where(exists, other, 0.0)
    first, second = jnp.where(below, own, other), jnp.where(below, other, own)
    far_first, far_second = pltpu.roll(first, 64, axis=1), pltpu.roll(second, 64, axis=1)
    rims_ref[0:LANES, :] = jnp.transpose(
        jnp.concatenate([first, jnp.where(lower, far_first, far_second)], axis=0)
    )
    rims_ref[LANES : 2 * LANES, :] = jnp.transpose(jnp.concatenate([second, far_second], axis=0))
    row_weights = [row_lane_ref[tap, 0:1, :] for tap in range(TAP_COUNT)]
    for row in range(4):
        turned_ref[row, 8 : 8 + LANES, :] = jnp.transpose(mixed_ref[row])
        rim = row_weights[0] * rims_ref[(row + 1) * 16 : (row + 2) * 16, :]
        for tap in range(1, TAP_COUNT):
            rim = rim + row_weights[tap] * rims_ref[(row + 1 + tap) * 16 : (row + 2 + tap) * 16, :]
        turned_ref[row, 0:8, :] = rim[0:8]
        turned_ref[row, 8 + LANES : 16 + LANES, :] = rim[8:16]


def resample_columns(below, col_lane_ref, z_ref, y_ref, turned_ref, first, count):
    row_at, row_count = lax.axis_index("row"), lax.axis_size("row")
    col_at, col_count = lax.axis_index("date"), lax.axis_size("date")
    lanes = lane_ids((1, LANES))
    lower = lanes < 64
    width = count * 8 + 8
    places = sublane_ids((width, LANES)) + first * 8
    inside = ((places >= 4) | (col_at > 0)) & ((places < 132) | (col_at < col_count - 1))
    row_inside = (lower & (below | (row_at > 0))) | (
        (lanes >= 64) & (jnp.logical_not(below) | (row_at < row_count - 1))
    )
    inside = inside & row_inside
    term = lax.broadcasted_iota(jnp.int32, (2 * LANES, 2 * LANES), 0) % LANES
    gives = lax.broadcasted_iota(jnp.int32, (2 * LANES, 2 * LANES), 1)
    same_part = ((term % 8) < 4) == (gives < LANES)
    sums = jnp.where(((term < 64) == ((gives % LANES) < 64)) & same_part, 1.0, 0.0).astype(HALF_FLOAT)

    def store_windows(target, row, values):
        high, low = split_halves(values)
        high = high.astype(FLOAT)
        rows = (
            jnp.where(lower, high, pltpu.roll(low, 64, axis=1)),
            jnp.where(lower, pltpu.roll(high, 64, axis=1), low),
        )
        for part in range(2):
            start = (row + 4 * part) * 16
            for block in range(count):
                target[first + block, start : start + 16, :] = rows[part][
                    block * 8 : block * 8 + 16
                ].astype(HALF_FLOAT)

    for row in range(4):
        begin = 1 + first * 8
        mixed = col_lane_ref[0, 0:1, :] * turned_ref[row, begin : begin + width, :]
        for tap in range(1, TAP_COUNT):
            mixed = mixed + col_lane_ref[tap, 0:1, :] * turned_ref[
                row, begin + tap : begin + tap + width, :
            ]
        z = jnp.where(inside, mixed, 0.0)
        high, low = split_halves(z)
        total = dot(jnp.concatenate([high, low.astype(HALF_FLOAT)], axis=1), sums, (1, 0))
        y = z * total[:, :LANES] + swapped(z) * total[:, LANES:]
        store_windows(z_ref, row, z)
        store_windows(y_ref, row, y)


def swapped(values):
    real = (lane_ids((1, LANES)) % 8) < 4
    return jnp.where(real, pltpu.roll(values, LANES - 4, axis=1), -pltpu.roll(values, 4, axis=1))


def exists_at(below):
    row_at, row_count = lax.axis_index("row"), lax.axis_size("row")
    return (below & (row_at < row_count - 1)) | (jnp.logical_not(below) & (row_at > 0))


def screen_kernel(near_ref, far_ref, near_out_ref, far_out_ref):
    below = near_is_below()
    near_out_ref[...] = jnp.where(exists_at(below), near_ref[...], 0.0)
    far_out_ref[...] = jnp.where(exists_at(jnp.logical_not(below)), far_ref[...], 0.0)


def near_kernel(
    own_b,
    own_a,
    near_b,
    near_a,
    row_sub_ref,
    row_lane_ref,
    col_lane_ref,
    z_ref,
    y_ref,
    mixed_ref,
    rims_ref,
    turned_ref,
):
    below = near_is_below()
    resample_rows(
        first_group(),
        (own_a, own_b),
        (near_a, near_b),
        below,
        row_sub_ref,
        row_lane_ref,
        mixed_ref,
        rims_ref,
        turned_ref,
    )
    resample_columns(below, col_lane_ref, z_ref, y_ref, turned_ref, 0, BLOCKS)


def link_kernel(
    own_b,
    own_a,
    far_b,
    far_a,
    row_sub_ref,
    row_lane_ref,
    col_lane_ref,
    near_z_ref,
    near_y_ref,
    picks_ref,
    population_ref,
    linked_ref,
    eigen_ref,
    far_z_ref,
    far_y_ref,
    mixed_ref,
    rims_ref,
    turned_ref,
    result_ref,
    first_ref,
    vectors_ref,
    chosen_ref,
):
    below = jnp.logical_not(near_is_below())
    resample_rows(
        first_group(),
        (own_a, own_b),
        (far_a, far_b),
        below,
        row_sub_ref,
        row_lane_ref,
        mixed_ref,
        rims_ref,
        turned_ref,
    )
    lower = lane_ids((1, LANES)) < 64

    def columns(first, count):
        resample_columns(below, col_lane_ref, far_z_ref, far_y_ref, turned_ref, first, count)

    def first_phase(first, count):
        for block in range(first, first + count):
            y = jnp.concatenate([near_y_ref[block], far_y_ref[block]], axis=0)
            vector = dot(picks_ref[block], y, (1, 0))
            vector = vector + pltpu.roll(vector, 64, axis=1)
            high, low = split_halves(jnp.concatenate([vector, swapped(vector)], axis=0))
            first_ref[block] = vector
            vectors_ref[block, :, :LANES] = high
            vectors_ref[block, :, LANES:] = low.astype(HALF_FLOAT)

    def inner_phase(first, count):
        for block in range(first, first + count):
            z = jnp.concatenate([near_z_ref[block], far_z_ref[block]], axis=0)
            inner = dot(vectors_ref[block], jnp.concatenate([z, z], axis=1), (1, 1))
            high, low = split_halves(inner)
            picks = picks_ref[block]
            picks = jnp.concatenate([picks, picks], axis=0)
            chosen_ref[block, :128, :] = high * picks
            chosen_ref[block, 128:, :] = low.astype(HALF_FLOAT) * picks

    def outer_phase(first, count):
        for block in range(first, first + count):
            z = jnp.concatenate([near_z_ref[block], far_z_ref[block]], axis=0)
            outer = dot(chosen_ref[block], z, (1, 0))
            outer = outer[:128] + outer[128:]
            outer = outer + pltpu.roll(outer, 64, axis=1)
            second = outer[:64] - swapped(outer[64:])
            both = jnp.where(lower, second, first_ref[block])
            for row in range(8):
                result_ref[row, block * 8 : block * 8 + 8, :] = both[row * 8 : row * 8 + 8]

    half = BLOCKS // 2
    columns(0, half)
    first_phase(0, half)
    columns(half, half)
    inner_phase(0, half)
    first_phase(half, half)
    outer_phase(0, half)
    inner_phase(half, half)
    outer_phase(half, half)

    inverse = 1.0 / population_ref[...]
    for row in range(8):
        turned = jnp.transpose(result_ref[row])
        second, first = turned[:64], turned[64:]
        scale = inverse[row : row + 1]
        square = scale * scale
        norm_first = jnp.sqrt(jnp.sum(first * first, axis=0, keepdims=True) * square + EPSILON)
        norm_last = jnp.sqrt(
            jnp.sum(second * second, axis=0, keepdims=True) * (square * square) + EPSILON
        )
        eigen_ref[row : row + 1, :] = norm_last / norm_first
        linked = second * (square * (jnp.sqrt(jnp.float32(NDATE)) / norm_last))
        for group in range(GROUPS):
            for part in range(2):
                begin = ((part * NDATE + 4 * group) * 8) + row
                at = group * 8 + part * 4
                linked_ref[pl.ds(begin, 4, stride=8), :] = linked[at : at + 4]


def canonical(received, dates_dev):
    sources = received.shape[0]
    if dates_dev == 4:
        return received
    cells = received.reshape(sources, 9, 2, dates_dev, LANES)
    cells = jnp.transpose(cells, (1, 2, 0, 3, 4)).reshape(9, 2, GROUPS, 4, LANES)
    return jnp.transpose(cells, (2, 0, 1, 3, 4)).reshape(GROUPS, 9 * TILE, LANES)


def partner(date, row, turn, rows_count):
    other = row + 1 if (row + date + turn) % 2 == 0 else row - 1
    if 0 <= other < rows_count:
        return date * rows_count + other
    return (date ^ 2) * rows_count + row


def vmem(count):
    return [pl.BlockSpec(memory_space=pltpu.VMEM)] * count


def on_device(slc, offsets, masks):
    dates_dev = slc.shape[1]
    rows_dev = slc.shape[2]
    cols_all = slc.shape[3]
    rows_count = lax.axis_size("row")
    cols_count = lax.axis_size("date")
    planes_dev = 2 * dates_dev
    assert rows_dev == TILE and cols_all == cols_count * LANES

    small = pltpu.CompilerParams(vmem_limit_bytes=4 * 1024 * 1024)
    images = slc.reshape(planes_dev, rows_dev, cols_all)
    moves = pl.CostEstimate(flops=0, bytes_accessed=600_000, transcendentals=0)
    half_shape = jax.ShapeDtypeStruct((GROUPS // 2, 9 * TILE, LANES), FLOAT)

    def swap_rows(cells, turn):
        return lax.ppermute(
            cells,
            ("date", "row"),
            [
                (date * rows_count + row, partner(date, row, turn, rows_count))
                for date in range(cols_count)
                for row in range(rows_count)
            ],
        )

    if cols_count == GROUPS:
        pieces = pl.pallas_call(
            pack_pieces,
            out_shape=[jax.ShapeDtypeStruct((9 * TILE, LANES), FLOAT)] * GROUPS,
            in_specs=vmem(1),
            out_specs=vmem(GROUPS),
            scratch_shapes=[pltpu.VMEM((GROUPS, 9 * TILE, LANES), FLOAT)],
            compiler_params=small,
            cost_estimate=moves,
            name="pack",
        )(images)
        pieces = list(pieces[:1]) + [
            lax.ppermute(pieces[turn], "date", [(i, i ^ turn) for i in range(GROUPS)])
            for turn in range(1, GROUPS)
        ]
        own = [
            pl.pallas_call(
                functools.partial(join_kernel, turns),
                out_shape=half_shape,
                in_specs=vmem(4),
                out_specs=vmem(1)[0],
                compiler_params=small,
                cost_estimate=moves,
                name="join",
            )(*[pieces[turn] for turn in turns])
            for turns in ((6, 7, 4, 5), (2, 3, 1, 0))
        ]
    else:
        outgoing = pl.pallas_call(
            pack_blocks,
            out_shape=jax.ShapeDtypeStruct((cols_count, 9 * planes_dev, LANES), FLOAT),
            in_specs=vmem(1),
            out_specs=vmem(1)[0],
            compiler_params=small,
            cost_estimate=moves,
            name="pack",
        )(images)
        received = lax.all_to_all(outgoing, "date", split_axis=0, concat_axis=0, tiled=True)
        received = canonical(received, dates_dev)
        own = [received[: GROUPS // 2], received[GROUPS // 2 :]]
    near_a, far_a, near_b, far_b = [swap_rows(half, turn) for half in own for turn in range(2)]

    picks, population, row_sub, row_lane, col_lane = pl.pallas_call(
        prepare_kernel,
        out_shape=(
            jax.ShapeDtypeStruct((BLOCKS, 64, 256), HALF_FLOAT),
            jax.ShapeDtypeStruct((TILE, LANES), FLOAT),
            jax.ShapeDtypeStruct((TAP_COUNT, 64, LANES), FLOAT),
            jax.ShapeDtypeStruct((TAP_COUNT, TILE, LANES), FLOAT),
            jax.ShapeDtypeStruct((TAP_COUNT, TILE, LANES), FLOAT),
        ),
        in_specs=[pl.BlockSpec(memory_space=pltpu.SMEM)] + vmem(1),
        out_specs=tuple(vmem(5)),
        scratch_shapes=[pltpu.VMEM((LANES, LANES), jnp.int32)],
        compiler_params=small,
        cost_estimate=pl.CostEstimate(flops=4_000_000, bytes_accessed=1_000_000, transcendentals=0),
        name="prepare",
    )(offsets, masks)

    near_a, far_a = pl.pallas_call(
        screen_kernel,
        out_shape=(half_shape, half_shape),
        in_specs=vmem(2),
        out_specs=tuple(vmem(2)),
        compiler_params=small,
        cost_estimate=moves,
        name="screen",
    )(near_a, far_a)

    half_scratch = [
        pltpu.VMEM((4, LANES, LANES), FLOAT),
        pltpu.VMEM((2 * LANES, LANES), FLOAT),
        pltpu.VMEM((4, LANES + 16, LANES), FLOAT),
    ]
    windows = jax.ShapeDtypeStruct((BLOCKS, LANES, LANES), HALF_FLOAT)
    near_z, near_y = pl.pallas_call(
        near_kernel,
        out_shape=(windows, windows),
        in_specs=vmem(7),
        out_specs=tuple(vmem(2)),
        scratch_shapes=half_scratch,
        compiler_params=small,
        cost_estimate=pl.CostEstimate(
            flops=200_000_000, bytes_accessed=2_000_000, transcendentals=0
        ),
        name="near",
    )(*own[::-1], near_b, near_a, row_sub, row_lane, col_lane)
    linked, eigen = pl.pallas_call(
        link_kernel,
        out_shape=(
            jax.ShapeDtypeStruct((2 * NDATE * TILE, LANES), FLOAT),
            jax.ShapeDtypeStruct((TILE, LANES), FLOAT),
        ),
        in_specs=vmem(11),
        out_specs=tuple(vmem(2)),
        scratch_shapes=[
            pltpu.VMEM((BLOCKS, LANES, LANES), HALF_FLOAT),
            pltpu.VMEM((BLOCKS, LANES, LANES), HALF_FLOAT),
        ]
        + half_scratch
        + [
            pltpu.VMEM((8, LANES, LANES), FLOAT),
            pltpu.VMEM((BLOCKS, 64, LANES), FLOAT),
            pltpu.VMEM((BLOCKS, 128, 256), HALF_FLOAT),
            pltpu.VMEM((BLOCKS, 256, 256), HALF_FLOAT),
        ],
        compiler_params=pltpu.CompilerParams(vmem_limit_bytes=16 * 1024 * 1024),
        cost_estimate=pl.CostEstimate(
            flops=1_000_000_000, bytes_accessed=2_000_000, transcendentals=0
        ),
        name="link",
    )(*own[::-1], far_b, far_a, row_sub, row_lane, col_lane, near_z, near_y, picks, population)
    return linked.reshape(2, NDATE, TILE, LANES), eigen


def solution(mesh):
    in_specs = (P(None, "date", "row", None), P(), P(None, "row", "date"))
    out_specs = (P(None, None, "row", "date"), P("row", "date"))
    return jax.shard_map(
        on_device, mesh=mesh, in_specs=in_specs, out_specs=out_specs, check_vma=False
    )
```

```python
import functools

import jax
import jax.numpy as jnp
from jax import lax
from jax.experimental import pallas as pl
from jax.experimental.pallas import tpu as pltpu
from jax.sharding import PartitionSpec as P

NDATE = 32
SLOT_COLS = 9
EPSILON = 1e-06
LANES = 128
TILE = 8
GROUPS = 8
TAP_COUNT = 8
WINDOW_ROWS = 16
WINDOW_COLS = 136
BLOCKS = 16

FLOAT = jnp.float32
HALF_FLOAT = jnp.bfloat16


def lane_ids(shape):
    return lax.broadcasted_iota(jnp.int32, shape, len(shape) - 1)


def sublane_ids(shape):
    return lax.broadcasted_iota(jnp.int32, shape, len(shape) - 2)


def pack_blocks(slc_ref, send_ref):
    planes = slc_ref.shape[0]
    blocks = send_ref.shape[0]
    for block in range(blocks):
        for plane in range(planes):
            send_ref[block, pl.ds(plane, TILE, stride=planes), :] = slc_ref[
                plane, :, block * LANES : (block + 1) * LANES
            ]
    lanes = lane_ids((planes, LANES))
    rims = [jnp.zeros((planes, LANES), FLOAT) for _ in range(blocks)]
    for row in range(TILE):
        start = 16 * row
        turned = [
            pltpu.roll(
                send_ref[block, row * planes : (row + 1) * planes, :],
                (start + 8) % LANES,
                axis=1,
            )
            for block in range(blocks)
        ]
        left = (lanes >= start) & (lanes < start + 8)
        right = (lanes >= start + 8) & (lanes < start + 16)
        for block in range(blocks):
            if block > 0:
                rims[block] = jnp.where(left, turned[block - 1], rims[block])
            if block < blocks - 1:
                rims[block] = jnp.where(right, turned[block + 1], rims[block])
    for block in range(blocks):
        send_ref[block, TILE * planes : (TILE + 1) * planes, :] = rims[block]


def pack_pieces(slc_ref, *rest):
    pieces, blocks_ref = rest[:-1], rest[-1]
    pack_blocks(slc_ref, blocks_ref)
    here = lax.axis_index("date")
    for turn, piece_ref in enumerate(pieces):
        piece_ref[...] = blocks_ref[here ^ turn]


def join_kernel(turns, *rest):
    here = lax.axis_index("date")
    for turn, piece_ref in zip(turns, rest[:-1]):
        rest[-1][(here ^ turn) % 4] = piece_ref[...]


def tap_weight(distance):
    spread = jnp.abs(2 * distance - 1)
    return jnp.where(spread == 1, 0.5625, jnp.where(spread == 3, -0.0625, 0.0)).astype(FLOAT)


def prepare_kernel(
    offsets_ref, masks_ref, picks_ref, population_ref, row_sub_ref, row_lane_ref, col_lane_ref, words_ref
):
    words = masks_ref.shape[0]
    below = near_is_below()
    total = jnp.zeros((TILE, LANES), jnp.int32)
    for word in range(words):
        bits = masks_ref[word]
        bits = bits - (lax.shift_right_logical(bits, 1) & 0x55555555)
        bits = (bits & 0x33333333) + (lax.shift_right_logical(bits, 2) & 0x33333333)
        bits = (bits + lax.shift_right_logical(bits, 4)) & 0x0F0F0F0F
        bits = bits + lax.shift_right_logical(bits, 8)
        bits = bits + lax.shift_right_logical(bits, 16)
        total = total + (bits & 0xFF)
    population_ref[...] = total.astype(FLOAT)

    lanes = lane_ids((TILE, LANES))
    subs = sublane_ids((TILE, LANES))
    lane_dates = ((lanes % 64) // 8) * 4 + lanes % 4
    row_shift = jnp.zeros((TILE, LANES), jnp.int32)
    col_shift = jnp.zeros((TILE, LANES), jnp.int32)
    for date in range(NDATE):
        here = lane_dates == date
        row_shift = jnp.where(here, offsets_ref[0, date], row_shift)
        col_shift = jnp.where(here, offsets_ref[1, date], col_shift)
    for tap in range(TAP_COUNT):
        row_lane_ref[tap] = tap_weight(tap - 3 - row_shift)
        col_lane_ref[tap] = tap_weight(tap - 3 - col_shift)
    for group in range(GROUPS):
        shift = jnp.zeros((TILE, LANES), jnp.int32)
        for date in range(4):
            shift = jnp.where(subs % 4 == date, offsets_ref[0, 4 * group + date], shift)
        for tap in range(TAP_COUNT):
            row_sub_ref[tap, group * TILE : (group + 1) * TILE, :] = tap_weight(tap - 3 - shift)

    flat = [masks_ref[word] for word in range(words)]
    flat = flat + [jnp.zeros((TILE, LANES), jnp.int32)] * (LANES // TILE - words)
    words_ref[...] = jnp.transpose(jnp.concatenate(flat, axis=0))

    def one_block(block, carry):
        packed = words_ref[pl.ds(pl.multiple_of(block * TILE, TILE), TILE), :]
        for row_pair in range(TILE // 2):
            spread = [[], []]
            for row in (2 * row_pair, 2 * row_pair + 1):
                row_words = [
                    jnp.broadcast_to(
                        packed[:, word * TILE + row : word * TILE + row + 1], (TILE, LANES)
                    )
                    for word in range(words)
                ]
                for half in range(2):
                    near = 8 * half + lanes // 16 - row
                    across = lanes % 16 - subs
                    inside = (near >= 0) & (near <= 8) & (across >= 0) & (across <= 8)
                    amount = jnp.where(inside, (near & 1) * SLOT_COLS + across, 31)
                    first = max(0, 8 * half - row) // 2
                    last = min(8, 8 * half + 7 - row) // 2
                    chosen = row_words[first]
                    for word in range(first + 1, last + 1):
                        chosen = jnp.where(near >= 2 * word, row_words[word], chosen)
                    bits = lax.shift_right_logical(chosen, amount) & 1
                    spread[half].append(bits.astype(FLOAT))
            low_half, high_half = [jnp.concatenate(half, axis=0) for half in spread]
            rows = slice(16 * row_pair, 16 * row_pair + 16)
            picks_ref[block, rows, :LANES] = jnp.where(below, high_half, low_half).astype(HALF_FLOAT)
            picks_ref[block, rows, LANES:] = jnp.where(below, low_half, high_half).astype(HALF_FLOAT)
        return carry

    lax.fori_loop(0, BLOCKS, one_block, 0)


def split_halves(values):
    high = values.astype(HALF_FLOAT)
    low = values - high.astype(FLOAT)
    return high, low


def dot(a, b, contract):
    return lax.dot_general(
        a, b, (((contract[0],), (contract[1],)), ((), ())), preferred_element_type=FLOAT
    )


def packed_rims(base, refs):
    halves = [ref[:, 8 * TILE : 9 * TILE, :].reshape(32, LANES) for ref in refs]
    return jnp.where(
        base == 0, jnp.concatenate(halves, axis=0), jnp.concatenate(halves[::-1], axis=0)
    )


def first_group():
    return (lax.axis_index("date") ^ 4) & 4 if lax.axis_size("date") == GROUPS else 0


def near_is_below():
    return (lax.axis_index("row") + lax.axis_index("date")) % 2 == 0


def exists_at(below):
    row_at, row_count = lax.axis_index("row"), lax.axis_size("row")
    return (below & (row_at < row_count - 1)) | (jnp.logical_not(below) & (row_at > 0))


def mix_rows(base, own_ref, other_ref, below, row_sub_ref, mixed_ref):
    exists = exists_at(below)

    def mix_group(slot, carry):
        group = base + slot
        weights = [
            row_sub_ref[tap, pl.ds(pl.multiple_of(group * TILE, TILE), TILE), :]
            for tap in range(TAP_COUNT)
        ]
        own = [own_ref[slot, row * TILE : (row + 1) * TILE, :] for row in range(TILE)]
        other = [
            jnp.where(exists, other_ref[slot, row * TILE : (row + 1) * TILE, :], 0.0)
            for row in range(TILE)
        ]
        raw = [jnp.where(below, a, b) for a, b in zip(own, other)]
        raw = raw + [jnp.where(below, b, a) for a, b in zip(own, other)]
        for row in range(8):
            mixed = weights[0] * raw[row + 1]
            for tap in range(1, TAP_COUNT):
                mixed = mixed + weights[tap] * raw[row + 1 + tap]
            start = pl.multiple_of((row // 4) * 64 + group * TILE, TILE)
            mixed_ref[row % 4, pl.ds(start, TILE), :] = mixed
        return carry

    lax.fori_loop(0, GROUPS // 2, mix_group, 0, unroll=2)


def turn_rows(base, own_refs, other_refs, below, row_lane_ref, mixed_ref, rims_ref, turned_ref):
    exists = exists_at(below)

    lanes = lane_ids((1, LANES))
    lower = lanes < 64
    own, other = [packed_rims(base, refs) for refs in (own_refs, other_refs)]
    other = jnp.where(exists, other, 0.0)
    first, second = jnp.where(below, own, other), jnp.where(below, other, own)
    far_first, far_second = pltpu.roll(first, 64, axis=1), pltpu.roll(second, 64, axis=1)
    rims_ref[0:LANES, :] = jnp.transpose(
        jnp.concatenate([first, jnp.where(lower, far_first, far_second)], axis=0)
    )
    rims_ref[LANES : 2 * LANES, :] = jnp.transpose(jnp.concatenate([second, far_second], axis=0))
    row_weights = [row_lane_ref[tap, 0:1, :] for tap in range(TAP_COUNT)]
    for row in range(4):
        turned_ref[row, 8 : 8 + LANES, :] = jnp.transpose(mixed_ref[row])
        rim = row_weights[0] * rims_ref[(row + 1) * 16 : (row + 2) * 16, :]
        for tap in range(1, TAP_COUNT):
            rim = rim + row_weights[tap] * rims_ref[(row + 1 + tap) * 16 : (row + 2 + tap) * 16, :]
        turned_ref[row, 0:8, :] = rim[0:8]
        turned_ref[row, 8 + LANES : 16 + LANES, :] = rim[8:16]


def resample_columns(below, col_lane_ref, z_ref, y_ref, turned_ref, first, count):
    row_at, row_count = lax.axis_index("row"), lax.axis_size("row")
    col_at, col_count = lax.axis_index("date"), lax.axis_size("date")
    lanes = lane_ids((1, LANES))
    lower = lanes < 64
    width = count * 8 + 8
    places = sublane_ids((width, LANES)) + first * 8
    inside = ((places >= 4) | (col_at > 0)) & ((places < 132) | (col_at < col_count - 1))
    row_inside = (lower & (below | (row_at > 0))) | (
        (lanes >= 64) & (jnp.logical_not(below) | (row_at < row_count - 1))
    )
    inside = inside & row_inside
    term = lax.broadcasted_iota(jnp.int32, (2 * LANES, 2 * LANES), 0) % LANES
    gives = lax.broadcasted_iota(jnp.int32, (2 * LANES, 2 * LANES), 1)
    same_part = ((term % 8) < 4) == (gives < LANES)
    sums = jnp.where(((term < 64) == ((gives % LANES) < 64)) & same_part, 1.0, 0.0).astype(HALF_FLOAT)

    def store_windows(target, row, values):
        high, low = split_halves(values)
        high = high.astype(FLOAT)
        rows = (
            jnp.where(lower, high, pltpu.roll(low, 64, axis=1)),
            jnp.where(lower, pltpu.roll(high, 64, axis=1), low),
        )
        for part in range(2):
            start = (row + 4 * part) * 16
            for block in range(count):
                target[first + block, start : start + 16, :] = rows[part][
                    block * 8 : block * 8 + 16
                ].astype(HALF_FLOAT)

    for row in range(4):
        begin = 1 + first * 8
        mixed = col_lane_ref[0, 0:1, :] * turned_ref[row, begin : begin + width, :]
        for tap in range(1, TAP_COUNT):
            mixed = mixed + col_lane_ref[tap, 0:1, :] * turned_ref[
                row, begin + tap : begin + tap + width, :
            ]
        z = jnp.where(inside, mixed, 0.0)
        high, low = split_halves(z)
        total = dot(jnp.concatenate([high, low.astype(HALF_FLOAT)], axis=1), sums, (1, 0))
        y = z * total[:, :LANES] + swapped(z) * total[:, LANES:]
        store_windows(z_ref, row, z)
        store_windows(y_ref, row, y)


def swapped(values):
    real = (lane_ids((1, LANES)) % 8) < 4
    return jnp.where(real, pltpu.roll(values, LANES - 4, axis=1), -pltpu.roll(values, 4, axis=1))


def near_kernel(
    own_b,
    own_a,
    near_b,
    near_a,
    picks_ref,
    row_sub_ref,
    row_lane_ref,
    col_lane_ref,
    z_ref,
    y_ref,
    first_ref,
    mixed_ref,
    rims_ref,
    turned_ref,
):
    below = near_is_below()
    base = first_group()
    mix_rows(base, own_a, near_a, below, row_sub_ref, mixed_ref)
    mix_rows(4 - base, own_b, near_b, below, row_sub_ref, mixed_ref)
    turn_rows(
        base, (own_a, own_b), (near_a, near_b), below, row_lane_ref, mixed_ref, rims_ref, turned_ref
    )
    resample_columns(below, col_lane_ref, z_ref, y_ref, turned_ref, 0, BLOCKS)
    for block in range(BLOCKS):
        first_ref[block] = dot(picks_ref[block, :, :LANES], y_ref[block], (1, 0))


def link_kernel(
    own_b,
    own_a,
    far_b,
    far_a,
    row_sub_ref,
    row_lane_ref,
    col_lane_ref,
    near_z_ref,
    near_first_ref,
    picks_ref,
    population_ref,
    linked_ref,
    eigen_ref,
    far_z_ref,
    far_y_ref,
    mixed_ref,
    rims_ref,
    turned_ref,
    result_ref,
    first_ref,
    vectors_ref,
    chosen_ref,
):
    below = jnp.logical_not(near_is_below())
    base = first_group()
    mix_rows(base, own_a, far_a, below, row_sub_ref, mixed_ref)
    mix_rows(4 - base, own_b, far_b, below, row_sub_ref, mixed_ref)
    turn_rows(
        base, (own_a, own_b), (far_a, far_b), below, row_lane_ref, mixed_ref, rims_ref, turned_ref
    )
    lower = lane_ids((1, LANES)) < 64

    def columns(first, count):
        resample_columns(below, col_lane_ref, far_z_ref, far_y_ref, turned_ref, first, count)

    def first_phase(first, count):
        for block in range(first, first + count):
            vector = dot(picks_ref[block, :, LANES:], far_y_ref[block], (1, 0))
            vector = vector + near_first_ref[block]
            vector = vector + pltpu.roll(vector, 64, axis=1)
            high, low = split_halves(jnp.concatenate([vector, swapped(vector)], axis=0))
            first_ref[block] = vector
            vectors_ref[block, :, :LANES] = high
            vectors_ref[block, :, LANES:] = low.astype(HALF_FLOAT)

    def inner_phase(first, count):
        for block in range(first, first + count):
            z = jnp.concatenate([near_z_ref[block], far_z_ref[block]], axis=0)
            inner = dot(vectors_ref[block], jnp.concatenate([z, z], axis=1), (1, 1))
            high, low = split_halves(inner)
            picks = picks_ref[block]
            picks = jnp.concatenate([picks, picks], axis=0)
            chosen_ref[block, :128, :] = high * picks
            chosen_ref[block, 128:, :] = low.astype(HALF_FLOAT) * picks

    def outer_phase(first, count):
        for block in range(first, first + count):
            z = jnp.concatenate([near_z_ref[block], far_z_ref[block]], axis=0)
            outer = dot(chosen_ref[block], z, (1, 0))
            outer = outer[:128] + outer[128:]
            outer = outer + pltpu.roll(outer, 64, axis=1)
            second = outer[:64] - swapped(outer[64:])
            both = jnp.where(lower, second, first_ref[block])
            for row in range(8):
                result_ref[row, block * 8 : block * 8 + 8, :] = both[row * 8 : row * 8 + 8]

    half = BLOCKS // 2
    columns(0, half)
    first_phase(0, half)
    columns(half, half)
    inner_phase(0, half)
    first_phase(half, half)
    outer_phase(0, half)
    inner_phase(half, half)
    outer_phase(half, half)

    inverse = 1.0 / population_ref[...]
    for row in range(8):
        turned = jnp.transpose(result_ref[row])
        second, first = turned[:64], turned[64:]
        scale = inverse[row : row + 1]
        square = scale * scale
        norm_first = jnp.sqrt(jnp.sum(first * first, axis=0, keepdims=True) * square + EPSILON)
        norm_last = jnp.sqrt(
            jnp.sum(second * second, axis=0, keepdims=True) * (square * square) + EPSILON
        )
        eigen_ref[row : row + 1, :] = norm_last / norm_first
        linked = second * (square * (jnp.sqrt(jnp.float32(NDATE)) / norm_last))
        for group in range(GROUPS):
            for part in range(2):
                begin = ((part * NDATE + 4 * group) * 8) + row
                at = group * 8 + part * 4
                linked_ref[pl.ds(begin, 4, stride=8), :] = linked[at : at + 4]


def canonical(received, dates_dev):
    sources = received.shape[0]
    if dates_dev == 4:
        return received
    cells = received.reshape(sources, 9, 2, dates_dev, LANES)
    cells = jnp.transpose(cells, (1, 2, 0, 3, 4)).reshape(9, 2, GROUPS, 4, LANES)
    return jnp.transpose(cells, (2, 0, 1, 3, 4)).reshape(GROUPS, 9 * TILE, LANES)


def partner(date, row, turn, rows_count):
    other = row + 1 if (row + date + turn) % 2 == 0 else row - 1
    if 0 <= other < rows_count:
        return date * rows_count + other
    return (date ^ 2) * rows_count + row


def vmem(count):
    return [pl.BlockSpec(memory_space=pltpu.VMEM)] * count


def on_device(slc, offsets, masks):
    dates_dev = slc.shape[1]
    rows_dev = slc.shape[2]
    cols_all = slc.shape[3]
    rows_count = lax.axis_size("row")
    cols_count = lax.axis_size("date")
    planes_dev = 2 * dates_dev
    assert rows_dev == TILE and cols_all == cols_count * LANES

    small = pltpu.CompilerParams(vmem_limit_bytes=4 * 1024 * 1024)
    images = slc.reshape(planes_dev, rows_dev, cols_all)
    moves = pl.CostEstimate(flops=0, bytes_accessed=600_000, transcendentals=0)
    half_shape = jax.ShapeDtypeStruct((GROUPS // 2, 9 * TILE, LANES), FLOAT)

    def swap_rows(cells, turn):
        return lax.ppermute(
            cells,
            ("date", "row"),
            [
                (date * rows_count + row, partner(date, row, turn, rows_count))
                for date in range(cols_count)
                for row in range(rows_count)
            ],
        )

    if cols_count == GROUPS:
        pieces = pl.pallas_call(
            pack_pieces,
            out_shape=[jax.ShapeDtypeStruct((9 * TILE, LANES), FLOAT)] * GROUPS,
            in_specs=vmem(1),
            out_specs=vmem(GROUPS),
            scratch_shapes=[pltpu.VMEM((GROUPS, 9 * TILE, LANES), FLOAT)],
            compiler_params=small,
            cost_estimate=moves,
            name="pack",
        )(images)
        pieces = list(pieces[:1]) + [
            lax.ppermute(pieces[turn], "date", [(i, i ^ turn) for i in range(GROUPS)])
            for turn in range(1, GROUPS)
        ]
        own = [
            pl.pallas_call(
                functools.partial(join_kernel, turns),
                out_shape=half_shape,
                in_specs=vmem(4),
                out_specs=vmem(1)[0],
                compiler_params=small,
                cost_estimate=moves,
                name="join",
            )(*[pieces[turn] for turn in turns])
            for turns in ((6, 7, 4, 5), (2, 3, 1, 0))
        ]
    else:
        outgoing = pl.pallas_call(
            pack_blocks,
            out_shape=jax.ShapeDtypeStruct((cols_count, 9 * planes_dev, LANES), FLOAT),
            in_specs=vmem(1),
            out_specs=vmem(1)[0],
            compiler_params=small,
            cost_estimate=moves,
            name="pack",
        )(images)
        received = lax.all_to_all(outgoing, "date", split_axis=0, concat_axis=0, tiled=True)
        received = canonical(received, dates_dev)
        own = [received[: GROUPS // 2], received[GROUPS // 2 :]]
    near_a, far_a, near_b, far_b = [swap_rows(half, turn) for half in own for turn in range(2)]

    picks, population, row_sub, row_lane, col_lane = pl.pallas_call(
        prepare_kernel,
        out_shape=(
            jax.ShapeDtypeStruct((BLOCKS, 64, 256), HALF_FLOAT),
            jax.ShapeDtypeStruct((TILE, LANES), FLOAT),
            jax.ShapeDtypeStruct((TAP_COUNT, 64, LANES), FLOAT),
            jax.ShapeDtypeStruct((TAP_COUNT, TILE, LANES), FLOAT),
            jax.ShapeDtypeStruct((TAP_COUNT, TILE, LANES), FLOAT),
        ),
        in_specs=[pl.BlockSpec(memory_space=pltpu.SMEM)] + vmem(1),
        out_specs=tuple(vmem(5)),
        scratch_shapes=[pltpu.VMEM((LANES, LANES), jnp.int32)],
        compiler_params=small,
        cost_estimate=pl.CostEstimate(flops=4_000_000, bytes_accessed=1_000_000, transcendentals=0),
        name="prepare",
    )(offsets, masks)

    half_scratch = [
        pltpu.VMEM((4, LANES, LANES), FLOAT),
        pltpu.VMEM((2 * LANES, LANES), FLOAT),
        pltpu.VMEM((4, LANES + 16, LANES), FLOAT),
    ]
    windows = jax.ShapeDtypeStruct((BLOCKS, LANES, LANES), HALF_FLOAT)
    near_z, _, near_first = pl.pallas_call(
        near_kernel,
        out_shape=(
            windows,
            windows,
            jax.ShapeDtypeStruct((BLOCKS, 64, LANES), FLOAT),
        ),
        in_specs=vmem(8),
        out_specs=tuple(vmem(3)),
        scratch_shapes=half_scratch,
        compiler_params=small,
        cost_estimate=pl.CostEstimate(
            flops=200_000_000, bytes_accessed=2_000_000, transcendentals=0
        ),
        name="near",
    )(*own[::-1], near_b, near_a, picks, row_sub, row_lane, col_lane)
    linked, eigen = pl.pallas_call(
        link_kernel,
        out_shape=(
            jax.ShapeDtypeStruct((2 * NDATE * TILE, LANES), FLOAT),
            jax.ShapeDtypeStruct((TILE, LANES), FLOAT),
        ),
        in_specs=vmem(11),
        out_specs=tuple(vmem(2)),
        scratch_shapes=[
            pltpu.VMEM((BLOCKS, LANES, LANES), HALF_FLOAT),
            pltpu.VMEM((BLOCKS, LANES, LANES), HALF_FLOAT),
        ]
        + half_scratch
        + [
            pltpu.VMEM((8, LANES, LANES), FLOAT),
            pltpu.VMEM((BLOCKS, 64, LANES), FLOAT),
            pltpu.VMEM((BLOCKS, 128, 256), HALF_FLOAT),
            pltpu.VMEM((BLOCKS, 256, 256), HALF_FLOAT),
        ],
        compiler_params=pltpu.CompilerParams(vmem_limit_bytes=16 * 1024 * 1024),
        cost_estimate=pl.CostEstimate(
            flops=1_000_000_000, bytes_accessed=2_000_000, transcendentals=0
        ),
        name="link",
    )(*own[::-1], far_b, far_a, row_sub, row_lane, col_lane, near_z, near_first, picks, population)
    return linked.reshape(2, NDATE, TILE, LANES), eigen


def solution(mesh):
    in_specs = (P(None, "date", "row", None), P(), P(None, "row", "date"))
    out_specs = (P(None, None, "row", "date"), P("row", "date"))
    return jax.shard_map(
        on_device, mesh=mesh, in_specs=in_specs, out_specs=out_specs, check_vma=False
    )
```

```python
import functools

import jax
import jax.numpy as jnp
from jax import lax
from jax.experimental import pallas as pl
from jax.experimental.pallas import tpu as pltpu
from jax.sharding import PartitionSpec as P

NDATE = 32
SLOT_COLS = 9
EPSILON = 1e-06
LANES = 128
TILE = 8
GROUPS = 8
TAP_COUNT = 8
WINDOW_ROWS = 16
WINDOW_COLS = 136
BLOCKS = 16

FLOAT = jnp.float32
HALF_FLOAT = jnp.bfloat16


def lane_ids(shape):
    return lax.broadcasted_iota(jnp.int32, shape, len(shape) - 1)


def sublane_ids(shape):
    return lax.broadcasted_iota(jnp.int32, shape, len(shape) - 2)


def pack_blocks(slc_ref, send_ref):
    planes = slc_ref.shape[0]
    blocks = send_ref.shape[0]
    for block in range(blocks):
        for plane in range(planes):
            send_ref[block, pl.ds(plane, TILE, stride=planes), :] = slc_ref[
                plane, :, block * LANES : (block + 1) * LANES
            ]
    lanes = lane_ids((planes, LANES))
    rims = [jnp.zeros((planes, LANES), FLOAT) for _ in range(blocks)]
    for row in range(TILE):
        start = 16 * row
        turned = [
            pltpu.roll(
                send_ref[block, row * planes : (row + 1) * planes, :],
                (start + 8) % LANES,
                axis=1,
            )
            for block in range(blocks)
        ]
        left = (lanes >= start) & (lanes < start + 8)
        right = (lanes >= start + 8) & (lanes < start + 16)
        for block in range(blocks):
            if block > 0:
                rims[block] = jnp.where(left, turned[block - 1], rims[block])
            if block < blocks - 1:
                rims[block] = jnp.where(right, turned[block + 1], rims[block])
    for block in range(blocks):
        send_ref[block, TILE * planes : (TILE + 1) * planes, :] = rims[block]


def pack_pieces(slc_ref, *rest):
    pieces, blocks_ref = rest[:-1], rest[-1]
    pack_blocks(slc_ref, blocks_ref)
    here = lax.axis_index("date")
    for turn, piece_ref in enumerate(pieces):
        piece_ref[...] = blocks_ref[here ^ turn]


def join_kernel(turns, *rest):
    here = lax.axis_index("date")
    for turn, piece_ref in zip(turns, rest[:-1]):
        rest[-1][(here ^ turn) % 4] = piece_ref[...]


def tap_weight(distance):
    spread = jnp.abs(2 * distance - 1)
    return jnp.where(spread == 1, 0.5625, jnp.where(spread == 3, -0.0625, 0.0)).astype(FLOAT)


def prepare_kernel(
    offsets_ref, masks_ref, picks_ref, population_ref, row_sub_ref, row_lane_ref, col_lane_ref, words_ref
):
    words = masks_ref.shape[0]
    below = near_is_below()
    total = jnp.zeros((TILE, LANES), jnp.int32)
    for word in range(words):
        bits = masks_ref[word]
        bits = bits - (lax.shift_right_logical(bits, 1) & 0x55555555)
        bits = (bits & 0x33333333) + (lax.shift_right_logical(bits, 2) & 0x33333333)
        bits = (bits + lax.shift_right_logical(bits, 4)) & 0x0F0F0F0F
        bits = bits + lax.shift_right_logical(bits, 8)
        bits = bits + lax.shift_right_logical(bits, 16)
        total = total + (bits & 0xFF)
    population_ref[...] = total.astype(FLOAT)

    lanes = lane_ids((TILE, LANES))
    subs = sublane_ids((TILE, LANES))
    lane_dates = ((lanes % 64) // 8) * 4 + lanes % 4
    row_shift = jnp.zeros((TILE, LANES), jnp.int32)
    col_shift = jnp.zeros((TILE, LANES), jnp.int32)
    for date in range(NDATE):
        here = lane_dates == date
        row_shift = jnp.where(here, offsets_ref[0, date], row_shift)
        col_shift = jnp.where(here, offsets_ref[1, date], col_shift)
    for tap in range(TAP_COUNT):
        row_lane_ref[tap] = tap_weight(tap - 3 - row_shift)
        col_lane_ref[tap] = tap_weight(tap - 3 - col_shift)
    for group in range(GROUPS):
        shift = jnp.zeros((TILE, LANES), jnp.int32)
        for date in range(4):
            shift = jnp.where(subs % 4 == date, offsets_ref[0, 4 * group + date], shift)
        for tap in range(TAP_COUNT):
            row_sub_ref[tap, group * TILE : (group + 1) * TILE, :] = tap_weight(tap - 3 - shift)

    flat = [masks_ref[word] for word in range(words)]
    flat = flat + [jnp.zeros((TILE, LANES), jnp.int32)] * (LANES // TILE - words)
    words_ref[...] = jnp.transpose(jnp.concatenate(flat, axis=0))

    def one_block(block, carry):
        packed = words_ref[pl.ds(pl.multiple_of(block * TILE, TILE), TILE), :]
        for row_pair in range(TILE // 2):
            spread = [[], []]
            for row in (2 * row_pair, 2 * row_pair + 1):
                row_words = [
                    jnp.broadcast_to(
                        packed[:, word * TILE + row : word * TILE + row + 1], (TILE, LANES)
                    )
                    for word in range(words)
                ]
                for half in range(2):
                    near = 8 * half + lanes // 16 - row
                    across = lanes % 16 - subs
                    inside = (near >= 0) & (near <= 8) & (across >= 0) & (across <= 8)
                    amount = jnp.where(inside, (near & 1) * SLOT_COLS + across, 31)
                    first = max(0, 8 * half - row) // 2
                    last = min(8, 8 * half + 7 - row) // 2
                    chosen = row_words[first]
                    for word in range(first + 1, last + 1):
                        chosen = jnp.where(near >= 2 * word, row_words[word], chosen)
                    bits = lax.shift_right_logical(chosen, amount) & 1
                    spread[half].append(bits.astype(FLOAT))
            low_half, high_half = [jnp.concatenate(half, axis=0) for half in spread]
            rows = slice(16 * row_pair, 16 * row_pair + 16)
            picks_ref[block, rows, :LANES] = jnp.where(below, high_half, low_half).astype(HALF_FLOAT)
            picks_ref[block, rows, LANES:] = jnp.where(below, low_half, high_half).astype(HALF_FLOAT)
        return carry

    lax.fori_loop(0, BLOCKS, one_block, 0)


def split_halves(values):
    high = values.astype(HALF_FLOAT)
    low = values - high.astype(FLOAT)
    return high, low


def dot(a, b, contract):
    return lax.dot_general(
        a, b, (((contract[0],), (contract[1],)), ((), ())), preferred_element_type=FLOAT
    )


def packed_rims(base, refs):
    halves = [ref[:, 8 * TILE : 9 * TILE, :].reshape(32, LANES) for ref in refs]
    return jnp.where(
        base == 0, jnp.concatenate(halves, axis=0), jnp.concatenate(halves[::-1], axis=0)
    )


def first_group():
    return (lax.axis_index("date") ^ 4) & 4 if lax.axis_size("date") == GROUPS else 0


def near_is_below():
    return (lax.axis_index("row") + lax.axis_index("date")) % 2 == 0


def resample_rows(
    base,
    own_refs,
    other_refs,
    below,
    row_sub_ref,
    row_lane_ref,
    mixed_ref,
    rims_ref,
    turned_ref,
):
    row_at, row_count = lax.axis_index("row"), lax.axis_size("row")

    exists = (below & (row_at < row_count - 1)) | (jnp.logical_not(below) & (row_at > 0))

    def mix_group(own_ref, other_ref, base, slot):
        group = base + slot
        weights = [
            row_sub_ref[tap, pl.ds(pl.multiple_of(group * TILE, TILE), TILE), :]
            for tap in range(TAP_COUNT)
        ]
        own = [own_ref[slot, row * TILE : (row + 1) * TILE, :] for row in range(TILE)]
        other = [
            jnp.where(exists, other_ref[slot, row * TILE : (row + 1) * TILE, :], 0.0)
            for row in range(TILE)
        ]
        raw = [jnp.where(below, a, b) for a, b in zip(own, other)]
        raw = raw + [jnp.where(below, b, a) for a, b in zip(own, other)]
        for row in range(8):
            mixed = weights[0] * raw[row + 1]
            for tap in range(1, TAP_COUNT):
                mixed = mixed + weights[tap] * raw[row + 1 + tap]
            start = pl.multiple_of((row // 4) * 64 + group * TILE, TILE)
            mixed_ref[row % 4, pl.ds(start, TILE), :] = mixed

    def mix_slot(slot, carry):
        mix_group(own_refs[0], other_refs[0], base, slot)
        mix_group(own_refs[1], other_refs[1], 4 - base, slot)
        return carry

    lax.fori_loop(0, GROUPS // 2, mix_slot, 0)

    lanes = lane_ids((1, LANES))
    lower = lanes < 64
    own, other = [packed_rims(base, refs) for refs in (own_refs, other_refs)]
    other = jnp.where(exists, other, 0.0)
    first, second = jnp.where(below, own, other), jnp.where(below, other, own)
    far_first, far_second = pltpu.roll(first, 64, axis=1), pltpu.roll(second, 64, axis=1)
    rims_ref[0:LANES, :] = jnp.transpose(
        jnp.concatenate([first, jnp.where(lower, far_first, far_second)], axis=0)
    )
    rims_ref[LANES : 2 * LANES, :] = jnp.transpose(jnp.concatenate([second, far_second], axis=0))
    row_weights = [row_lane_ref[tap, 0:1, :] for tap in range(TAP_COUNT)]
    for row in range(4):
        turned_ref[row, 8 : 8 + LANES, :] = jnp.transpose(mixed_ref[row])
        rim = row_weights[0] * rims_ref[(row + 1) * 16 : (row + 2) * 16, :]
        for tap in range(1, TAP_COUNT):
            rim = rim + row_weights[tap] * rims_ref[(row + 1 + tap) * 16 : (row + 2 + tap) * 16, :]
        turned_ref[row, 0:8, :] = rim[0:8]
        turned_ref[row, 8 + LANES : 16 + LANES, :] = rim[8:16]


def resample_columns(below, col_lane_ref, z_ref, y_ref, turned_ref, first, count):
    row_at, row_count = lax.axis_index("row"), lax.axis_size("row")
    col_at, col_count = lax.axis_index("date"), lax.axis_size("date")
    lanes = lane_ids((1, LANES))
    lower = lanes < 64
    width = count * 8 + 8
    places = sublane_ids((width, LANES)) + first * 8
    inside = ((places >= 4) | (col_at > 0)) & ((places < 132) | (col_at < col_count - 1))
    row_inside = (lower & (below | (row_at > 0))) | (
        (lanes >= 64) & (jnp.logical_not(below) | (row_at < row_count - 1))
    )
    inside = inside & row_inside
    term = lax.broadcasted_iota(jnp.int32, (2 * LANES, 2 * LANES), 0) % LANES
    gives = lax.broadcasted_iota(jnp.int32, (2 * LANES, 2 * LANES), 1)
    same_part = ((term % 8) < 4) == (gives < LANES)
    sums = jnp.where(((term < 64) == ((gives % LANES) < 64)) & same_part, 1.0, 0.0).astype(HALF_FLOAT)

    def store_windows(target, row, values):
        high, low = split_halves(values)
        high = high.astype(FLOAT)
        rows = (
            jnp.where(lower, high, pltpu.roll(low, 64, axis=1)),
            jnp.where(lower, pltpu.roll(high, 64, axis=1), low),
        )
        for part in range(2):
            start = (row + 4 * part) * 16
            for block in range(count):
                target[first + block, start : start + 16, :] = rows[part][
                    block * 8 : block * 8 + 16
                ].astype(HALF_FLOAT)

    for row in range(4):
        begin = 1 + first * 8
        mixed = col_lane_ref[0, 0:1, :] * turned_ref[row, begin : begin + width, :]
        for tap in range(1, TAP_COUNT):
            mixed = mixed + col_lane_ref[tap, 0:1, :] * turned_ref[
                row, begin + tap : begin + tap + width, :
            ]
        z = jnp.where(inside, mixed, 0.0)
        high, low = split_halves(z)
        total = dot(jnp.concatenate([high, low.astype(HALF_FLOAT)], axis=1), sums, (1, 0))
        y = z * total[:, :LANES] + swapped(z) * total[:, LANES:]
        store_windows(z_ref, row, z)
        store_windows(y_ref, row, y)


def swapped(values):
    real = (lane_ids((1, LANES)) % 8) < 4
    return jnp.where(real, pltpu.roll(values, LANES - 4, axis=1), -pltpu.roll(values, 4, axis=1))


def near_kernel(
    own_b,
    own_a,
    near_b,
    near_a,
    row_sub_ref,
    row_lane_ref,
    col_lane_ref,
    z_ref,
    y_ref,
    mixed_ref,
    rims_ref,
    turned_ref,
):
    below = near_is_below()
    resample_rows(
        first_group(),
        (own_a, own_b),
        (near_a, near_b),
        below,
        row_sub_ref,
        row_lane_ref,
        mixed_ref,
        rims_ref,
        turned_ref,
    )
    resample_columns(below, col_lane_ref, z_ref, y_ref, turned_ref, 0, BLOCKS)


def link_kernel(
    own_b,
    own_a,
    far_b,
    far_a,
    row_sub_ref,
    row_lane_ref,
    col_lane_ref,
    near_z_ref,
    near_y_ref,
    picks_ref,
    population_ref,
    linked_ref,
    eigen_ref,
    far_z_ref,
    far_y_ref,
    mixed_ref,
    rims_ref,
    turned_ref,
    result_ref,
    first_ref,
    vectors_ref,
    chosen_ref,
):
    below = jnp.logical_not(near_is_below())
    resample_rows(
        first_group(),
        (own_a, own_b),
        (far_a, far_b),
        below,
        row_sub_ref,
        row_lane_ref,
        mixed_ref,
        rims_ref,
        turned_ref,
    )
    lower = lane_ids((1, LANES)) < 64

    def columns(first, count):
        resample_columns(below, col_lane_ref, far_z_ref, far_y_ref, turned_ref, first, count)

    def first_phase(first, count):
        for block in range(first, first + count):
            y = jnp.concatenate([near_y_ref[block], far_y_ref[block]], axis=0)
            vector = dot(picks_ref[block], y, (1, 0))
            vector = vector + pltpu.roll(vector, 64, axis=1)
            high, low = split_halves(jnp.concatenate([vector, swapped(vector)], axis=0))
            first_ref[block] = vector
            vectors_ref[block, :128, :] = high
            vectors_ref[block, 128:, :] = low.astype(HALF_FLOAT)

    def inner_phase(first, count):
        for block in range(first, first + count):
            z = jnp.concatenate([near_z_ref[block], far_z_ref[block]], axis=0)
            inner = dot(vectors_ref[block], z, (1, 1))
            inner = inner[:128] + inner[128:]
            high, low = split_halves(inner)
            picks = picks_ref[block]
            picks = jnp.concatenate([picks, picks], axis=0)
            chosen_ref[block, :128, :] = high * picks
            chosen_ref[block, 128:, :] = low.astype(HALF_FLOAT) * picks

    def outer_phase(first, count):
        for block in range(first, first + count):
            z = jnp.concatenate([near_z_ref[block], far_z_ref[block]], axis=0)
            outer = dot(chosen_ref[block], z, (1, 0))
            outer = outer[:128] + outer[128:]
            outer = outer + pltpu.roll(outer, 64, axis=1)
            second = outer[:64] - swapped(outer[64:])
            both = jnp.where(lower, second, first_ref[block])
            for row in range(8):
                result_ref[row, block * 8 : block * 8 + 8, :] = both[row * 8 : row * 8 + 8]

    half = BLOCKS // 2
    columns(0, half)
    first_phase(0, half)
    columns(half, half)
    inner_phase(0, half)
    first_phase(half, half)
    outer_phase(0, half)
    inner_phase(half, half)
    outer_phase(half, half)

    inverse = 1.0 / population_ref[...]
    for row in range(8):
        turned = jnp.transpose(result_ref[row])
        second, first = turned[:64], turned[64:]
        scale = inverse[row : row + 1]
        square = scale * scale
        norm_first = jnp.sqrt(jnp.sum(first * first, axis=0, keepdims=True) * square + EPSILON)
        norm_last = jnp.sqrt(
            jnp.sum(second * second, axis=0, keepdims=True) * (square * square) + EPSILON
        )
        eigen_ref[row : row + 1, :] = norm_last / norm_first
        linked = second * (square * (jnp.sqrt(jnp.float32(NDATE)) / norm_last))
        for group in range(GROUPS):
            for part in range(2):
                begin = ((part * NDATE + 4 * group) * 8) + row
                at = group * 8 + part * 4
                linked_ref[pl.ds(begin, 4, stride=8), :] = linked[at : at + 4]


def canonical(received, dates_dev):
    sources = received.shape[0]
    if dates_dev == 4:
        return received
    cells = received.reshape(sources, 9, 2, dates_dev, LANES)
    cells = jnp.transpose(cells, (1, 2, 0, 3, 4)).reshape(9, 2, GROUPS, 4, LANES)
    return jnp.transpose(cells, (2, 0, 1, 3, 4)).reshape(GROUPS, 9 * TILE, LANES)


def partner(date, row, turn, rows_count):
    other = row + 1 if (row + date + turn) % 2 == 0 else row - 1
    if 0 <= other < rows_count:
        return date * rows_count + other
    return (date ^ 2) * rows_count + row


def vmem(count):
    return [pl.BlockSpec(memory_space=pltpu.VMEM)] * count


def on_device(slc, offsets, masks):
    dates_dev = slc.shape[1]
    rows_dev = slc.shape[2]
    cols_all = slc.shape[3]
    rows_count = lax.axis_size("row")
    cols_count = lax.axis_size("date")
    planes_dev = 2 * dates_dev
    assert rows_dev == TILE and cols_all == cols_count * LANES

    small = pltpu.CompilerParams(vmem_limit_bytes=4 * 1024 * 1024)
    images = slc.reshape(planes_dev, rows_dev, cols_all)
    moves = pl.CostEstimate(flops=0, bytes_accessed=600_000, transcendentals=0)
    half_shape = jax.ShapeDtypeStruct((GROUPS // 2, 9 * TILE, LANES), FLOAT)

    def swap_rows(cells, turn):
        return lax.ppermute(
            cells,
            ("date", "row"),
            [
                (date * rows_count + row, partner(date, row, turn, rows_count))
                for date in range(cols_count)
                for row in range(rows_count)
            ],
        )

    if cols_count == GROUPS:
        pieces = pl.pallas_call(
            pack_pieces,
            out_shape=[jax.ShapeDtypeStruct((9 * TILE, LANES), FLOAT)] * GROUPS,
            in_specs=vmem(1),
            out_specs=vmem(GROUPS),
            scratch_shapes=[pltpu.VMEM((GROUPS, 9 * TILE, LANES), FLOAT)],
            compiler_params=small,
            cost_estimate=moves,
            name="pack",
        )(images)
        pieces = list(pieces[:1]) + [
            lax.ppermute(pieces[turn], "date", [(i, i ^ turn) for i in range(GROUPS)])
            for turn in range(1, GROUPS)
        ]
        own = [
            pl.pallas_call(
                functools.partial(join_kernel, turns),
                out_shape=half_shape,
                in_specs=vmem(4),
                out_specs=vmem(1)[0],
                compiler_params=small,
                cost_estimate=moves,
                name="join",
            )(*[pieces[turn] for turn in turns])
            for turns in ((6, 7, 4, 5), (2, 3, 1, 0))
        ]
    else:
        outgoing = pl.pallas_call(
            pack_blocks,
            out_shape=jax.ShapeDtypeStruct((cols_count, 9 * planes_dev, LANES), FLOAT),
            in_specs=vmem(1),
            out_specs=vmem(1)[0],
            compiler_params=small,
            cost_estimate=moves,
            name="pack",
        )(images)
        received = lax.all_to_all(outgoing, "date", split_axis=0, concat_axis=0, tiled=True)
        received = canonical(received, dates_dev)
        own = [received[: GROUPS // 2], received[GROUPS // 2 :]]
    near_a, far_a, near_b, far_b = [swap_rows(half, turn) for half in own for turn in range(2)]

    picks, population, row_sub, row_lane, col_lane = pl.pallas_call(
        prepare_kernel,
        out_shape=(
            jax.ShapeDtypeStruct((BLOCKS, 64, 256), HALF_FLOAT),
            jax.ShapeDtypeStruct((TILE, LANES), FLOAT),
            jax.ShapeDtypeStruct((TAP_COUNT, 64, LANES), FLOAT),
            jax.ShapeDtypeStruct((TAP_COUNT, TILE, LANES), FLOAT),
            jax.ShapeDtypeStruct((TAP_COUNT, TILE, LANES), FLOAT),
        ),
        in_specs=[pl.BlockSpec(memory_space=pltpu.SMEM)] + vmem(1),
        out_specs=tuple(vmem(5)),
        scratch_shapes=[pltpu.VMEM((LANES, LANES), jnp.int32)],
        compiler_params=small,
        cost_estimate=pl.CostEstimate(flops=4_000_000, bytes_accessed=1_000_000, transcendentals=0),
        name="prepare",
    )(offsets, masks)

    half_scratch = [
        pltpu.VMEM((4, LANES, LANES), FLOAT),
        pltpu.VMEM((2 * LANES, LANES), FLOAT),
        pltpu.VMEM((4, LANES + 16, LANES), FLOAT),
    ]
    windows = jax.ShapeDtypeStruct((BLOCKS, LANES, LANES), HALF_FLOAT)
    near_z, near_y = pl.pallas_call(
        near_kernel,
        out_shape=(windows, windows),
        in_specs=vmem(7),
        out_specs=tuple(vmem(2)),
        scratch_shapes=half_scratch,
        compiler_params=small,
        cost_estimate=pl.CostEstimate(
            flops=200_000_000, bytes_accessed=2_000_000, transcendentals=0
        ),
        name="near",
    )(*own[::-1], near_b, near_a, row_sub, row_lane, col_lane)
    linked, eigen = pl.pallas_call(
        link_kernel,
        out_shape=(
            jax.ShapeDtypeStruct((2 * NDATE * TILE, LANES), FLOAT),
            jax.ShapeDtypeStruct((TILE, LANES), FLOAT),
        ),
        in_specs=vmem(11),
        out_specs=tuple(vmem(2)),
        scratch_shapes=[
            pltpu.VMEM((BLOCKS, LANES, LANES), HALF_FLOAT),
            pltpu.VMEM((BLOCKS, LANES, LANES), HALF_FLOAT),
        ]
        + half_scratch
        + [
            pltpu.VMEM((8, LANES, LANES), FLOAT),
            pltpu.VMEM((BLOCKS, 64, LANES), FLOAT),
            pltpu.VMEM((BLOCKS, 256, LANES), HALF_FLOAT),
            pltpu.VMEM((BLOCKS, 256, 256), HALF_FLOAT),
        ],
        compiler_params=pltpu.CompilerParams(vmem_limit_bytes=16 * 1024 * 1024),
        cost_estimate=pl.CostEstimate(
            flops=1_000_000_000, bytes_accessed=2_000_000, transcendentals=0
        ),
        name="link",
    )(*own[::-1], far_b, far_a, row_sub, row_lane, col_lane, near_z, near_y, picks, population)
    return linked.reshape(2, NDATE, TILE, LANES), eigen


def solution(mesh):
    in_specs = (P(None, "date", "row", None), P(), P(None, "row", "date"))
    out_specs = (P(None, None, "row", "date"), P("row", "date"))
    return jax.shard_map(
        on_device, mesh=mesh, in_specs=in_specs, out_specs=out_specs, check_vma=False
    )
```

```python
import functools

import jax
import jax.numpy as jnp
from jax import lax
from jax.experimental import pallas as pl
from jax.experimental.pallas import tpu as pltpu
from jax.sharding import PartitionSpec as P

NDATE = 32
SLOT_COLS = 9
EPSILON = 1e-06
LANES = 128
TILE = 8
GROUPS = 8
TAP_COUNT = 8
WINDOW_ROWS = 16
WINDOW_COLS = 136
BLOCKS = 16

FLOAT = jnp.float32
HALF_FLOAT = jnp.bfloat16


def lane_ids(shape):
    return lax.broadcasted_iota(jnp.int32, shape, len(shape) - 1)


def sublane_ids(shape):
    return lax.broadcasted_iota(jnp.int32, shape, len(shape) - 2)


def pack_blocks(slc_ref, send_ref):
    planes = slc_ref.shape[0]
    blocks = send_ref.shape[0]
    for block in range(blocks):
        for plane in range(planes):
            send_ref[block, pl.ds(plane, TILE, stride=planes), :] = slc_ref[
                plane, :, block * LANES : (block + 1) * LANES
            ]
    lanes = lane_ids((planes, LANES))
    rims = [jnp.zeros((planes, LANES), FLOAT) for _ in range(blocks)]
    for row in range(TILE):
        start = 16 * row
        turned = [
            pltpu.roll(
                send_ref[block, row * planes : (row + 1) * planes, :],
                (start + 8) % LANES,
                axis=1,
            )
            for block in range(blocks)
        ]
        left = (lanes >= start) & (lanes < start + 8)
        right = (lanes >= start + 8) & (lanes < start + 16)
        for block in range(blocks):
            if block > 0:
                rims[block] = jnp.where(left, turned[block - 1], rims[block])
            if block < blocks - 1:
                rims[block] = jnp.where(right, turned[block + 1], rims[block])
    for block in range(blocks):
        send_ref[block, TILE * planes : (TILE + 1) * planes, :] = rims[block]


def pack_pieces(slc_ref, *rest):
    pieces, blocks_ref = rest[:-1], rest[-1]
    pack_blocks(slc_ref, blocks_ref)
    here = lax.axis_index("date")
    for turn, piece_ref in enumerate(pieces):
        piece_ref[...] = blocks_ref[here ^ turn]


def join_kernel(turns, *rest):
    here = lax.axis_index("date")
    for turn, piece_ref in zip(turns, rest[:-1]):
        rest[-1][(here ^ turn) % 4] = piece_ref[...]


def tap_weight(distance):
    spread = jnp.abs(2 * distance - 1)
    return jnp.where(spread == 1, 0.5625, jnp.where(spread == 3, -0.0625, 0.0)).astype(FLOAT)


def prepare_kernel(
    offsets_ref, masks_ref, picks_ref, population_ref, row_sub_ref, row_lane_ref, col_lane_ref,
    sums_ref, words_ref
):
    words = masks_ref.shape[0]
    below = near_is_below()
    total = jnp.zeros((TILE, LANES), jnp.int32)
    for word in range(words):
        bits = masks_ref[word]
        bits = bits - (lax.shift_right_logical(bits, 1) & 0x55555555)
        bits = (bits & 0x33333333) + (lax.shift_right_logical(bits, 2) & 0x33333333)
        bits = (bits + lax.shift_right_logical(bits, 4)) & 0x0F0F0F0F
        bits = bits + lax.shift_right_logical(bits, 8)
        bits = bits + lax.shift_right_logical(bits, 16)
        total = total + (bits & 0xFF)
    population_ref[...] = total.astype(FLOAT)

    lanes = lane_ids((TILE, LANES))
    subs = sublane_ids((TILE, LANES))
    lane_dates = ((lanes % 64) // 8) * 4 + lanes % 4
    row_shift = jnp.zeros((TILE, LANES), jnp.int32)
    col_shift = jnp.zeros((TILE, LANES), jnp.int32)
    for date in range(NDATE):
        here = lane_dates == date
        row_shift = jnp.where(here, offsets_ref[0, date], row_shift)
        col_shift = jnp.where(here, offsets_ref[1, date], col_shift)
    for tap in range(TAP_COUNT):
        row_lane_ref[tap] = tap_weight(tap - 3 - row_shift)
        col_lane_ref[tap] = tap_weight(tap - 3 - col_shift)
    for group in range(GROUPS):
        shift = jnp.zeros((TILE, LANES), jnp.int32)
        for date in range(4):
            shift = jnp.where(subs % 4 == date, offsets_ref[0, 4 * group + date], shift)
        for tap in range(TAP_COUNT):
            row_sub_ref[tap, group * TILE : (group + 1) * TILE, :] = tap_weight(tap - 3 - shift)

    term = lax.broadcasted_iota(jnp.int32, (2 * LANES, 2 * LANES), 0) % LANES
    gives = lax.broadcasted_iota(jnp.int32, (2 * LANES, 2 * LANES), 1)
    same_part = ((term % 8) < 4) == (gives < LANES)
    sums_ref[...] = jnp.where(((term < 64) == ((gives % LANES) < 64)) & same_part, 1.0, 0.0).astype(HALF_FLOAT)

    flat = [masks_ref[word] for word in range(words)]
    flat = flat + [jnp.zeros((TILE, LANES), jnp.int32)] * (LANES // TILE - words)
    words_ref[...] = jnp.transpose(jnp.concatenate(flat, axis=0))

    def one_block(block, carry):
        packed = words_ref[pl.ds(pl.multiple_of(block * TILE, TILE), TILE), :]
        for row_pair in range(TILE // 2):
            spread = [[], []]
            for row in (2 * row_pair, 2 * row_pair + 1):
                row_words = [
                    jnp.broadcast_to(
                        packed[:, word * TILE + row : word * TILE + row + 1], (TILE, LANES)
                    )
                    for word in range(words)
                ]
                for half in range(2):
                    near = 8 * half + lanes // 16 - row
                    across = lanes % 16 - subs
                    inside = (near >= 0) & (near <= 8) & (across >= 0) & (across <= 8)
                    amount = jnp.where(inside, (near & 1) * SLOT_COLS + across, 31)
                    first = max(0, 8 * half - row) // 2
                    last = min(8, 8 * half + 7 - row) // 2
                    chosen = row_words[first]
                    for word in range(first + 1, last + 1):
                        chosen = jnp.where(near >= 2 * word, row_words[word], chosen)
                    bits = lax.shift_right_logical(chosen, amount) & 1
                    spread[half].append(bits.astype(FLOAT))
            low_half, high_half = [jnp.concatenate(half, axis=0) for half in spread]
            rows = slice(16 * row_pair, 16 * row_pair + 16)
            picks_ref[block, rows, :LANES] = jnp.where(below, high_half, low_half).astype(HALF_FLOAT)
            picks_ref[block, rows, LANES:] = jnp.where(below, low_half, high_half).astype(HALF_FLOAT)
        return carry

    lax.fori_loop(0, BLOCKS, one_block, 0)


def split_halves(values):
    high = values.astype(HALF_FLOAT)
    low = values - high.astype(FLOAT)
    return high, low


def dot(a, b, contract):
    return lax.dot_general(
        a, b, (((contract[0],), (contract[1],)), ((), ())), preferred_element_type=FLOAT
    )


def packed_rims(base, refs):
    halves = [ref[:, 8 * TILE : 9 * TILE, :].reshape(32, LANES) for ref in refs]
    return jnp.where(
        base == 0, jnp.concatenate(halves, axis=0), jnp.concatenate(halves[::-1], axis=0)
    )


def first_group():
    return (lax.axis_index("date") ^ 4) & 4 if lax.axis_size("date") == GROUPS else 0


def near_is_below():
    return (lax.axis_index("row") + lax.axis_index("date")) % 2 == 0


def resample_rows(
    base,
    own_refs,
    other_refs,
    below,
    row_sub_ref,
    row_lane_ref,
    mixed_ref,
    rims_ref,
    turned_ref,
):
    row_at, row_count = lax.axis_index("row"), lax.axis_size("row")

    exists = (below & (row_at < row_count - 1)) | (jnp.logical_not(below) & (row_at > 0))

    def mix_group(own_ref, other_ref, base, slot):
        group = base + slot
        weights = [
            row_sub_ref[tap, pl.ds(pl.multiple_of(group * TILE, TILE), TILE), :]
            for tap in range(TAP_COUNT)
        ]
        own = [own_ref[slot, row * TILE : (row + 1) * TILE, :] for row in range(TILE)]
        other = [
            jnp.where(exists, other_ref[slot, row * TILE : (row + 1) * TILE, :], 0.0)
            for row in range(TILE)
        ]
        raw = [jnp.where(below, a, b) for a, b in zip(own, other)]
        raw = raw + [jnp.where(below, b, a) for a, b in zip(own, other)]
        for row in range(8):
            mixed = weights[0] * raw[row + 1]
            for tap in range(1, TAP_COUNT):
                mixed = mixed + weights[tap] * raw[row + 1 + tap]
            start = pl.multiple_of((row // 4) * 64 + group * TILE, TILE)
            mixed_ref[row % 4, pl.ds(start, TILE), :] = mixed

    def mix_slot(slot, carry):
        mix_group(own_refs[0], other_refs[0], base, slot)
        mix_group(own_refs[1], other_refs[1], 4 - base, slot)
        return carry

    lax.fori_loop(0, GROUPS // 2, mix_slot, 0, unroll=GROUPS // 2)

    lanes = lane_ids((1, LANES))
    lower = lanes < 64
    own, other = [packed_rims(base, refs) for refs in (own_refs, other_refs)]
    other = jnp.where(exists, other, 0.0)
    first, second = jnp.where(below, own, other), jnp.where(below, other, own)
    far_first, far_second = pltpu.roll(first, 64, axis=1), pltpu.roll(second, 64, axis=1)
    rims_ref[0:LANES, :] = jnp.transpose(
        jnp.concatenate([first, jnp.where(lower, far_first, far_second)], axis=0)
    )
    rims_ref[LANES : 2 * LANES, :] = jnp.transpose(jnp.concatenate([second, far_second], axis=0))
    row_weights = [row_lane_ref[tap, 0:1, :] for tap in range(TAP_COUNT)]
    for row in range(4):
        turned_ref[row, 8 : 8 + LANES, :] = jnp.transpose(mixed_ref[row])
        rim = row_weights[0] * rims_ref[(row + 1) * 16 : (row + 2) * 16, :]
        for tap in range(1, TAP_COUNT):
            rim = rim + row_weights[tap] * rims_ref[(row + 1 + tap) * 16 : (row + 2 + tap) * 16, :]
        turned_ref[row, 0:8, :] = rim[0:8]
        turned_ref[row, 8 + LANES : 16 + LANES, :] = rim[8:16]


def resample_columns(below, col_lane_ref, sums_ref, z_ref, y_ref, turned_ref, first, count):
    row_at, row_count = lax.axis_index("row"), lax.axis_size("row")
    col_at, col_count = lax.axis_index("date"), lax.axis_size("date")
    lanes = lane_ids((1, LANES))
    lower = lanes < 64
    width = count * 8 + 8
    places = sublane_ids((width, LANES)) + first * 8
    inside = ((places >= 4) | (col_at > 0)) & ((places < 132) | (col_at < col_count - 1))
    row_inside = (lower & (below | (row_at > 0))) | (
        (lanes >= 64) & (jnp.logical_not(below) | (row_at < row_count - 1))
    )
    inside = inside & row_inside

    def store_windows(target, row, values):
        high, low = split_halves(values)
        high = high.astype(FLOAT)
        rows = (
            jnp.where(lower, high, pltpu.roll(low, 64, axis=1)),
            jnp.where(lower, pltpu.roll(high, 64, axis=1), low),
        )
        for part in range(2):
            start = (row + 4 * part) * 16
            for block in range(count):
                target[first + block, start : start + 16, :] = rows[part][
                    block * 8 : block * 8 + 16
                ].astype(HALF_FLOAT)

    for row in range(4):
        begin = 1 + first * 8
        mixed = col_lane_ref[0, 0:1, :] * turned_ref[row, begin : begin + width, :]
        for tap in range(1, TAP_COUNT):
            mixed = mixed + col_lane_ref[tap, 0:1, :] * turned_ref[
                row, begin + tap : begin + tap + width, :
            ]
        z = jnp.where(inside, mixed, 0.0)
        high, low = split_halves(z)
        total = dot(
            jnp.concatenate([high, low.astype(HALF_FLOAT)], axis=1), sums_ref[...], (1, 0)
        )
        y = z * total[:, :LANES] + swapped(z) * total[:, LANES:]
        store_windows(z_ref, row, z)
        store_windows(y_ref, row, y)


def swapped(values):
    real = (lane_ids((1, LANES)) % 8) < 4
    return jnp.where(real, pltpu.roll(values, LANES - 4, axis=1), -pltpu.roll(values, 4, axis=1))


def near_kernel(
    own_b,
    own_a,
    near_b,
    near_a,
    row_sub_ref,
    row_lane_ref,
    col_lane_ref,
    sums_ref,
    z_ref,
    y_ref,
    mixed_ref,
    rims_ref,
    turned_ref,
):
    below = near_is_below()
    resample_rows(
        first_group(),
        (own_a, own_b),
        (near_a, near_b),
        below,
        row_sub_ref,
        row_lane_ref,
        mixed_ref,
        rims_ref,
        turned_ref,
    )
    resample_columns(below, col_lane_ref, sums_ref, z_ref, y_ref, turned_ref, 0, BLOCKS)


def link_kernel(
    own_b,
    own_a,
    far_b,
    far_a,
    row_sub_ref,
    row_lane_ref,
    col_lane_ref,
    sums_ref,
    near_z_ref,
    near_y_ref,
    picks_ref,
    population_ref,
    linked_ref,
    eigen_ref,
    far_z_ref,
    far_y_ref,
    mixed_ref,
    rims_ref,
    turned_ref,
    result_ref,
    first_ref,
    vectors_ref,
    chosen_ref,
):
    below = jnp.logical_not(near_is_below())
    resample_rows(
        first_group(),
        (own_a, own_b),
        (far_a, far_b),
        below,
        row_sub_ref,
        row_lane_ref,
        mixed_ref,
        rims_ref,
        turned_ref,
    )
    lower = lane_ids((1, LANES)) < 64

    def columns(first, count):
        resample_columns(
            below, col_lane_ref, sums_ref, far_z_ref, far_y_ref, turned_ref, first, count
        )

    def first_phase(first, count):
        for block in range(first, first + count):
            y = jnp.concatenate([near_y_ref[block], far_y_ref[block]], axis=0)
            vector = dot(picks_ref[block], y, (1, 0))
            vector = vector + pltpu.roll(vector, 64, axis=1)
            high, low = split_halves(jnp.concatenate([vector, swapped(vector)], axis=0))
            first_ref[block] = vector
            vectors_ref[block, :, :LANES] = high
            vectors_ref[block, :, LANES:] = low.astype(HALF_FLOAT)

    def inner_phase(first, count):
        for block in range(first, first + count):
            z = jnp.concatenate([near_z_ref[block], far_z_ref[block]], axis=0)
            inner = dot(vectors_ref[block], jnp.concatenate([z, z], axis=1), (1, 1))
            high, low = split_halves(inner)
            picks = picks_ref[block]
            picks = jnp.concatenate([picks, picks], axis=0)
            chosen_ref[block, :128, :] = high * picks
            chosen_ref[block, 128:, :] = low.astype(HALF_FLOAT) * picks

    def outer_phase(first, count):
        for block in range(first, first + count):
            z = jnp.concatenate([near_z_ref[block], far_z_ref[block]], axis=0)
            outer = dot(chosen_ref[block], z, (1, 0))
            outer = outer[:128] + outer[128:]
            outer = outer + pltpu.roll(outer, 64, axis=1)
            second = outer[:64] - swapped(outer[64:])
            both = jnp.where(lower, second, first_ref[block])
            for row in range(8):
                result_ref[row, block * 8 : block * 8 + 8, :] = both[row * 8 : row * 8 + 8]

    half = BLOCKS // 2
    columns(0, half)
    first_phase(0, half)
    columns(half, half)
    inner_phase(0, half)
    first_phase(half, half)
    outer_phase(0, half)
    inner_phase(half, half)
    outer_phase(half, half)

    inverse = 1.0 / population_ref[...]
    for row in range(8):
        turned = jnp.transpose(result_ref[row])
        second, first = turned[:64], turned[64:]
        scale = inverse[row : row + 1]
        square = scale * scale
        norm_first = jnp.sqrt(jnp.sum(first * first, axis=0, keepdims=True) * square + EPSILON)
        norm_last = jnp.sqrt(
            jnp.sum(second * second, axis=0, keepdims=True) * (square * square) + EPSILON
        )
        eigen_ref[row : row + 1, :] = norm_last / norm_first
        linked = second * (square * (jnp.sqrt(jnp.float32(NDATE)) / norm_last))
        for group in range(GROUPS):
            for part in range(2):
                begin = ((part * NDATE + 4 * group) * 8) + row
                at = group * 8 + part * 4
                linked_ref[pl.ds(begin, 4, stride=8), :] = linked[at : at + 4]


def canonical(received, dates_dev):
    sources = received.shape[0]
    if dates_dev == 4:
        return received
    cells = received.reshape(sources, 9, 2, dates_dev, LANES)
    cells = jnp.transpose(cells, (1, 2, 0, 3, 4)).reshape(9, 2, GROUPS, 4, LANES)
    return jnp.transpose(cells, (2, 0, 1, 3, 4)).reshape(GROUPS, 9 * TILE, LANES)


def partner(date, row, turn, rows_count):
    other = row + 1 if (row + date + turn) % 2 == 0 else row - 1
    if 0 <= other < rows_count:
        return date * rows_count + other
    return (date ^ 2) * rows_count + row


def vmem(count):
    return [pl.BlockSpec(memory_space=pltpu.VMEM)] * count


def on_device(slc, offsets, masks):
    dates_dev = slc.shape[1]
    rows_dev = slc.shape[2]
    cols_all = slc.shape[3]
    rows_count = lax.axis_size("row")
    cols_count = lax.axis_size("date")
    planes_dev = 2 * dates_dev
    assert rows_dev == TILE and cols_all == cols_count * LANES

    small = pltpu.CompilerParams(vmem_limit_bytes=4 * 1024 * 1024)
    images = slc.reshape(planes_dev, rows_dev, cols_all)
    moves = pl.CostEstimate(flops=0, bytes_accessed=600_000, transcendentals=0)
    half_shape = jax.ShapeDtypeStruct((GROUPS // 2, 9 * TILE, LANES), FLOAT)

    def swap_rows(cells, turn):
        return lax.ppermute(
            cells,
            ("date", "row"),
            [
                (date * rows_count + row, partner(date, row, turn, rows_count))
                for date in range(cols_count)
                for row in range(rows_count)
            ],
        )

    if cols_count == GROUPS:
        pieces = pl.pallas_call(
            pack_pieces,
            out_shape=[jax.ShapeDtypeStruct((9 * TILE, LANES), FLOAT)] * GROUPS,
            in_specs=vmem(1),
            out_specs=vmem(GROUPS),
            scratch_shapes=[pltpu.VMEM((GROUPS, 9 * TILE, LANES), FLOAT)],
            compiler_params=small,
            cost_estimate=moves,
            name="pack",
        )(images)
        pieces = list(pieces[:1]) + [
            lax.ppermute(pieces[turn], "date", [(i, i ^ turn) for i in range(GROUPS)])
            for turn in range(1, GROUPS)
        ]
        own = [
            pl.pallas_call(
                functools.partial(join_kernel, turns),
                out_shape=half_shape,
                in_specs=vmem(4),
                out_specs=vmem(1)[0],
                compiler_params=small,
                cost_estimate=moves,
                name="join",
            )(*[pieces[turn] for turn in turns])
            for turns in ((6, 7, 4, 5), (2, 3, 1, 0))
        ]
    else:
        outgoing = pl.pallas_call(
            pack_blocks,
            out_shape=jax.ShapeDtypeStruct((cols_count, 9 * planes_dev, LANES), FLOAT),
            in_specs=vmem(1),
            out_specs=vmem(1)[0],
            compiler_params=small,
            cost_estimate=moves,
            name="pack",
        )(images)
        received = lax.all_to_all(outgoing, "date", split_axis=0, concat_axis=0, tiled=True)
        received = canonical(received, dates_dev)
        own = [received[: GROUPS // 2], received[GROUPS // 2 :]]
    near_a, far_a, near_b, far_b = [swap_rows(half, turn) for half in own for turn in range(2)]

    picks, population, row_sub, row_lane, col_lane, sums = pl.pallas_call(
        prepare_kernel,
        out_shape=(
            jax.ShapeDtypeStruct((BLOCKS, 64, 256), HALF_FLOAT),
            jax.ShapeDtypeStruct((TILE, LANES), FLOAT),
            jax.ShapeDtypeStruct((TAP_COUNT, 64, LANES), FLOAT),
            jax.ShapeDtypeStruct((TAP_COUNT, TILE, LANES), FLOAT),
            jax.ShapeDtypeStruct((TAP_COUNT, TILE, LANES), FLOAT),
            jax.ShapeDtypeStruct((2 * LANES, 2 * LANES), HALF_FLOAT),
        ),
        in_specs=[pl.BlockSpec(memory_space=pltpu.SMEM)] + vmem(1),
        out_specs=tuple(vmem(6)),
        scratch_shapes=[pltpu.VMEM((LANES, LANES), jnp.int32)],
        compiler_params=small,
        cost_estimate=pl.CostEstimate(flops=4_000_000, bytes_accessed=1_000_000, transcendentals=0),
        name="prepare",
    )(offsets, masks)

    half_scratch = [
        pltpu.VMEM((4, LANES, LANES), FLOAT),
        pltpu.VMEM((2 * LANES, LANES), FLOAT),
        pltpu.VMEM((4, LANES + 16, LANES), FLOAT),
    ]
    windows = jax.ShapeDtypeStruct((BLOCKS, LANES, LANES), HALF_FLOAT)
    near_z, near_y = pl.pallas_call(
        near_kernel,
        out_shape=(windows, windows),
        in_specs=vmem(8),
        out_specs=tuple(vmem(2)),
        scratch_shapes=half_scratch,
        compiler_params=small,
        cost_estimate=pl.CostEstimate(
            flops=200_000_000, bytes_accessed=2_000_000, transcendentals=0
        ),
        name="near",
    )(*own[::-1], near_b, near_a, row_sub, row_lane, col_lane, sums)
    linked, eigen = pl.pallas_call(
        link_kernel,
        out_shape=(
            jax.ShapeDtypeStruct((2 * NDATE * TILE, LANES), FLOAT),
            jax.ShapeDtypeStruct((TILE, LANES), FLOAT),
        ),
        in_specs=vmem(12),
        out_specs=tuple(vmem(2)),
        scratch_shapes=[
            pltpu.VMEM((BLOCKS, LANES, LANES), HALF_FLOAT),
            pltpu.VMEM((BLOCKS, LANES, LANES), HALF_FLOAT),
        ]
        + half_scratch
        + [
            pltpu.VMEM((8, LANES, LANES), FLOAT),
            pltpu.VMEM((BLOCKS, 64, LANES), FLOAT),
            pltpu.VMEM((BLOCKS, 128, 256), HALF_FLOAT),
            pltpu.VMEM((BLOCKS, 256, 256), HALF_FLOAT),
        ],
        compiler_params=pltpu.CompilerParams(vmem_limit_bytes=16 * 1024 * 1024),
        cost_estimate=pl.CostEstimate(
            flops=1_000_000_000, bytes_accessed=2_000_000, transcendentals=0
        ),
        name="link",
    )(*own[::-1], far_b, far_a, row_sub, row_lane, col_lane, sums, near_z, near_y, picks, population)
    return linked.reshape(2, NDATE, TILE, LANES), eigen


def solution(mesh):
    in_specs = (P(None, "date", "row", None), P(), P(None, "row", "date"))
    out_specs = (P(None, None, "row", "date"), P("row", "date"))
    return jax.shard_map(
        on_device, mesh=mesh, in_specs=in_specs, out_specs=out_specs, check_vma=False
    )
```

```python
import functools

import jax
import jax.numpy as jnp
from jax import lax
from jax.experimental import pallas as pl
from jax.experimental.pallas import tpu as pltpu
from jax.sharding import PartitionSpec as P

NDATE = 32
SLOT_COLS = 9
EPSILON = 1e-06
LANES = 128
TILE = 8
GROUPS = 8
TAP_COUNT = 8
WINDOW_ROWS = 16
WINDOW_COLS = 136
BLOCKS = 16

FLOAT = jnp.float32
HALF_FLOAT = jnp.bfloat16


def lane_ids(shape):
    return lax.broadcasted_iota(jnp.int32, shape, len(shape) - 1)


def sublane_ids(shape):
    return lax.broadcasted_iota(jnp.int32, shape, len(shape) - 2)


def pack_blocks(slc_ref, send_ref):
    planes = slc_ref.shape[0]
    blocks = send_ref.shape[0]
    for block in range(blocks):
        for plane in range(planes):
            send_ref[block, pl.ds(plane, TILE, stride=planes), :] = slc_ref[
                plane, :, block * LANES : (block + 1) * LANES
            ]
    lanes = lane_ids((planes, LANES))
    rims = [jnp.zeros((planes, LANES), FLOAT) for _ in range(blocks)]
    for row in range(TILE):
        start = 16 * row
        turned = [
            pltpu.roll(
                send_ref[block, row * planes : (row + 1) * planes, :],
                (start + 8) % LANES,
                axis=1,
            )
            for block in range(blocks)
        ]
        left = (lanes >= start) & (lanes < start + 8)
        right = (lanes >= start + 8) & (lanes < start + 16)
        for block in range(blocks):
            if block > 0:
                rims[block] = jnp.where(left, turned[block - 1], rims[block])
            if block < blocks - 1:
                rims[block] = jnp.where(right, turned[block + 1], rims[block])
    for block in range(blocks):
        send_ref[block, TILE * planes : (TILE + 1) * planes, :] = rims[block]


def pack_pieces(slc_ref, *rest):
    pieces, blocks_ref = rest[:-1], rest[-1]
    pack_blocks(slc_ref, blocks_ref)
    here = lax.axis_index("date")
    for turn, piece_ref in enumerate(pieces):
        piece_ref[...] = blocks_ref[here ^ turn]


def join_kernel(turns, *rest):
    here = lax.axis_index("date")
    for turn, piece_ref in zip(turns, rest[:-1]):
        rest[-1][(here ^ turn) % 4] = piece_ref[...]


def tap_weight(distance):
    spread = jnp.abs(2 * distance - 1)
    return jnp.where(spread == 1, 0.5625, jnp.where(spread == 3, -0.0625, 0.0)).astype(FLOAT)


def prepare_kernel(
    offsets_ref, masks_ref, picks_ref, population_ref, row_sub_ref, row_lane_ref, col_lane_ref,
    sums_ref, words_ref
):
    words = masks_ref.shape[0]
    below = near_is_below()
    total = jnp.zeros((TILE, LANES), jnp.int32)
    for word in range(words):
        bits = masks_ref[word]
        bits = bits - (lax.shift_right_logical(bits, 1) & 0x55555555)
        bits = (bits & 0x33333333) + (lax.shift_right_logical(bits, 2) & 0x33333333)
        bits = (bits + lax.shift_right_logical(bits, 4)) & 0x0F0F0F0F
        bits = bits + lax.shift_right_logical(bits, 8)
        bits = bits + lax.shift_right_logical(bits, 16)
        total = total + (bits & 0xFF)
    population_ref[...] = total.astype(FLOAT)

    lanes = lane_ids((TILE, LANES))
    subs = sublane_ids((TILE, LANES))
    lane_dates = ((lanes % 64) // 8) * 4 + lanes % 4
    row_shift = jnp.zeros((TILE, LANES), jnp.int32)
    col_shift = jnp.zeros((TILE, LANES), jnp.int32)
    for date in range(NDATE):
        here = lane_dates == date
        row_shift = jnp.where(here, offsets_ref[0, date], row_shift)
        col_shift = jnp.where(here, offsets_ref[1, date], col_shift)
    for tap in range(TAP_COUNT):
        row_lane_ref[tap] = tap_weight(tap - 3 - row_shift)
        col_lane_ref[tap] = tap_weight(tap - 3 - col_shift)
    for group in range(GROUPS):
        shift = jnp.zeros((TILE, LANES), jnp.int32)
        for date in range(4):
            shift = jnp.where(subs % 4 == date, offsets_ref[0, 4 * group + date], shift)
        for tap in range(TAP_COUNT):
            row_sub_ref[tap, group * TILE : (group + 1) * TILE, :] = tap_weight(tap - 3 - shift)

    term = lax.broadcasted_iota(jnp.int32, (2 * LANES, 2 * LANES), 0) % LANES
    gives = lax.broadcasted_iota(jnp.int32, (2 * LANES, 2 * LANES), 1)
    same_part = ((term % 8) < 4) == (gives < LANES)
    sums_ref[...] = jnp.where(((term < 64) == ((gives % LANES) < 64)) & same_part, 1.0, 0.0).astype(HALF_FLOAT)

    flat = [masks_ref[word] for word in range(words)]
    flat = flat + [jnp.zeros((TILE, LANES), jnp.int32)] * (LANES // TILE - words)
    words_ref[...] = jnp.transpose(jnp.concatenate(flat, axis=0))

    def one_block(block, carry):
        packed = words_ref[pl.ds(pl.multiple_of(block * TILE, TILE), TILE), :]
        for row_pair in range(TILE // 2):
            spread = [[], []]
            for row in (2 * row_pair, 2 * row_pair + 1):
                row_words = [
                    jnp.broadcast_to(
                        packed[:, word * TILE + row : word * TILE + row + 1], (TILE, LANES)
                    )
                    for word in range(words)
                ]
                for half in range(2):
                    near = 8 * half + lanes // 16 - row
                    across = lanes % 16 - subs
                    inside = (near >= 0) & (near <= 8) & (across >= 0) & (across <= 8)
                    amount = jnp.where(inside, (near & 1) * SLOT_COLS + across, 31)
                    first = max(0, 8 * half - row) // 2
                    last = min(8, 8 * half + 7 - row) // 2
                    chosen = row_words[first]
                    for word in range(first + 1, last + 1):
                        chosen = jnp.where(near >= 2 * word, row_words[word], chosen)
                    bits = lax.shift_right_logical(chosen, amount) & 1
                    spread[half].append(bits.astype(FLOAT))
            low_half, high_half = [jnp.concatenate(half, axis=0) for half in spread]
            rows = slice(16 * row_pair, 16 * row_pair + 16)
            picks_ref[block, rows, :LANES] = jnp.where(below, high_half, low_half).astype(HALF_FLOAT)
            picks_ref[block, rows, LANES:] = jnp.where(below, low_half, high_half).astype(HALF_FLOAT)
        return carry

    lax.fori_loop(0, BLOCKS, one_block, 0)


def split_halves(values):
    high = values.astype(HALF_FLOAT)
    low = values - high.astype(FLOAT)
    return high, low


def dot(a, b, contract):
    return lax.dot_general(
        a, b, (((contract[0],), (contract[1],)), ((), ())), preferred_element_type=FLOAT
    )


def packed_rims(base, refs):
    halves = [ref[:, 8 * TILE : 9 * TILE, :].reshape(32, LANES) for ref in refs]
    return jnp.where(
        base == 0, jnp.concatenate(halves, axis=0), jnp.concatenate(halves[::-1], axis=0)
    )


def first_group():
    return (lax.axis_index("date") ^ 4) & 4 if lax.axis_size("date") == GROUPS else 0


def near_is_below():
    return (lax.axis_index("row") + lax.axis_index("date")) % 2 == 0


def resample_rows(
    base,
    own_refs,
    other_refs,
    below,
    row_sub_ref,
    row_lane_ref,
    mixed_ref,
    rims_ref,
    turned_ref,
):
    row_at, row_count = lax.axis_index("row"), lax.axis_size("row")

    exists = (below & (row_at < row_count - 1)) | (jnp.logical_not(below) & (row_at > 0))

    def mix_group(own_ref, other_ref, base, slot):
        group = base + slot
        weights = [
            row_sub_ref[tap, pl.ds(pl.multiple_of(group * TILE, TILE), TILE), :]
            for tap in range(TAP_COUNT)
        ]
        own = [own_ref[slot, row * TILE : (row + 1) * TILE, :] for row in range(TILE)]
        other = [
            jnp.where(exists, other_ref[slot, row * TILE : (row + 1) * TILE, :], 0.0)
            for row in range(TILE)
        ]
        raw = [jnp.where(below, a, b) for a, b in zip(own, other)]
        raw = raw + [jnp.where(below, b, a) for a, b in zip(own, other)]
        for row in range(8):
            mixed = weights[0] * raw[row + 1]
            for tap in range(1, TAP_COUNT):
                mixed = mixed + weights[tap] * raw[row + 1 + tap]
            start = pl.multiple_of((row // 4) * 64 + group * TILE, TILE)
            mixed_ref[row % 4, pl.ds(start, TILE), :] = mixed

    def mix_slot(slot, carry):
        mix_group(own_refs[0], other_refs[0], base, slot)
        mix_group(own_refs[1], other_refs[1], 4 - base, slot)
        return carry

    lax.fori_loop(0, GROUPS // 2, mix_slot, 0, unroll=GROUPS // 2)

    lanes = lane_ids((1, LANES))
    lower = lanes < 64
    own, other = [packed_rims(base, refs) for refs in (own_refs, other_refs)]
    other = jnp.where(exists, other, 0.0)
    first, second = jnp.where(below, own, other), jnp.where(below, other, own)
    far_first, far_second = pltpu.roll(first, 64, axis=1), pltpu.roll(second, 64, axis=1)
    rims_ref[0:LANES, :] = jnp.transpose(
        jnp.concatenate([first, jnp.where(lower, far_first, far_second)], axis=0)
    )
    rims_ref[LANES : 2 * LANES, :] = jnp.transpose(jnp.concatenate([second, far_second], axis=0))
    row_weights = [row_lane_ref[tap, 0:1, :] for tap in range(TAP_COUNT)]
    for row in range(4):
        turned_ref[row, 8 : 8 + LANES, :] = jnp.transpose(mixed_ref[row])
        rim = row_weights[0] * rims_ref[(row + 1) * 16 : (row + 2) * 16, :]
        for tap in range(1, TAP_COUNT):
            rim = rim + row_weights[tap] * rims_ref[(row + 1 + tap) * 16 : (row + 2 + tap) * 16, :]
        turned_ref[row, 0:8, :] = rim[0:8]
        turned_ref[row, 8 + LANES : 16 + LANES, :] = rim[8:16]


def resample_columns(below, col_lane_ref, sums_ref, z_ref, y_ref, turned_ref, first, count):
    row_at, row_count = lax.axis_index("row"), lax.axis_size("row")
    col_at, col_count = lax.axis_index("date"), lax.axis_size("date")
    lanes = lane_ids((1, LANES))
    lower = lanes < 64
    width = count * 8 + 8
    places = sublane_ids((width, LANES)) + first * 8
    inside = ((places >= 4) | (col_at > 0)) & ((places < 132) | (col_at < col_count - 1))
    row_inside = (lower & (below | (row_at > 0))) | (
        (lanes >= 64) & (jnp.logical_not(below) | (row_at < row_count - 1))
    )
    inside = inside & row_inside

    def store_windows(target, row, values):
        high, low = split_halves(values)
        high = high.astype(FLOAT)
        rows = (
            jnp.where(lower, high, pltpu.roll(low, 64, axis=1)),
            jnp.where(lower, pltpu.roll(high, 64, axis=1), low),
        )
        for part in range(2):
            start = (row + 4 * part) * 16
            for block in range(count):
                target[first + block, start : start + 16, :] = rows[part][
                    block * 8 : block * 8 + 16
                ].astype(HALF_FLOAT)

    for row in range(4):
        begin = 1 + first * 8
        mixed = col_lane_ref[0, 0:1, :] * turned_ref[row, begin : begin + width, :]
        for tap in range(1, TAP_COUNT):
            mixed = mixed + col_lane_ref[tap, 0:1, :] * turned_ref[
                row, begin + tap : begin + tap + width, :
            ]
        z = jnp.where(inside, mixed, 0.0)
        high, low = split_halves(z)
        total = dot(
            jnp.concatenate([high, low.astype(HALF_FLOAT)], axis=1), sums_ref[...], (1, 0)
        )
        y = z * total[:, :LANES] + swapped(z) * total[:, LANES:]
        store_windows(z_ref, row, z)
        store_windows(y_ref, row, y)


def swapped(values):
    real = (lane_ids((1, LANES)) % 8) < 4
    return jnp.where(real, pltpu.roll(values, LANES - 4, axis=1), -pltpu.roll(values, 4, axis=1))


def near_kernel(
    own_b,
    own_a,
    near_b,
    near_a,
    row_sub_ref,
    row_lane_ref,
    col_lane_ref,
    sums_ref,
    z_ref,
    y_ref,
    mixed_ref,
    rims_ref,
    turned_ref,
):
    below = near_is_below()
    resample_rows(
        first_group(),
        (own_a, own_b),
        (near_a, near_b),
        below,
        row_sub_ref,
        row_lane_ref,
        mixed_ref,
        rims_ref,
        turned_ref,
    )
    resample_columns(below, col_lane_ref, sums_ref, z_ref, y_ref, turned_ref, 0, BLOCKS)


def link_kernel(
    own_b,
    own_a,
    far_b,
    far_a,
    row_sub_ref,
    row_lane_ref,
    col_lane_ref,
    sums_ref,
    near_z_ref,
    near_y_ref,
    picks_ref,
    population_ref,
    linked_ref,
    eigen_ref,
    far_z_ref,
    far_y_ref,
    mixed_ref,
    rims_ref,
    turned_ref,
    result_ref,
    first_ref,
    vectors_ref,
    chosen_ref,
):
    below = jnp.logical_not(near_is_below())
    resample_rows(
        first_group(),
        (own_a, own_b),
        (far_a, far_b),
        below,
        row_sub_ref,
        row_lane_ref,
        mixed_ref,
        rims_ref,
        turned_ref,
    )
    lower = lane_ids((1, LANES)) < 64

    def columns(first, count):
        resample_columns(
            below, col_lane_ref, sums_ref, far_z_ref, far_y_ref, turned_ref, first, count
        )

    def first_phase(first, count):
        for block in range(first, first + count):
            y = jnp.concatenate([near_y_ref[block], far_y_ref[block]], axis=0)
            vector = dot(picks_ref[block], y, (1, 0))
            vector = vector + pltpu.roll(vector, 64, axis=1)
            high, low = split_halves(jnp.concatenate([vector, swapped(vector)], axis=0))
            first_ref[block] = vector
            vectors_ref[block, :, :LANES] = high
            vectors_ref[block, :, LANES:] = low.astype(HALF_FLOAT)

    def inner_phase(first, count):
        for block in range(first, first + count):
            z = jnp.concatenate([near_z_ref[block], far_z_ref[block]], axis=0)
            inner = dot(vectors_ref[block], jnp.concatenate([z, z], axis=1), (1, 1))
            high, low = split_halves(inner)
            picks = picks_ref[block]
            picks = jnp.concatenate([picks, picks], axis=0)
            chosen_ref[block, :128, :] = high * picks
            chosen_ref[block, 128:, :] = low.astype(HALF_FLOAT) * picks

    def outer_phase(first, count):
        for block in range(first, first + count):
            z = jnp.concatenate([near_z_ref[block], far_z_ref[block]], axis=0)
            outer = dot(chosen_ref[block], z, (1, 0))
            outer = outer[:128] + outer[128:]
            outer = outer + pltpu.roll(outer, 64, axis=1)
            second = outer[:64] - swapped(outer[64:])
            both = jnp.where(lower, second, first_ref[block])
            for row in range(8):
                result_ref[row, block * 8 : block * 8 + 8, :] = both[row * 8 : row * 8 + 8]

    half = BLOCKS // 2
    columns(0, half)
    first_phase(0, half)
    inner_phase(0, half)
    columns(half, half)
    outer_phase(0, half)
    first_phase(half, half)
    inner_phase(half, half)
    outer_phase(half, half)

    inverse = 1.0 / population_ref[...]
    for row in range(8):
        turned = jnp.transpose(result_ref[row])
        second, first = turned[:64], turned[64:]
        scale = inverse[row : row + 1]
        square = scale * scale
        norm_first = jnp.sqrt(jnp.sum(first * first, axis=0, keepdims=True) * square + EPSILON)
        norm_last = jnp.sqrt(
            jnp.sum(second * second, axis=0, keepdims=True) * (square * square) + EPSILON
        )
        eigen_ref[row : row + 1, :] = norm_last / norm_first
        linked = second * (square * (jnp.sqrt(jnp.float32(NDATE)) / norm_last))
        for group in range(GROUPS):
            for part in range(2):
                begin = ((part * NDATE + 4 * group) * 8) + row
                at = group * 8 + part * 4
                linked_ref[pl.ds(begin, 4, stride=8), :] = linked[at : at + 4]


def canonical(received, dates_dev):
    sources = received.shape[0]
    if dates_dev == 4:
        return received
    cells = received.reshape(sources, 9, 2, dates_dev, LANES)
    cells = jnp.transpose(cells, (1, 2, 0, 3, 4)).reshape(9, 2, GROUPS, 4, LANES)
    return jnp.transpose(cells, (2, 0, 1, 3, 4)).reshape(GROUPS, 9 * TILE, LANES)


def partner(date, row, turn, rows_count):
    other = row + 1 if (row + date + turn) % 2 == 0 else row - 1
    if 0 <= other < rows_count:
        return date * rows_count + other
    return (date ^ 2) * rows_count + row


def vmem(count):
    return [pl.BlockSpec(memory_space=pltpu.VMEM)] * count


def on_device(slc, offsets, masks):
    dates_dev = slc.shape[1]
    rows_dev = slc.shape[2]
    cols_all = slc.shape[3]
    rows_count = lax.axis_size("row")
    cols_count = lax.axis_size("date")
    planes_dev = 2 * dates_dev
    assert rows_dev == TILE and cols_all == cols_count * LANES

    small = pltpu.CompilerParams(vmem_limit_bytes=4 * 1024 * 1024)
    images = slc.reshape(planes_dev, rows_dev, cols_all)
    moves = pl.CostEstimate(flops=0, bytes_accessed=600_000, transcendentals=0)
    half_shape = jax.ShapeDtypeStruct((GROUPS // 2, 9 * TILE, LANES), FLOAT)

    def swap_rows(cells, turn):
        return lax.ppermute(
            cells,
            ("date", "row"),
            [
                (date * rows_count + row, partner(date, row, turn, rows_count))
                for date in range(cols_count)
                for row in range(rows_count)
            ],
        )

    if cols_count == GROUPS:
        pieces = pl.pallas_call(
            pack_pieces,
            out_shape=[jax.ShapeDtypeStruct((9 * TILE, LANES), FLOAT)] * GROUPS,
            in_specs=vmem(1),
            out_specs=vmem(GROUPS),
            scratch_shapes=[pltpu.VMEM((GROUPS, 9 * TILE, LANES), FLOAT)],
            compiler_params=small,
            cost_estimate=moves,
            name="pack",
        )(images)
        pieces = list(pieces[:1]) + [
            lax.ppermute(pieces[turn], "date", [(i, i ^ turn) for i in range(GROUPS)])
            for turn in range(1, GROUPS)
        ]
        own = [
            pl.pallas_call(
                functools.partial(join_kernel, turns),
                out_shape=half_shape,
                in_specs=vmem(4),
                out_specs=vmem(1)[0],
                compiler_params=small,
                cost_estimate=moves,
                name="join",
            )(*[pieces[turn] for turn in turns])
            for turns in ((6, 7, 4, 5), (2, 3, 1, 0))
        ]
    else:
        outgoing = pl.pallas_call(
            pack_blocks,
            out_shape=jax.ShapeDtypeStruct((cols_count, 9 * planes_dev, LANES), FLOAT),
            in_specs=vmem(1),
            out_specs=vmem(1)[0],
            compiler_params=small,
            cost_estimate=moves,
            name="pack",
        )(images)
        received = lax.all_to_all(outgoing, "date", split_axis=0, concat_axis=0, tiled=True)
        received = canonical(received, dates_dev)
        own = [received[: GROUPS // 2], received[GROUPS // 2 :]]
    near_a, far_a, near_b, far_b = [swap_rows(half, turn) for half in own for turn in range(2)]

    picks, population, row_sub, row_lane, col_lane, sums = pl.pallas_call(
        prepare_kernel,
        out_shape=(
            jax.ShapeDtypeStruct((BLOCKS, 64, 256), HALF_FLOAT),
            jax.ShapeDtypeStruct((TILE, LANES), FLOAT),
            jax.ShapeDtypeStruct((TAP_COUNT, 64, LANES), FLOAT),
            jax.ShapeDtypeStruct((TAP_COUNT, TILE, LANES), FLOAT),
            jax.ShapeDtypeStruct((TAP_COUNT, TILE, LANES), FLOAT),
            jax.ShapeDtypeStruct((2 * LANES, 2 * LANES), HALF_FLOAT),
        ),
        in_specs=[pl.BlockSpec(memory_space=pltpu.SMEM)] + vmem(1),
        out_specs=tuple(vmem(6)),
        scratch_shapes=[pltpu.VMEM((LANES, LANES), jnp.int32)],
        compiler_params=small,
        cost_estimate=pl.CostEstimate(flops=4_000_000, bytes_accessed=1_000_000, transcendentals=0),
        name="prepare",
    )(offsets, masks)

    half_scratch = [
        pltpu.VMEM((4, LANES, LANES), FLOAT),
        pltpu.VMEM((2 * LANES, LANES), FLOAT),
        pltpu.VMEM((4, LANES + 16, LANES), FLOAT),
    ]
    windows = jax.ShapeDtypeStruct((BLOCKS, LANES, LANES), HALF_FLOAT)
    near_z, near_y = pl.pallas_call(
        near_kernel,
        out_shape=(windows, windows),
        in_specs=vmem(8),
        out_specs=tuple(vmem(2)),
        scratch_shapes=half_scratch,
        compiler_params=small,
        cost_estimate=pl.CostEstimate(
            flops=200_000_000, bytes_accessed=2_000_000, transcendentals=0
        ),
        name="near",
    )(*own[::-1], near_b, near_a, row_sub, row_lane, col_lane, sums)
    linked, eigen = pl.pallas_call(
        link_kernel,
        out_shape=(
            jax.ShapeDtypeStruct((2 * NDATE * TILE, LANES), FLOAT),
            jax.ShapeDtypeStruct((TILE, LANES), FLOAT),
        ),
        in_specs=vmem(12),
        out_specs=tuple(vmem(2)),
        scratch_shapes=[
            pltpu.VMEM((BLOCKS, LANES, LANES), HALF_FLOAT),
            pltpu.VMEM((BLOCKS, LANES, LANES), HALF_FLOAT),
        ]
        + half_scratch
        + [
            pltpu.VMEM((8, LANES, LANES), FLOAT),
            pltpu.VMEM((BLOCKS, 64, LANES), FLOAT),
            pltpu.VMEM((BLOCKS, 128, 256), HALF_FLOAT),
            pltpu.VMEM((BLOCKS, 256, 256), HALF_FLOAT),
        ],
        compiler_params=pltpu.CompilerParams(vmem_limit_bytes=16 * 1024 * 1024),
        cost_estimate=pl.CostEstimate(
            flops=1_000_000_000, bytes_accessed=2_000_000, transcendentals=0
        ),
        name="link",
    )(*own[::-1], far_b, far_a, row_sub, row_lane, col_lane, sums, near_z, near_y, picks, population)
    return linked.reshape(2, NDATE, TILE, LANES), eigen


def solution(mesh):
    in_specs = (P(None, "date", "row", None), P(), P(None, "row", "date"))
    out_specs = (P(None, None, "row", "date"), P("row", "date"))
    return jax.shard_map(
        on_device, mesh=mesh, in_specs=in_specs, out_specs=out_specs, check_vma=False
    )
```
